128 devices in a mesh: lon: 32 (over y_hi, x, z), lat: 4 (over y_lo, core).
Axes of the slice: x: 4, y: 4 (y_hi: 2, y_lo: 2; y = y_hi * 2 + y_lo), z: 4, core: 2. Of those that a mesh axis runs over, the one named last changes fastest.
Arguments:
- features: bfloat16 [96, 384, 1536], P('lat', 'lon'), may hold values from -6 to 6
- upstream: bfloat16 [96, 384, 1536], P('lat', 'lon'), may hold values from -6 to 6
- region_ids: int32 [96, 384], P('lat', 'lon'), may hold values from 0 to 3, as said below
- qkv_weight: bfloat16 [1536, 2304], replicated, may hold values from -0.15625 to 0.15625
- query_bias: float32 [768], replicated, may hold values from -3 to 3
- value_bias: float32 [768], replicated, may hold values from -3 to 3
- logit_scale: float32 [12], replicated, may hold values from 1 to 2.5
- pair_bias: float32 [12, 72, 72], replicated, may hold values from -3 to 3
- proj_weight: bfloat16 [1536, 768], replicated, may hold values from -0.21875 to 0.21875
- norm_gain: float32 [1536], replicated, may hold values from 0.25 to 1.75
Outputs:
- input_grad: bfloat16 [96, 384, 1536], P('lat', 'lon')
- qkv_weight_grad: float32 [1536, 2304], P(('lon', 'lat'))
- proj_weight_grad: float32 [1536, 768], P(('lon', 'lat'))
- gain_grad: float32 [1536], replicated
- query_bias_grad: float32 [768], replicated
- value_bias_grad: float32 [768], replicated
- scale_grad: float32 [12], replicated
- pair_grad: float32 [12, 72, 72], replicated
The draws below stay inside these ranges and needn't reach their ends.
Inputs may be any that keep to these rules, and one draw needn't show every extreme that they name: `region_ids`: within each window of 6 x 12 cells of the shifted grid, a boundary row and a boundary column split the cells into at most four rectangular classes: 2 for rows at or below the boundary row plus 1 for columns at or right of the boundary column; the window's last cell is always class 3.
All inputs are finite; a program needn't handle non-finite values.
Results may differ from the reference program's by a relative error of at most 0.015.
Values may be sent and summed in bfloat16 or wider, within the bound.
No kernel may reach another device: no remote copies, remote signals or barrier semaphores. Data moves between devices by JAX's collectives and lax.ppermute only.
A program may use at most 128 MiB of HBM per device.

```python
import jax
import jax.numpy as jnp
from jax import lax

C = 1536
HEADS = 12
HEAD_DIM = 64
WIN_H = 6
WIN_W = 12
SHIFT_H = 3
SHIFT_W = 6
HC = 768
WIN = 72
LAT = 96
LON = 384


def draw_region_ids(key, part):
    key = jax.random.fold_in(key, 11)
    row_key, col_key = jax.random.split(key)
    rows_win = LAT // WIN_H
    cols_win = LON // WIN_W
    row_bound = jax.random.randint(row_key, (rows_win, cols_win), 0, WIN_H)
    col_bound = jax.random.randint(col_key, (rows_win, cols_win), 0, WIN_W)
    row_bound = row_bound.at[0, 0].set(SHIFT_H)
    col_bound = col_bound.at[0, 0].set(SHIFT_W)
    row_full = jnp.repeat(jnp.repeat(row_bound, WIN_H, 0), WIN_W, 1)
    col_full = jnp.repeat(jnp.repeat(col_bound, WIN_H, 0), WIN_W, 1)
    row_pos = (jnp.arange(LAT, dtype=jnp.int32) % WIN_H)[:, None]
    col_pos = (jnp.arange(LON, dtype=jnp.int32) % WIN_W)[None, :]
    lower = (row_pos >= row_full).astype(jnp.int32)
    right = (col_pos >= col_full).astype(jnp.int32)
    return 2 * lower + right


def raised(drawn, key, source, target, parts, factor):
    def block_of(axis_at):
        return (jnp.arange(drawn.shape[axis_at]) // (drawn.shape[axis_at] // parts)).reshape((-1,) + (1,) * (drawn.ndim - 1 - axis_at))

    one_side = jax.random.permutation(key, parts)[block_of(target)]
    other_side = (block_of(target) + parts // 2) % parts
    return jnp.where((block_of(source) == one_side) | (block_of(source) == other_side), factor * drawn, drawn)


def block_levels(key, shape, cuts, low, largest):
    gain = 1.0
    for axis_at, blocks in cuts:
        heights = jax.random.uniform(jax.random.fold_in(jax.random.fold_in(key, 6), axis_at), (blocks,), jnp.float32, low / len(cuts), largest / len(cuts))
        gain = gain * jnp.repeat(jnp.exp(heights), shape[axis_at] // blocks).reshape((-1,) + (1,) * (len(shape) - 1 - axis_at))
    return gain


def noise(own_key, shape, deviation, reach, shards=(), held_as=jnp.bfloat16):
    result = deviation * jax.random.normal(own_key, shape, jnp.float32)
    if shards:
        result = result * block_levels(own_key, shape, shards, -0.22, 0.18)
    return jnp.clip(result, -reach, reach).astype(held_as)


def gaussian_with(stream_key, dims, spread, bound, cuts, heavy, kind=jnp.bfloat16):
    result = spread * jax.random.normal(stream_key, dims, jnp.float32)
    if cuts:
        result = result * block_levels(stream_key, dims, cuts, -0.22, 0.18)
    return jnp.clip(raised(result, jax.random.fold_in(stream_key, 3), *heavy), -bound, bound).astype(kind)


def setup_inputs(seed: int = 0) -> dict:
    keys = jax.random.split(jax.random.key(seed), 11)
    return {
        "features": gaussian_with(keys[0], (LAT, LON, C), 1.0, 6.0, ((0, 4), (1, 32)), (1, 2, 32, 2.75)),
        "upstream": gaussian_with(keys[1], (LAT, LON, C), 1.0, 6.0, ((0, 4), (1, 32)), (1, 2, 32, 2.75)),
        "region_ids": draw_region_ids(jax.random.fold_in(keys[10], 71), 0),
        "qkv_weight": noise(keys[3], (C, 3 * HC), C ** -0.5, 0.15625),
        "query_bias": noise(keys[4], (HC,), 0.5, 3.0, (), jnp.float32),
        "value_bias": noise(keys[5], (HC,), 0.5, 3.0, (), jnp.float32),
        "logit_scale": jnp.clip(jax.random.uniform(keys[6], (HEADS,), jnp.float32, 1.0, 2.5), 1.0, 2.5),
        "pair_bias": noise(keys[7], (HEADS, WIN, WIN), 1.0, 3.0, (), jnp.float32),
        "proj_weight": noise(keys[8], (C, HC), HC ** -0.5, 0.21875),
        "norm_gain": jnp.clip(1.0 + 0.15 * jax.random.normal(keys[9], (C,), jnp.float32), 0.25, 1.75),
    }


cosine_eps = 1e-06
norm_eps = 1e-05
CONTRACT_LAST = (((1,), (1,)), ((), ()))
CONTRACT_FIRST = (((0,), (0,)), ((), ()))

def contract(form, left, right):
    return jnp.einsum(form, left.astype(jnp.float32), right.astype(jnp.float32))

def window_backward(feature_win, upstream_win, region_win, qkv_weight, query_bias, value_bias, logit_scale, pair_bias, proj_weight, norm_gain):
    num_windows = feature_win.shape[0]
    window_len = feature_win.shape[1]
    model_width = feature_win.shape[2]
    inner_width = query_bias.shape[0]
    head_count = logit_scale.shape[0]
    head_size = inner_width // head_count
    flat_x = feature_win.reshape(num_windows * window_len, model_width)
    projected = jnp.dot(flat_x, qkv_weight, preferred_element_type=jnp.float32)
    projected = projected + jnp.concatenate([query_bias, jnp.zeros_like(query_bias), value_bias])
    shaped = projected.reshape(num_windows, window_len, 3, head_count, head_size)
    queries = shaped[:, :, 0]
    key_rows = shaped[:, :, 1]
    value_rows = shaped[:, :, 2]
    query_inv = lax.rsqrt(lax.optimization_barrier(jnp.sum(queries * queries, -1, keepdims=True)) + cosine_eps)
    key_inv = lax.rsqrt(lax.optimization_barrier(jnp.sum(key_rows * key_rows, -1, keepdims=True)) + cosine_eps)
    query_unit = queries * query_inv
    key_unit = key_rows * key_inv
    query_low = query_unit.astype(jnp.bfloat16)
    key_low = key_unit.astype(jnp.bfloat16)
    value_low = value_rows.astype(jnp.bfloat16)
    factor = jnp.exp(logit_scale)[None, :, None, None]
    cosine = contract('nqhd,nkhd->nhqk', query_low, key_low)
    same_region = region_win[:, :, None] == region_win[:, None, :]
    penalty = jnp.where(same_region, 0.0, -100.0).astype(jnp.float32)[:, None]
    scores = cosine * factor + pair_bias[None] + penalty
    exp_scores = jnp.exp(scores)
    attention = exp_scores / lax.optimization_barrier(jnp.sum(exp_scores, -1, keepdims=True))
    attention_low = attention.astype(jnp.bfloat16)
    attended = contract('nhqk,nkhd->nqhd', attention_low, value_low).astype(jnp.bfloat16)
    attended = attended.reshape(num_windows * window_len, inner_width)
    mixed = lax.dot_general(attended, proj_weight, CONTRACT_LAST, preferred_element_type=jnp.float32)
    center = mixed - lax.optimization_barrier(jnp.mean(mixed, -1, keepdims=True))
    inv_std = lax.rsqrt(lax.optimization_barrier(jnp.mean(center * center, -1, keepdims=True)) + norm_eps)
    normed = center * inv_std
    upstream_f = upstream_win.reshape(num_windows * window_len, model_width).astype(jnp.float32)
    gain_part = lax.optimization_barrier(jnp.sum(upstream_f * normed, 0))
    scaled = upstream_f * norm_gain
    mixed_grad = inv_std * (scaled - lax.optimization_barrier(jnp.mean(scaled, -1, keepdims=True)) - normed * lax.optimization_barrier(jnp.mean(scaled * normed, -1, keepdims=True)))
    mixed_low = mixed_grad.astype(jnp.bfloat16)
    attended_grad = jnp.dot(mixed_low, proj_weight, preferred_element_type=jnp.float32).astype(jnp.bfloat16)
    attended_grad = attended_grad.reshape(num_windows, window_len, head_count, head_size)
    prob_grad = contract('nqhd,nkhd->nhqk', attended_grad, value_low)
    value_grad = contract('nhqk,nqhd->nkhd', attention_low, attended_grad)
    score_grad = attention * (prob_grad - lax.optimization_barrier(jnp.sum(attention * prob_grad, -1, keepdims=True)))
    pair_part = lax.optimization_barrier(jnp.sum(score_grad, 0))
    scale_part = lax.optimization_barrier(jnp.sum(score_grad * cosine, (0, 2, 3))) * jnp.exp(logit_scale)
    cosine_grad = (score_grad * factor).astype(jnp.bfloat16)
    query_unit_grad = contract('nhqk,nkhd->nqhd', cosine_grad, key_low)
    key_unit_grad = contract('nhqk,nqhd->nkhd', cosine_grad, query_low)
    query_grad = query_inv * (query_unit_grad - query_unit * lax.optimization_barrier(jnp.sum(query_unit * query_unit_grad, -1, keepdims=True)))
    key_grad = key_inv * (key_unit_grad - key_unit * lax.optimization_barrier(jnp.sum(key_unit * key_unit_grad, -1, keepdims=True)))
    qbias_part = lax.optimization_barrier(jnp.sum(query_grad, (0, 1))).reshape(inner_width)
    vbias_part = lax.optimization_barrier(jnp.sum(value_grad, (0, 1))).reshape(inner_width)
    projected_grad = jnp.stack([query_grad, key_grad, value_grad], 2).reshape(num_windows * window_len, 3 * inner_width)
    projected_low = projected_grad.astype(jnp.bfloat16)
    branch = lax.dot_general(projected_low, qkv_weight, CONTRACT_LAST, preferred_element_type=jnp.float32)
    branch = branch.astype(jnp.bfloat16).reshape(num_windows, window_len, model_width)
    return (branch, flat_x, projected_low, mixed_low, attended, (gain_part, qbias_part, vbias_part, scale_part, pair_part))

def reference(features, upstream, region_ids, qkv_weight, query_bias, value_bias, logit_scale, pair_bias, proj_weight, norm_gain):
    rows_win = LAT // WIN_H
    cols_win = LON // WIN_W

    def split_windows(grid):
        depth = grid.shape[-1]
        grid = grid.reshape(rows_win, WIN_H, cols_win, WIN_W, depth).transpose(0, 2, 1, 3, 4)
        return grid.reshape(rows_win, cols_win, WIN_H * WIN_W, depth)
    shifted_features = jnp.roll(features, (-SHIFT_H, -SHIFT_W), (0, 1))
    shifted_upstream = jnp.roll(upstream, (-SHIFT_H, -SHIFT_W), (0, 1))
    feature_all = split_windows(shifted_features)
    upstream_all = split_windows(shifted_upstream)
    region_all = split_windows(region_ids[:, :, None])[..., 0]
    inner_width = HEADS * HEAD_DIM
    window_len = WIN_H * WIN_W
    initial = (jnp.zeros((C, 3 * inner_width), jnp.float32), jnp.zeros((C, inner_width), jnp.float32), jnp.zeros((C,), jnp.float32), jnp.zeros((inner_width,), jnp.float32), jnp.zeros((inner_width,), jnp.float32), jnp.zeros((HEADS,), jnp.float32), jnp.zeros((HEADS, window_len, window_len), jnp.float32))

    def step(carry, pieces):
        branch, flat_x, projected_low, mixed_low, attended, small = window_backward(pieces[0], pieces[1], pieces[2], qkv_weight, query_bias, value_bias, logit_scale, pair_bias, proj_weight, norm_gain)
        qkv_term = lax.dot_general(flat_x, projected_low, CONTRACT_FIRST, preferred_element_type=jnp.float32)
        proj_term = lax.dot_general(mixed_low, attended, CONTRACT_FIRST, preferred_element_type=jnp.float32)
        rest = jax.tree.map(jnp.add, tuple(carry[2:]), small)
        return ((carry[0] + qkv_term, carry[1] + proj_term) + tuple(rest), branch)
    totals, branches = lax.scan(step, initial, (feature_all, upstream_all, region_all))
    branch_grid = branches.reshape(rows_win, cols_win, WIN_H, WIN_W, C).transpose(0, 2, 1, 3, 4).reshape(LAT, LON, C)
    rolled_back = jnp.roll(branch_grid, (SHIFT_H, SHIFT_W), (0, 1))
    input_grad = (upstream.astype(jnp.float32) + rolled_back.astype(jnp.float32)).astype(jnp.bfloat16)
    return (input_grad, totals[0], totals[1], totals[2], totals[3], totals[4], totals[5], totals[6])
```

```python
import functools

import jax
import jax.numpy as jnp
import numpy as np
from jax import lax
from jax.experimental import pallas as pl
from jax.experimental.pallas import tpu as pltpu
from jax.sharding import Mesh
from jax.sharding import PartitionSpec as P

HEADS = 12
HEAD_DIM = 64
WIN_H = 6
WIN_W = 12
SHIFT_H = 3
SHIFT_W = 6
WIN = 72
C = 1536
HC = 768
HALF = 384
CELLS = 288
WINDOWS = 4
COSINE_EPS = 1e-06
NORM_EPS = 1e-05

F32 = jnp.float32
BF16 = jnp.bfloat16
LON = ("yh", "x", "z")
LAT = ("yl", "c")
Y = ("yh", "yl")
ORDERS = (("x", "y", "z"), ("y", "z", "x"), ("z", "x", "y"))
AXES = {"x": ("x",), "y": Y, "z": ("z",)}
KEEP = np.array([[[0, 3], [1, 2], [1, 2], [0, 3]], [[0, 1], [0, 1], [2, 3], [2, 3]]], np.int32)
SEND = np.array([[[1, 2], [0, 3], [0, 3], [1, 2]], [[2, 3], [2, 3], [0, 1], [0, 1]]], np.int32)
FIRST = np.concatenate([KEEP, SEND], -1)
SECOND = np.array([[[0, 1], [0, 1], [1, 0], [1, 0]], [[0, 1], [1, 0], [0, 1], [1, 0]]], np.int32)
PAIR_ROWS = 432
SMALL_ROWS = 464
NT = (((1,), (1,)), ((), ()))
TN = (((0,), (0,)), ((), ()))
NN = (((1,), (0,)), ((), ()))
VMEM = pl.BlockSpec(memory_space=pltpu.VMEM)
SMEM = pl.BlockSpec(memory_space=pltpu.SMEM)


def dot(left, right, dims=NN):
    return lax.dot_general(left, right, dims, preferred_element_type=F32)


def call(body, outs, operands, scalars=1, scratch=(), flops=0, name=None):
    moved = sum(int(np.prod(o.shape)) * o.dtype.itemsize for o in (*outs, *operands))
    return pl.pallas_call(
        body,
        out_shape=list(outs),
        in_specs=[SMEM] * scalars + [VMEM] * (len(operands) - scalars),
        out_specs=[VMEM] * len(outs),
        scratch_shapes=list(scratch),
        compiler_params=pltpu.CompilerParams(vmem_limit_bytes=52 * 2**20),
        cost_estimate=pl.CostEstimate(flops=flops, bytes_accessed=moved, transcendentals=0),
        name=name,
    )(*operands)


def shape(dims, dtype):
    return jax.ShapeDtypeStruct(dims, dtype)


def head_sum(value):
    rows = lax.broadcasted_iota(jnp.int32, (128, 128), 0) // HEAD_DIM
    cols = lax.broadcasted_iota(jnp.int32, (128, 128), 1) // HEAD_DIM
    ones = (rows == cols).astype(F32).astype(BF16)
    high = value.astype(BF16)
    low = (value - high.astype(F32)).astype(BF16)
    return dot(high, ones) + dot(low, ones)


def low_half(rows):
    return lax.broadcasted_iota(jnp.int32, (rows, 128), 1) < HEAD_DIM


def stacked(value):
    mask = low_half(WIN)
    return jnp.concatenate([jnp.where(mask, value, 0.0), jnp.where(mask, 0.0, value)], 0).astype(BF16)


def unstacked(value):
    return jnp.where(low_half(WIN), value[:WIN], value[WIN:])


def normalized(rows):
    inv = lax.rsqrt(head_sum(rows * rows) + COSINE_EPS)
    return rows * inv, inv


def penalties(region_row, region_col):
    out = []
    for w in range(WINDOWS):
        same = region_row[w : w + 1, :] == region_col[w * WIN : (w + 1) * WIN, :]
        one = jnp.where(same, 0.0, -100.0).astype(F32)
        out.append(jnp.concatenate([one, one], 0))
    return out


def two_heads(scale_ref, head):
    top = lax.broadcasted_iota(jnp.int32, (2 * WIN, 1), 0) < WIN
    return jnp.where(top, scale_ref[head], scale_ref[head + 1])


def softmax_of(cosine, factor, bias, penalty):
    exp_scores = jnp.exp(cosine * factor + bias + penalty)
    return exp_scores / jnp.sum(exp_scores, -1, keepdims=True)


def forward_body(scale, x, w, bias, pair_bias, row, col, projected, attended):
    pens = penalties(row[...], col[...])
    xv = x[...]
    for g in range(3):
        for j in range(3):
            lo = j * HC + g * 256
            projected[:, lo : lo + 256] = dot(xv, w[:, lo : lo + 256]) + bias[:, lo : lo + 256]
        for half in range(2):
            lo = g * 256 + half * 128
            head = lo // HEAD_DIM
            factor = two_heads(scale, head)
            q = normalized(projected[:, lo : lo + 128])[0]
            k = normalized(projected[:, HC + lo : HC + lo + 128])[0]
            v = projected[:, 2 * HC + lo : 2 * HC + lo + 128]
            pb = pair_bias[head * WIN : (head + 2) * WIN, :]
            outs = []
            for n in range(WINDOWS):
                at = slice(n * WIN, (n + 1) * WIN)
                cosine = dot(stacked(q[at]), k[at].astype(BF16), NT)
                attention = softmax_of(cosine, factor, pb, pens[n])
                outs.append(unstacked(dot(attention.astype(BF16), v[at].astype(BF16))))
            attended[:, lo : lo + 128] = jnp.concatenate(outs, 0).astype(BF16)


def norm_body(attended, u, pw, gain, mixed_low, attended_grad, gain_part):
    total = jnp.zeros((1, C), F32)
    for r in range(3):
        at = slice(r * 96, (r + 1) * 96)
        mixed = dot(attended[at, :], pw[...], NT)
        center = mixed - jnp.mean(mixed, -1, keepdims=True)
        inv_std = lax.rsqrt(jnp.mean(center * center, -1, keepdims=True) + NORM_EPS)
        normed = center * inv_std
        up = u[at, :].astype(F32)
        total = total + jnp.sum(up * normed, 0, keepdims=True)
        scaled = up * gain[...]
        grad = inv_std * (
            scaled
            - jnp.mean(scaled, -1, keepdims=True)
            - normed * jnp.mean(scaled * normed, -1, keepdims=True)
        )
        low = grad.astype(BF16)
        mixed_low[at, :] = low
        attended_grad[at, :] = dot(low, pw[...]).astype(BF16).astype(F32)
    gain_part[...] = total


def attention_body(
    side, scale, projected, attended_grad, gain_part, pair_bias, row, col, grads, small, gq, gk, gv
):
    pens = penalties(row[...], col[...])
    which = side[0]
    base = which * HALF
    small[...] = jnp.zeros_like(small)
    lines = []
    scale_line = jnp.zeros((1, 128), F32)
    lane = lax.broadcasted_iota(jnp.int32, (1, 128), 1)
    for hp in range(3):
        lo = pl.multiple_of(base + hp * 128, 128)
        head = which * 6 + 2 * hp
        factor = two_heads(scale, head)
        q, q_inv = normalized(projected[:, pl.ds(lo, 128)])
        k, k_inv = normalized(projected[:, pl.ds(pl.multiple_of(lo + HC, 128), 128)])
        v = projected[:, pl.ds(pl.multiple_of(lo + 2 * HC, 128), 128)]
        da = attended_grad[:, pl.ds(lo, 128)]
        pb = pair_bias[pl.ds(pl.multiple_of(head * WIN, 8), 2 * WIN), :]
        pair = jnp.zeros((2 * WIN, WIN), F32)
        scaled = jnp.zeros((2 * WIN, WIN), F32)
        for n in range(WINDOWS):
            at = slice(n * WIN, (n + 1) * WIN)
            qs = stacked(q[at])
            das = stacked(da[at])
            kb = k[at].astype(BF16)
            cosine = dot(qs, kb, NT)
            attention = softmax_of(cosine, factor, pb, pens[n])
            prob_grad = dot(das, v[at].astype(BF16), NT)
            gv[at, :] = dot(attention.astype(BF16), das, TN)
            score_grad = attention * (
                prob_grad - jnp.sum(attention * prob_grad, -1, keepdims=True)
            )
            pair = pair + score_grad
            scaled = scaled + score_grad * cosine
            cosine_grad = (score_grad * factor).astype(BF16)
            gq[at, :] = unstacked(dot(cosine_grad, kb))
            gk[at, :] = dot(cosine_grad, qs, TN)
        small[hp * 2 * WIN : (hp + 1) * 2 * WIN, :WIN] = pair.astype(BF16)
        for i in range(2):
            one = jnp.sum(jnp.sum(scaled[i * WIN : (i + 1) * WIN], 0, keepdims=True), 1, keepdims=True)
            scale_line = scale_line + jnp.where(lane == 2 * hp + i, one * scale[head + i], 0.0)
        q_grad = q_inv * (gq[...] - q * head_sum(q * gq[...]))
        k_grad = k_inv * (gk[...] - k * head_sum(k * gk[...]))
        cols = slice(hp * 128, (hp + 1) * 128)
        grads[:, cols] = q_grad.astype(BF16)
        grads[:, HALF + hp * 128 : HALF + (hp + 1) * 128] = k_grad.astype(BF16)
        grads[:, 2 * HALF + hp * 128 : 2 * HALF + (hp + 1) * 128] = gv[...].astype(BF16)
        lines.append(jnp.sum(q_grad, 0, keepdims=True))
        lines.append(jnp.sum(gv[...], 0, keepdims=True))
    for i in range(6):
        lines.append(gain_part[:, pl.ds(pl.multiple_of(which * HC + i * 128, 128), 128)])
    lines.append(scale_line)
    lines.append(jnp.zeros((3, 128), F32))
    block = jnp.concatenate(lines, 0)
    high = block.astype(BF16)
    low = (block - high.astype(F32)).astype(BF16)
    small[PAIR_ROWS : PAIR_ROWS + 16, :] = high
    small[PAIR_ROWS + 16 :, :] = low


def add_small_body(left, right, out):
    a, b = left[...].astype(F32), right[...].astype(F32)
    out[:PAIR_ROWS, :] = (a[:PAIR_ROWS] + b[:PAIR_ROWS]).astype(BF16)
    block = (a[PAIR_ROWS : PAIR_ROWS + 16] + a[PAIR_ROWS + 16 :]) + (
        b[PAIR_ROWS : PAIR_ROWS + 16] + b[PAIR_ROWS + 16 :]
    )
    high = block.astype(BF16)
    out[PAIR_ROWS : PAIR_ROWS + 16, :] = high
    out[PAIR_ROWS + 16 :, :] = (block - high.astype(F32)).astype(BF16)


def row_of(place):
    y = place["y"]
    return 24 * ((y // 2) * 32 + place["x"] * 8 + place["z"] * 2 + y % 2)


def weight_body(order, x0, x1, p0, p1, m0, m1, a0, a1, *rest):
    outs, (left, grads, total) = rest[:6], rest[6:]
    left[:CELLS, :] = x0[...]
    left[CELLS:, :] = x1[...]
    grads[:CELLS, :] = p0[...]
    grads[CELLS:, :] = p1[...]
    for m in range(4):
        at = slice(m * 384, (m + 1) * 384)
        part = dot(left[:, at], grads[...], TN)
        for j in range(3):
            total[at, j * 512 : j * 512 + HALF] = part[:, j * HALF : (j + 1) * HALF]
    left[:CELLS, :] = m0[...]
    left[CELLS:, :] = m1[...]
    grads[:CELLS, :HALF] = a0[...]
    grads[CELLS:, :HALF] = a1[...]
    for m in range(4):
        at = slice(m * 384, (m + 1) * 384)
        part = dot(left[:, at], grads[:, :HALF], TN)
        for j in range(3):
            total[at, j * 512 + HALF : (j + 1) * 512] = part[:, j * 128 : (j + 1) * 128]
    for j in range(3):
        cols = slice(j * 512, (j + 1) * 512)
        for i in range(4):
            out = outs[2 * j + i // 2]
            for second in range(4):
                for third in range(4):
                    places = (order[4 * j + i], second, third)
                    start = row_of(dict(zip(ORDERS[j], places)))
                    rows = pl.ds(pl.multiple_of(start, 8), 24)
                    out[i % 2, second, third] = total[rows, cols].astype(BF16)


def halve_body(order, keep, recv, keep_out, send_out):
    count = keep_out.shape[0]
    for i in range(count):
        for base, out in ((0, keep_out), (count, send_out)):
            at = order[base + i]
            out[i] = (keep[at].astype(F32) + recv[at].astype(F32)).astype(BF16)


def branch_body(side, w, mine, theirs, branch, grads):
    which = side[0]
    for j in range(3):
        cols = slice(j * HALF, (j + 1) * HALF)
        grads[:, pl.ds(pl.multiple_of(j * HC + which * HALF, 128), HALF)] = mine[:, cols]
        grads[:, pl.ds(pl.multiple_of(j * HC + (1 - which) * HALF, 128), HALF)] = theirs[:, cols]
    for n in range(6):
        at = slice(n * 256, (n + 1) * 256)
        branch[:, at] = dot(grads[...], w[at, :], NT).astype(BF16)


def permuted(value, axes, target):
    sizes = [lax.axis_size(a) for a in axes]
    pairs = []
    for source in range(int(np.prod(sizes))):
        place = np.unravel_index(source, sizes)
        to = target(*[int(v) for v in place])
        pairs.append((source, int(np.ravel_multi_index(to, sizes))))
    return lax.ppermute(value, axes, pairs)


def lon_step(value, steps):
    return permuted(value, LON, lambda *at: np.unravel_index((np.ravel_multi_index(at, (2, 4, 4)) + steps) % 32, (2, 4, 4)))


def lat_step(value, steps):
    return permuted(value, LAT, lambda *at: np.unravel_index((np.ravel_multi_index(at, (2, 2)) + steps) % 4, (2, 2)))


def both_step(value, steps):
    def target(yh, x, z, yl, c):
        lon = (np.ravel_multi_index((yh, x, z), (2, 4, 4)) + steps) % 32
        lat = (yl * 2 + c + steps) % 4
        return (*np.unravel_index(lon, (2, 4, 4)), lat // 2, lat % 2)

    return permuted(value, LON + LAT, target)


def core_swap(value):
    return permuted(value, ("c",), lambda c: (1 - c,))


def ring_swap(value, axis, step):
    def partner(place, c):
        return place ^ 1 if (step == 0) == (c == 0) else 3 - place

    if axis == "y":
        def target(yh, yl, c):
            to = partner(yh * 2 + yl, c)
            return (to // 2, to % 2, c)
    else:
        def target(place, c):
            return (partner(place, c), c)

    return permuted(value, AXES[axis] + ("c",), target)


def rolled(grid):
    lon = lon_step(grid[SHIFT_H:, :SHIFT_W].reshape(-1, C), -1).reshape(-1, SHIFT_W, C)
    lat = lat_step(grid[:SHIFT_H, SHIFT_W:].reshape(-1, C), -1).reshape(-1, SHIFT_W, C)
    both = both_step(grid[:SHIFT_H, :SHIFT_W].reshape(-1, C), -1).reshape(-1, SHIFT_W, C)
    top = jnp.concatenate([grid[SHIFT_H:, SHIFT_W:], lon], 1)
    bottom = jnp.concatenate([lat, both], 1)
    return jnp.concatenate([top, bottom], 0).reshape(-1, C)


def shards(
    features,
    upstream,
    region_ids,
    qkv_weight,
    query_bias,
    value_bias,
    logit_scale,
    pair_bias,
    proj_weight,
    norm_gain,
):
    core = lax.axis_index("c")
    place = {"x": lax.axis_index("x"), "z": lax.axis_index("z"), "y": lax.axis_index("yh") * 2 + lax.axis_index("yl")}
    mine = core.astype(jnp.int32).reshape(1)
    theirs = 1 - mine
    scale = jnp.exp(logit_scale)
    bias = jnp.concatenate([query_bias, jnp.zeros_like(query_bias), value_bias]).reshape(1, -1)
    pair_rows = pair_bias.reshape(HEADS * WIN, WIN)
    region_row = region_ids.reshape(WINDOWS, WIN)
    region_col = region_ids.reshape(-1, 1)
    gain = norm_gain.reshape(1, C)

    x = rolled(features)
    u = rolled(upstream)
    x_other = core_swap(x)
    projected, attended = call(
        forward_body,
        [shape((CELLS, 3 * HC), F32), shape((CELLS, HC), BF16)],
        [scale, x, qkv_weight, bias, pair_rows, region_row, region_col],
        flops=2 * CELLS * C * 3 * HC,
        name="forward",
    )
    mixed_low, attended_grad, gain_part = call(
        norm_body,
        [shape((CELLS, C), BF16), shape((CELLS, HC), F32), shape((1, C), F32)],
        [attended, u, proj_weight, gain],
        scalars=0,
        flops=4 * CELLS * C * HC,
        name="norm",
    )
    mixed_other = core_swap(mixed_low)
    attended_theirs = lax.dynamic_slice(attended, (0, theirs[0] * HALF), (CELLS, HALF))
    attended_mine = lax.dynamic_slice(attended, (0, mine[0] * HALF), (CELLS, HALF))
    attended_other = core_swap(attended_theirs)

    def attention(side):
        return call(
            attention_body,
            [shape((CELLS, 3 * HALF), BF16), shape((SMALL_ROWS, 128), BF16)],
            [side, scale, projected, attended_grad, gain_part, pair_rows, region_row, region_col],
            scalars=2,
            scratch=[pltpu.VMEM((CELLS, 128), F32)] * 3,
            flops=2 * CELLS * WIN * 128 * 6 * 3,
            name="attention",
        )

    grads_theirs, small_theirs = attention(theirs)
    grads_other = core_swap(grads_theirs)
    small_other = core_swap(small_theirs)
    grads_mine, small_mine = attention(mine)

    def add_small(left, right):
        return call(add_small_body, [shape((SMALL_ROWS, 128), BF16)], [left, right], scalars=0, name="add_small")[0]

    small = add_small(small_mine, small_other)

    def table(values, axis):
        return jnp.asarray(values)[core, place[axis]]

    orders = jnp.concatenate([table(FIRST, names[0]) for names in ORDERS])
    parts = call(
        weight_body,
        [shape((2, 4, 4, 24, 512), BF16)] * 6,
        [orders, x, x_other, grads_mine, grads_other, mixed_low, mixed_other, attended_mine, attended_other],
        scratch=[
            pltpu.VMEM((2 * CELLS, C), BF16),
            pltpu.VMEM((2 * CELLS, 3 * HALF), BF16),
            pltpu.VMEM((C, C), F32),
        ],
        flops=4 * CELLS * C * C,
        name="weights",
    )
    (branch,) = call(
        branch_body,
        [shape((CELLS, C), BF16)],
        [mine, qkv_weight, grads_mine, grads_theirs],
        scratch=[pltpu.VMEM((CELLS, 3 * HC), BF16)],
        flops=2 * CELLS * C * 3 * HC,
        name="branch",
    )

    def halve(order, keep, recv, name):
        half = (order.shape[0] // 2,) + keep.shape[1:]
        keep, send = call(halve_body, [shape(half, BF16)] * 2, [order, keep, recv], name=name)
        if half[0] == 1:
            keep, send = keep.reshape(half[1:]), send.reshape(half[1:])
        return keep, send

    sums = []
    for j, names in enumerate(ORDERS):
        keep, send = parts[2 * j], parts[2 * j + 1]
        for step in range(5):
            recv = ring_swap(send, names[step // 2], step % 2)
            if step % 2 == 0:
                keep, send = halve(table(SECOND, names[step // 2]), keep, recv, "halve")
            else:
                keep, send = halve(table(FIRST, names[step // 2 + 1]), keep, recv, "quarter")
        recv = ring_swap(send, names[2], 1)
        sums.append(keep.astype(F32) + recv.astype(F32))

    for axis in ("x", "y", "z"):
        for step in range(2):
            small = add_small(small, ring_swap(small, axis, step))

    total = jnp.stack(sums)
    top, bottom = total[:, :12], total[:, 12:]
    rows_mine = jnp.where(core == 0, top, bottom)
    rows_other = core_swap(jnp.where(core == 0, bottom, top))
    first = jnp.where(core == 0, rows_mine, rows_other)
    second = jnp.where(core == 0, rows_other, rows_mine)
    qkv_weight_grad = jnp.concatenate(
        [piece for j in range(3) for piece in (first[j, :, :HALF], second[j, :, :HALF])], 1
    )
    proj_weight_grad = jnp.concatenate(
        [side[j, :, HALF:] for side in (first, second) for j in range(3)], 1
    )

    small_far = core_swap(small)
    lows = jnp.where(core == 0, small, small_far).astype(F32)
    highs = jnp.where(core == 0, small_far, small).astype(F32)
    both = jnp.stack([lows, highs])
    pair_grad = both[:, :PAIR_ROWS, :WIN].reshape(HEADS, WIN, WIN)
    lines = both[:, PAIR_ROWS : PAIR_ROWS + 16] + both[:, PAIR_ROWS + 16 :]
    query_bias_grad = lines[:, 0:6:2].reshape(HC)
    value_bias_grad = lines[:, 1:6:2].reshape(HC)
    gain_grad = lines[:, 6:12].reshape(C)
    scale_grad = lines[:, 12, :6].reshape(HEADS)

    grid = branch.reshape(24, 12, C)
    keep_rows = 24 - SHIFT_H
    lon = lon_step(grid[:keep_rows, SHIFT_W:].reshape(-1, C), 1).reshape(-1, SHIFT_W, C)
    lat = lat_step(grid[keep_rows:, :SHIFT_W].reshape(-1, C), 1).reshape(-1, SHIFT_W, C)
    corner = both_step(grid[keep_rows:, SHIFT_W:].reshape(-1, C), 1).reshape(-1, SHIFT_W, C)
    back = jnp.concatenate(
        [
            jnp.concatenate([corner, lat], 1),
            jnp.concatenate([lon, grid[:keep_rows, :SHIFT_W]], 1),
        ],
        0,
    )
    input_grad = (upstream.astype(F32) + back.astype(F32)).astype(BF16)
    return (
        input_grad,
        qkv_weight_grad,
        proj_weight_grad,
        gain_grad,
        query_bias_grad,
        value_bias_grad,
        scale_grad,
        pair_grad,
    )


def solution(mesh):
    fine = Mesh(mesh.devices.reshape(2, 4, 4, 2, 2), ("yh", "x", "z", "yl", "c"))
    every = LON + LAT
    return jax.shard_map(
        shards,
        mesh=fine,
        in_specs=(P(LAT, LON, None), P(LAT, LON, None), P(LAT, LON)) + (P(),) * 7,
        out_specs=(P(LAT, LON, None), P(every, None), P(every, None)) + (P(),) * 5,
        check_vma=False,
    )
```

```python
import functools

import jax
import jax.numpy as jnp
import numpy as np
from jax import lax
from jax.experimental import pallas as pl
from jax.experimental.pallas import tpu as pltpu
from jax.sharding import Mesh
from jax.sharding import PartitionSpec as P

HEADS = 12
HEAD_DIM = 64
WIN_H = 6
WIN_W = 12
SHIFT_H = 3
SHIFT_W = 6
WIN = 72
C = 1536
HC = 768
HALF = 384
CELLS = 288
WINDOWS = 4
COSINE_EPS = 1e-06
NORM_EPS = 1e-05

F32 = jnp.float32
BF16 = jnp.bfloat16
LON = ("yh", "x", "z")
LAT = ("yl", "c")
Y = ("yh", "yl")
ORDERS = (("x", "y", "z"), ("y", "z", "x"), ("z", "x", "y"))
AXES = {"x": ("x",), "y": Y, "z": ("z",)}
KEEP = np.array([[[0, 3], [1, 2], [1, 2], [0, 3]], [[0, 1], [0, 1], [2, 3], [2, 3]]], np.int32)
SEND = np.array([[[1, 2], [0, 3], [0, 3], [1, 2]], [[2, 3], [2, 3], [0, 1], [0, 1]]], np.int32)
FIRST = np.concatenate([KEEP, SEND], -1)
SECOND = np.array([[[0, 1], [0, 1], [1, 0], [1, 0]], [[0, 1], [1, 0], [0, 1], [1, 0]]], np.int32)
BLOCK = (24, 512)
EXTRA = 2
NT = (((1,), (1,)), ((), ()))
TN = (((0,), (0,)), ((), ()))
NN = (((1,), (0,)), ((), ()))
VMEM = pl.BlockSpec(memory_space=pltpu.VMEM)
HBM = pl.BlockSpec(memory_space=pltpu.HBM)
SMEM = pl.BlockSpec(memory_space=pltpu.SMEM)


def dot(left, right, dims=NN):
    return lax.dot_general(left, right, dims, preferred_element_type=F32)


def cost(outs, operands, flops):
    moved = sum(int(np.prod(o.shape)) * o.dtype.itemsize for o in (*outs, *operands))
    return pl.CostEstimate(flops=flops, bytes_accessed=moved, transcendentals=0)


def call(body, outs, operands, scalars=1, scratch=(), flops=0, vmem=16, far=(), name=None):
    specs = [SMEM] * scalars + [VMEM] * (len(operands) - scalars)
    for i in far:
        specs[i] = HBM
    return pl.pallas_call(
        body,
        out_shape=list(outs),
        in_specs=specs,
        out_specs=[VMEM] * len(outs),
        scratch_shapes=list(scratch),
        compiler_params=pltpu.CompilerParams(vmem_limit_bytes=vmem * 2**20),
        cost_estimate=cost(outs, operands, flops),
        name=name,
    )(*operands)


def grid_call(body, grid, scalars, ins, outs, scratch=(), flops=0, vmem=16, name=None):
    operands = [array for array, _, _ in ins]
    results = [result for result, _, _ in outs]
    spec = pltpu.PrefetchScalarGridSpec(
        num_scalar_prefetch=len(scalars),
        grid=grid,
        in_specs=[pl.BlockSpec(block, at) for _, block, at in ins],
        out_specs=[pl.BlockSpec(block, at) for _, block, at in outs],
        scratch_shapes=list(scratch),
    )
    return pl.pallas_call(
        body,
        grid_spec=spec,
        out_shape=results,
        compiler_params=pltpu.CompilerParams(vmem_limit_bytes=vmem * 2**20),
        cost_estimate=cost(results, operands, flops),
        name=name,
    )(*scalars, *operands)


def shape(dims, dtype):
    return jax.ShapeDtypeStruct(dims, dtype)


def head_sum(value):
    rows = lax.broadcasted_iota(jnp.int32, (128, 128), 0) // HEAD_DIM
    cols = lax.broadcasted_iota(jnp.int32, (128, 128), 1) // HEAD_DIM
    ones = (rows == cols).astype(F32).astype(BF16)
    high = value.astype(BF16)
    low = (value - high.astype(F32)).astype(BF16)
    return dot(high, ones) + dot(low, ones)


def low_half(rows):
    return lax.broadcasted_iota(jnp.int32, (rows, 128), 1) < HEAD_DIM


def stacked(value):
    mask = low_half(WIN)
    return jnp.concatenate([jnp.where(mask, value, 0.0), jnp.where(mask, 0.0, value)], 0).astype(BF16)


def unstacked(value):
    return jnp.where(low_half(WIN), value[:WIN], value[WIN:])


def normalized(rows):
    inv = lax.rsqrt(head_sum(rows * rows) + COSINE_EPS)
    return rows * inv, inv


def penalties(region_row, region_col):
    out = []
    for w in range(WINDOWS):
        same = region_row[w : w + 1, :] == region_col[w * WIN : (w + 1) * WIN, :]
        one = jnp.where(same, 0.0, -100.0).astype(F32)
        out.append(jnp.concatenate([one, one], 0))
    return out


def two_heads(scale_ref, head):
    top = lax.broadcasted_iota(jnp.int32, (2 * WIN, 1), 0) < WIN
    return jnp.where(top, scale_ref[head], scale_ref[head + 1])


def softmax_of(scores):
    exp_scores = [jnp.exp(one) for one in scores]
    sums = [jnp.sum(one, -1, keepdims=True) for one in exp_scores]
    return [one / total for one, total in zip(exp_scores, sums)]


SPANS = [slice(n * WIN, (n + 1) * WIN) for n in range(WINDOWS)]


def window_rows(own, lon, lat, both, grid, rows):
    for j in range(12):
        column, low = (own[j + SHIFT_W], lat) if j < SHIFT_W else (lon[j - SHIFT_W], both)
        at = j % SHIFT_W * SHIFT_H
        column = jnp.concatenate(
            [column.astype(F32)[SHIFT_H:], low[...].astype(F32)[at : at + SHIFT_H]], 0
        )
        for t in range(12):
            grid[t, j * 24 : (j + 1) * 24, :] = column[:, t * 128 : (t + 1) * 128]
    for r in range(24):
        for t in range(12):
            rows[r * 12 : (r + 1) * 12, t * 128 : (t + 1) * 128] = grid[t, pl.ds(r, 12, stride=24), :]


def forward_body(
    scale, own, lon, lat, both, w, bias, pair_bias, row, col, x, projected, attended, grid, rows, wide, sems
):
    copies = []
    for g in range(3):
        for j in range(3):
            at = pl.ds(j * HC + g * 256, 256)
            copies.append(pltpu.make_async_copy(w.at[:, at], wide.at[:, at], sems.at[3 * g + j]))
            copies[-1].start()
    window_rows(own, lon, lat, both, grid, rows)
    x[...] = rows[...].astype(BF16)
    pens = penalties(row[...], col[...])
    for g in range(3):
        for j in range(3):
            lo = j * HC + g * 256
            copies[3 * g + j].wait()
            projected[:, lo : lo + 256] = dot(x[...], wide[:, lo : lo + 256]) + bias[:, lo : lo + 256]
        for half in range(2):
            lo = g * 256 + half * 128
            head = lo // HEAD_DIM
            factor = two_heads(scale, head)
            q = normalized(projected[:, lo : lo + 128])[0]
            k = normalized(projected[:, HC + lo : HC + lo + 128])[0]
            v = projected[:, 2 * HC + lo : 2 * HC + lo + 128]
            pb = pair_bias[head * WIN : (head + 2) * WIN, :]
            cosines = [dot(stacked(q[at]), k[at].astype(BF16), NT) for at in SPANS]
            attention = softmax_of([c * factor + pb + pen for c, pen in zip(cosines, pens)])
            outs = [dot(a.astype(BF16), v[at].astype(BF16)) for a, at in zip(attention, SPANS)]
            attended[:, lo : lo + 128] = jnp.concatenate([unstacked(o) for o in outs], 0).astype(BF16)


def norm_part(attended, rows, pw, gain, mixed_low, attended_grad, gain_part, mixed_all):
    for n in range(6):
        at = slice(n * 256, (n + 1) * 256)
        mixed_all[:, at] = dot(attended[...], pw[at, :], NT)
    total = jnp.zeros((1, C), F32)
    for r in range(6):
        at = slice(r * 48, (r + 1) * 48)
        mixed = mixed_all[at, :]
        center = mixed - jnp.mean(mixed, -1, keepdims=True)
        inv_std = lax.rsqrt(jnp.mean(center * center, -1, keepdims=True) + NORM_EPS)
        normed = center * inv_std
        up = rows[at, :]
        total = total + jnp.sum(up * normed, 0, keepdims=True)
        scaled = up * gain[...]
        grad = inv_std * (
            scaled
            - jnp.mean(scaled, -1, keepdims=True)
            - normed * jnp.mean(scaled * normed, -1, keepdims=True)
        )
        mixed_low[at, :] = grad.astype(BF16)
    gain_part[...] = total
    for n in range(3):
        at = slice(n * 256, (n + 1) * 256)
        attended_grad[:, at] = dot(mixed_low[...], pw[:, at]).astype(BF16).astype(F32)


def attention_pair(scale, head, q, k, v, da, pb, pens, gains):
    factor = two_heads(scale, head)
    q, q_inv = normalized(q)
    k, k_inv = normalized(k)
    qs = [stacked(q[at]) for at in SPANS]
    das = [stacked(da[at]) for at in SPANS]
    kb = [k[at].astype(BF16) for at in SPANS]
    vb = [v[at].astype(BF16) for at in SPANS]
    cosines = [dot(a, b, NT) for a, b in zip(qs, kb)]
    prob_grads = [dot(a, b, NT) for a, b in zip(das, vb)]
    attention = softmax_of([c * factor + pb + pen for c, pen in zip(cosines, pens)])
    v_grad = jnp.concatenate([dot(a.astype(BF16), b, TN) for a, b in zip(attention, das)], 0)
    means = [jnp.sum(a * p, -1, keepdims=True) for a, p in zip(attention, prob_grads)]
    score_grads = [a * (p - m) for a, p, m in zip(attention, prob_grads, means)]
    cosine_grads = [(s * factor).astype(BF16) for s in score_grads]
    gq = jnp.concatenate([unstacked(dot(c, b)) for c, b in zip(cosine_grads, kb)], 0)
    gk = jnp.concatenate([dot(c, b, TN) for c, b in zip(cosine_grads, qs)], 0)
    pair = (score_grads[0] + score_grads[1]) + (score_grads[2] + score_grads[3])
    scaled = sum(s * c for s, c in zip(score_grads, cosines))
    lane = lax.broadcasted_iota(jnp.int32, (1, 128), 1)
    scale_line = jnp.zeros((1, 128), F32)
    for i in range(2):
        one = jnp.sum(jnp.sum(scaled[i * WIN : (i + 1) * WIN], 0, keepdims=True), 1, keepdims=True)
        scale_line = scale_line + jnp.where(lane == i, one * scale[head + i], 0.0)
    q_grad = q_inv * (gq - q * head_sum(q * gq))
    k_grad = k_inv * (gk - k * head_sum(k * gk))
    lines = jnp.concatenate(
        [
            jnp.sum(q_grad, 0, keepdims=True),
            jnp.sum(v_grad, 0, keepdims=True),
            scale_line,
            gains[:, :128],
            gains[:, 128:],
            jnp.zeros((11, 128), F32),
        ],
        0,
    )
    return (q_grad, k_grad, v_grad), pair, lines


def store_pair(grads, small, at, parts, pair, lines):
    for i, part in enumerate(parts):
        grads[:, at * HALF + i * 128 : at * HALF + (i + 1) * 128] = part.astype(BF16)
    rows = slice(at * 48, (at + 1) * 48)
    for g in range(3):
        small[rows, g * 128 : g * 128 + WIN] = pair[g * 48 : (g + 1) * 48]
    small[at * 48 : at * 48 + 16, 384:] = lines


def attention_body(
    side, scale, q_ref, k_ref, v_ref, da_ref, pair_bias, row, col, gain_part, grads, small
):
    pens = penalties(row[...], col[...])
    head = side[0] * 6 + 2 * pl.program_id(0)
    small[...] = jnp.zeros_like(small)
    store_pair(
        grads,
        small,
        0,
        *attention_pair(
            scale, head, q_ref[...], k_ref[...], v_ref[...], da_ref[...], pair_bias[...], pens, gain_part[...]
        ),
    )


def backward_body(
    side,
    scale,
    attended,
    own,
    lon,
    lat,
    both,
    pw,
    gain,
    projected,
    pair_bias,
    row,
    col,
    mixed_low,
    attended_grad,
    gain_part,
    grads,
    small,
    grid,
    rows,
    mixed_all,
):
    window_rows(own, lon, lat, both, grid, rows)
    norm_part(attended, rows, pw, gain, mixed_low, attended_grad, gain_part, mixed_all)
    pens = penalties(row[...], col[...])
    small[...] = jnp.zeros_like(small)
    for hp in range(3):
        def lanes(base):
            return pl.ds(pl.multiple_of(base + side[0] * HALF + hp * 128, 128), 128)

        head = side[0] * 6 + 2 * hp
        gains = gain_part[:, pl.ds(pl.multiple_of(side[0] * HC + hp * 256, 128), 256)]
        store_pair(
            grads,
            small,
            hp,
            *attention_pair(
                scale,
                head,
                projected[:, lanes(0)],
                projected[:, lanes(HC)],
                projected[:, lanes(2 * HC)],
                attended_grad[:, lanes(0)],
                pair_bias[pl.ds(pl.multiple_of(head * WIN, 8), 2 * WIN), :],
                pens,
                gains,
            ),
        )


def write_coded(value, lines, outs, base):
    high = lines.astype(BF16)
    low = (lines - high.astype(F32)).astype(BF16)
    for i, tail in enumerate((high, low)):
        block = jnp.concatenate([value[i][:, :384].astype(BF16), tail], 1)
        for out in outs:
            out[base + i] = block


def add_coded(keep, recv, outs, source, base):
    value = [keep[source + i].astype(F32) + recv[source + i].astype(F32) for i in range(EXTRA)]
    write_coded(value, value[0][:, 384:] + value[1][:, 384:], outs, base)


def row_of(place):
    y = place["y"]
    return 24 * ((y // 2) * 32 + place["x"] * 8 + place["z"] * 2 + y % 2)


def weight_body(order, x0, x1, p0, p1, m0, m1, a0, a1, s0, s1, *rest):
    outs, (left, grads, total) = rest[:6], rest[6:]
    left[:CELLS, :] = x0[...]
    left[CELLS:, :] = x1[...]
    grads[:CELLS, :] = p0[...]
    grads[CELLS:, :] = p1[...]
    for m in range(4):
        at = slice(m * 384, (m + 1) * 384)
        part = dot(left[:, at], grads[...], TN)
        for j in range(3):
            total[at, j * 512 : j * 512 + HALF] = part[:, j * HALF : (j + 1) * HALF]
    left[:CELLS, :] = m0[...]
    left[CELLS:, :] = m1[...]
    grads[:CELLS, :HALF] = a0[...]
    grads[CELLS:, :HALF] = a1[...]
    for m in range(4):
        at = slice(m * 384, (m + 1) * 384)
        part = dot(left[:, at], grads[:, :HALF], TN)
        for j in range(3):
            total[at, j * 512 + HALF : (j + 1) * 512] = part[:, j * 128 : (j + 1) * 128]
    for j in range(3):
        cols = slice(j * 512, (j + 1) * 512)
        for i in range(4):
            out = outs[2 * j + i // 2]
            for second in range(4):
                for third in range(4):
                    places = (order[4 * j + i], second, third)
                    start = row_of(dict(zip(ORDERS[j], places)))
                    rows = pl.ds(pl.multiple_of(start, 8), 24)
                    out[i % 2 * 16 + second * 4 + third] = total[rows, cols].astype(BF16)
        at = slice(j * 48, (j + 1) * 48)
        value = s0[at, :] + s1[at, :]
        write_coded([value[:24], value[24:]], value[:24, 384:], outs[2 * j : 2 * j + 2], 32)


def halve_body(count, size, order, *refs):
    ins, outs = refs[:6], refs[6:]
    for j in range(3):
        keep, recv = ins[2 * j : 2 * j + 2]
        for i in range(2 * count):
            out = outs[2 * j + i // count]
            for b in range(size):
                at = order[2 * count * j + i] * size + b
                out[i % count * size + b] = (keep[at].astype(F32) + recv[at].astype(F32)).astype(BF16)
        add_coded(keep, recv, outs[2 * j : 2 * j + 2], 2 * count * size, count * size)


def total_body(*refs):
    ins, out = refs[:6], refs[6]
    for j in range(3):
        keep, recv = ins[2 * j : 2 * j + 2]
        out[3 * j] = (keep[0].astype(F32) + recv[0].astype(F32)).astype(BF16)
        add_coded(keep, recv, [out], 1, 3 * j + 1)


def finish_body(core, own, other, qkv, proj, pair, gain, qb, vb, scale):
    which = core[0]
    for side in range(2):
        for j in range(3):
            def block(i):
                return jnp.where(which == side, own[3 * j + i].astype(F32), other[3 * j + i].astype(F32))

            rows = block(0)
            rows = jnp.where(which == 0, rows[:12], rows[12:])
            at = side * HALF + j * 128
            for t in range(3):
                qkv[:, t * HC + at : t * HC + at + 128] = rows[:, t * 128 : (t + 1) * 128]
            proj[:, at : at + 128] = rows[:, HALF:]
            top, bottom = block(1), block(2)
            for g in range(3):
                start = (side * 3 + j) * 144 + g * 48
                pair[start : start + 24, :] = top[:, g * 128 : g * 128 + WIN]
                pair[start + 24 : start + 48, :] = bottom[:, g * 128 : g * 128 + WIN]
            lines = top[:, 384:] + bottom[:, 384:]
            qb[:, at : at + 128] = lines[0:1]
            vb[:, at : at + 128] = lines[1:2]
            scale[side * 3 + j : side * 3 + j + 1, :] = lines[2:3]
            gain[:, side * HC + j * 256 : side * HC + j * 256 + 128] = lines[3:4]
            gain[:, side * HC + j * 256 + 128 : side * HC + j * 256 + 256] = lines[4:5]


def branch_body(side, w, own, theirs, branch, low, grads, rows):
    which = side[0]

    @pl.when(pl.program_id(0) == 0)
    def _():
        for pair in range(3):
            for j in range(3):
                at = j * HC + pair * 128
                cols = slice(pair * HALF + j * 128, pair * HALF + (j + 1) * 128)
                grads[:, pl.ds(pl.multiple_of(at + which * HALF, 128), 128)] = own[:, cols]
                grads[:, pl.ds(pl.multiple_of(at + (1 - which) * HALF, 128), 128)] = theirs[:, cols]

    product = dot(grads[...], w[...], NT)
    for i in range(2):
        rows[i] = product[:, i * 128 : (i + 1) * 128]
    lows = []
    for j in range(12):
        column = jnp.concatenate([rows[i, pl.ds(j, 24, stride=12), :] for i in range(2)], 1)
        branch[j] = column.astype(BF16)
        lows.append(column[24 - SHIFT_H :])
    low[...] = jnp.concatenate(lows, 0).astype(BF16)


def down_body(grid, low, go, stay):
    for j in range(12):
        came = low[...].astype(F32)[j * SHIFT_H : (j + 1) * SHIFT_H]
        column = jnp.concatenate([came, grid[j].astype(F32)[: 24 - SHIFT_H]], 0).astype(BF16)
        if j < SHIFT_W:
            stay[j] = column
        else:
            go[j - SHIFT_W] = column


def permuted(value, axes, target):
    sizes = [lax.axis_size(a) for a in axes]
    pairs = []
    for source in range(int(np.prod(sizes))):
        place = np.unravel_index(source, sizes)
        to = target(*[int(v) for v in place])
        pairs.append((source, int(np.ravel_multi_index(to, sizes))))
    return lax.ppermute(value, axes, pairs)


def lon_step(value, steps):
    return permuted(value, LON, lambda *at: np.unravel_index((np.ravel_multi_index(at, (2, 4, 4)) + steps) % 32, (2, 4, 4)))


def lat_step(value, steps):
    return permuted(value, LAT, lambda *at: np.unravel_index((np.ravel_multi_index(at, (2, 2)) + steps) % 4, (2, 2)))


def both_step(value, steps):
    def target(yh, x, z, yl, c):
        lon = (np.ravel_multi_index((yh, x, z), (2, 4, 4)) + steps) % 32
        lat = (yl * 2 + c + steps) % 4
        return (*np.unravel_index(lon, (2, 4, 4)), lat // 2, lat % 2)

    return permuted(value, LON + LAT, target)


def core_swap(value):
    return permuted(value, ("c",), lambda c: (1 - c,))


def ring_swap(value, axis, step):
    def partner(place, c):
        return place ^ 1 if (step == 0) == (c == 0) else 3 - place

    if axis == "y":
        def target(yh, yl, c):
            to = partner(yh * 2 + yl, c)
            return (to // 2, to % 2, c)
    else:
        def target(place, c):
            return (partner(place, c), c)

    return permuted(value, AXES[axis] + ("c",), target)


def messages(grid):
    return [
        grid[:SHIFT_W],
        grid[SHIFT_W:, :SHIFT_H].reshape(-1, C),
        grid[:SHIFT_W, :SHIFT_H].reshape(-1, C),
    ]


def moved(lon, lat, both):
    return [lon_step(lon, -1), lat_step(lat, -1), both_step(both, -1)]


def shards(
    features,
    upstream,
    region_ids,
    qkv_weight,
    query_bias,
    value_bias,
    logit_scale,
    pair_bias,
    proj_weight,
    norm_gain,
):
    core = lax.axis_index("c")
    place = {"x": lax.axis_index("x"), "z": lax.axis_index("z"), "y": lax.axis_index("yh") * 2 + lax.axis_index("yl")}
    mine = core.astype(jnp.int32).reshape(1)
    theirs = 1 - mine
    scale = jnp.exp(logit_scale)
    bias = jnp.concatenate([query_bias, jnp.zeros_like(query_bias), value_bias]).reshape(1, -1)
    pair_rows = pair_bias.reshape(HEADS * WIN, WIN)
    region_row = region_ids.reshape(WINDOWS, WIN)
    region_col = region_ids.reshape(-1, 1)
    gain = norm_gain.reshape(1, C)

    features = features.transpose(1, 0, 2)
    upstream = upstream.transpose(1, 0, 2)
    came = moved(*messages(features))
    going, came[1] = lax.optimization_barrier((messages(upstream), came[1]))
    came_late = moved(*going)
    x, projected, attended = call(
        forward_body,
        [shape((CELLS, C), BF16), shape((CELLS, 3 * HC), F32), shape((CELLS, HC), BF16)],
        [scale, features, *came, qkv_weight, bias, pair_rows, region_row, region_col],
        scratch=[
            pltpu.VMEM((12, CELLS, 128), F32),
            pltpu.VMEM((CELLS, C), F32),
            pltpu.VMEM((C, 3 * HC), BF16),
            pltpu.SemaphoreType.DMA((9,)),
        ],
        flops=2 * CELLS * C * 3 * HC,
        vmem=24,
        far=(5,),
        name="forward",
    )
    x_other = core_swap(x)
    mixed_low, attended_grad, gain_part, grads_theirs, small_theirs = call(
        backward_body,
        [
            shape((CELLS, C), BF16),
            shape((CELLS, HC), F32),
            shape((1, C), F32),
            shape((CELLS, 3 * HALF), BF16),
            shape((144, 512), F32),
        ],
        [
            theirs,
            scale,
            attended,
            upstream,
            *came_late,
            proj_weight,
            gain,
            projected,
            pair_rows,
            region_row,
            region_col,
        ],
        scalars=2,
        scratch=[pltpu.VMEM((12, CELLS, 128), F32)] + [pltpu.VMEM((CELLS, C), F32)] * 2,
        flops=4 * CELLS * C * HC + 2 * CELLS * WIN * 128 * 18,
        vmem=24,
        name="backward",
    )
    mixed_other = core_swap(mixed_low)
    attended_theirs = lax.dynamic_slice(attended, (0, theirs[0] * HALF), (CELLS, HALF))
    attended_mine = lax.dynamic_slice(attended, (0, mine[0] * HALF), (CELLS, HALF))
    attended_other = core_swap(attended_theirs)

    def attention(side):
        def cols(base):
            return lambda i, side, scale: (0, base + side[0] * 3 + i)

        whole = lambda i, side, scale: (0, 0)
        block = (CELLS, 128)
        return grid_call(
            attention_body,
            (3,),
            [side, scale],
            [
                (projected, block, cols(0)),
                (projected, block, cols(6)),
                (projected, block, cols(12)),
                (attended_grad, block, cols(0)),
                (pair_rows, (2 * WIN, WIN), lambda i, side, scale: (side[0] * 3 + i, 0)),
                (region_row, (WINDOWS, WIN), whole),
                (region_col, (CELLS, 1), whole),
                (gain_part, (1, 256), cols(0)),
            ],
            [
                (shape((CELLS, 3 * HALF), BF16), (CELLS, HALF), lambda i, side, scale: (0, i)),
                (shape((144, 512), F32), (48, 512), lambda i, side, scale: (i, 0)),
            ],
            flops=2 * CELLS * WIN * 128 * 6 * 3,
            name="attention",
        )

    def tables(values, step):
        return jnp.concatenate([jnp.asarray(values)[core, place[names[step]]] for names in ORDERS])

    grads_other = core_swap(grads_theirs)
    small_other = core_swap(small_theirs)
    grads_mine, small_mine = attention(mine)

    parts = call(
        weight_body,
        [shape((32 + EXTRA,) + BLOCK, BF16)] * 6,
        [
            tables(FIRST, 0),
            x,
            x_other,
            grads_mine,
            grads_other,
            mixed_low,
            mixed_other,
            attended_mine,
            attended_other,
            small_mine,
            small_other,
        ],
        scratch=[
            pltpu.VMEM((2 * CELLS, C), BF16),
            pltpu.VMEM((2 * CELLS, 3 * HALF), BF16),
            pltpu.VMEM((C, C), F32),
        ],
        flops=4 * CELLS * C * C,
        vmem=28,
        name="weights",
    )
    side, parts = lax.optimization_barrier((mine, parts))
    whole = lambda i, side: (0, 0)
    branch, low = grid_call(
        branch_body,
        (6,),
        [side],
        [
            (qkv_weight, (256, 3 * HC), lambda i, side: (i, 0)),
            (grads_mine, (CELLS, 3 * HALF), whole),
            (grads_theirs, (CELLS, 3 * HALF), whole),
        ],
        [
            (shape((12, 24, C), BF16), (12, 24, 256), lambda i, side: (0, 0, i)),
            (shape((36, C), BF16), (36, 256), lambda i, side: (0, i)),
        ],
        scratch=[pltpu.VMEM((CELLS, 3 * HC), BF16), pltpu.VMEM((2, CELLS, 128), F32)],
        flops=2 * CELLS * C * 3 * HC,
        name="branch",
    )
    go, stay = call(
        down_body,
        [shape((SHIFT_W, 24, C), BF16)] * 2,
        [branch, lat_step(low, 1)],
        scalars=0,
        name="down",
    )
    back = jnp.concatenate([lon_step(go, 1), stay], 0)
    input_grad = (upstream.astype(F32) + back.astype(F32)).astype(BF16)
    for step in range(6):
        terms = []
        for j, names in enumerate(ORDERS):
            terms += [parts[2 * j], ring_swap(parts[2 * j + 1], names[step // 2], step % 2)]
        if step == 5:
            break
        left = 32 >> step
        if step % 2 == 0:
            body = functools.partial(halve_body, 1, left // 2)
            order = tables(SECOND, step // 2)
        else:
            body = functools.partial(halve_body, 2, left // 4)
            order = tables(FIRST, step // 2 + 1)
        if step == 0:
            order, low = lax.optimization_barrier((order, low))
        if step == 1:
            order, stay = lax.optimization_barrier((order, stay))
        parts = call(body, [shape((left // 2 + EXTRA,) + BLOCK, BF16)] * 6, [order, *terms], name="halve")
    terms, input_grad = lax.optimization_barrier((terms, input_grad))
    (sums,) = call(total_body, [shape((9,) + BLOCK, BF16)], terms, scalars=0, name="total")
    sums_other = core_swap(sums)
    qkv_weight_grad, proj_weight_grad, pair_grad, gain_grad, query_bias_grad, value_bias_grad, scale_grad = call(
        finish_body,
        [
            shape((12, 3 * HC), F32),
            shape((12, HC), F32),
            shape((HEADS * WIN, WIN), F32),
            shape((1, C), F32),
            shape((1, HC), F32),
            shape((1, HC), F32),
            shape((6, 128), F32),
        ],
        [mine, sums, sums_other],
        name="finish",
    )
    pair_grad = pair_grad.reshape(HEADS, WIN, WIN)
    gain_grad = gain_grad.reshape(C)
    query_bias_grad = query_bias_grad.reshape(HC)
    value_bias_grad = value_bias_grad.reshape(HC)
    scale_grad = scale_grad[:, :2].reshape(HEADS)

    return (
        input_grad.transpose(1, 0, 2),
        qkv_weight_grad,
        proj_weight_grad,
        gain_grad,
        query_bias_grad,
        value_bias_grad,
        scale_grad,
        pair_grad,
    )


def solution(mesh):
    fine = Mesh(mesh.devices.reshape(2, 4, 4, 2, 2), ("yh", "x", "z", "yl", "c"))
    every = LON + LAT
    return jax.shard_map(
        shards,
        mesh=fine,
        in_specs=(P(LAT, LON, None), P(LAT, LON, None), P(LAT, LON)) + (P(),) * 7,
        out_specs=(P(LAT, LON, None), P(every, None), P(every, None)) + (P(),) * 5,
        check_vma=False,
    )
```

```python
import functools

import jax
import jax.numpy as jnp
import numpy as np
from jax import lax
from jax.experimental import pallas as pl
from jax.experimental.pallas import tpu as pltpu
from jax.sharding import Mesh
from jax.sharding import PartitionSpec as P

HEADS = 12
HEAD_DIM = 64
WIN_H = 6
WIN_W = 12
SHIFT_H = 3
SHIFT_W = 6
WIN = 72
C = 1536
HC = 768
HALF = 384
CELLS = 288
WINDOWS = 4
COSINE_EPS = 1e-06
NORM_EPS = 1e-05

F32 = jnp.float32
BF16 = jnp.bfloat16
LON = ("yh", "x", "z")
LAT = ("yl", "c")
Y = ("yh", "yl")
ORDERS = (("x", "y", "z"), ("y", "z", "x"), ("z", "x", "y"))
AXES = {"x": ("x",), "y": Y, "z": ("z",)}
KEEP = np.array([[[0, 3], [1, 2], [1, 2], [0, 3]], [[0, 1], [0, 1], [2, 3], [2, 3]]], np.int32)
SEND = np.array([[[1, 2], [0, 3], [0, 3], [1, 2]], [[2, 3], [2, 3], [0, 1], [0, 1]]], np.int32)
FIRST = np.concatenate([KEEP, SEND], -1)
SECOND = np.array([[[0, 1], [0, 1], [1, 0], [1, 0]], [[0, 1], [1, 0], [0, 1], [1, 0]]], np.int32)
BLOCK = (24, 512)
EXTRA = 2
NT = (((1,), (1,)), ((), ()))
TN = (((0,), (0,)), ((), ()))
NN = (((1,), (0,)), ((), ()))
VMEM = pl.BlockSpec(memory_space=pltpu.VMEM)
HBM = pl.BlockSpec(memory_space=pltpu.HBM)
ANY = pl.BlockSpec(memory_space=pl.ANY)
SMEM = pl.BlockSpec(memory_space=pltpu.SMEM)


def dot(left, right, dims=NN):
    return lax.dot_general(left, right, dims, preferred_element_type=F32)


def cost(outs, operands, flops):
    moved = sum(int(np.prod(o.shape)) * o.dtype.itemsize for o in (*outs, *operands))
    return pl.CostEstimate(flops=flops, bytes_accessed=moved, transcendentals=0)


def call(body, outs, operands, scalars=1, scratch=(), flops=0, vmem=50, far=(), near=(), name=None):
    specs = [SMEM] * scalars + [VMEM] * (len(operands) - scalars)
    for i in far:
        specs[i] = HBM
    for i in near:
        specs[i] = ANY
    return pl.pallas_call(
        body,
        out_shape=list(outs),
        in_specs=specs,
        out_specs=[VMEM] * len(outs),
        scratch_shapes=list(scratch),
        compiler_params=pltpu.CompilerParams(vmem_limit_bytes=vmem * 2**20),
        cost_estimate=cost(outs, operands, flops),
        name=name,
    )(*operands)


def grid_call(body, grid, scalars, ins, outs, scratch=(), flops=0, vmem=50, name=None):
    operands = [array for array, _, _ in ins]
    results = [result for result, _, _ in outs]
    spec = pltpu.PrefetchScalarGridSpec(
        num_scalar_prefetch=len(scalars),
        grid=grid,
        in_specs=[pl.BlockSpec(block, at) for _, block, at in ins],
        out_specs=[pl.BlockSpec(block, at) for _, block, at in outs],
        scratch_shapes=list(scratch),
    )
    return pl.pallas_call(
        body,
        grid_spec=spec,
        out_shape=results,
        compiler_params=pltpu.CompilerParams(vmem_limit_bytes=vmem * 2**20),
        cost_estimate=cost(results, operands, flops),
        name=name,
    )(*scalars, *operands)


def shape(dims, dtype):
    return jax.ShapeDtypeStruct(dims, dtype)


def head_sum(value):
    rows = lax.broadcasted_iota(jnp.int32, (128, 128), 0) // HEAD_DIM
    cols = lax.broadcasted_iota(jnp.int32, (128, 128), 1) // HEAD_DIM
    ones = (rows == cols).astype(F32).astype(BF16)
    high = value.astype(BF16)
    low = (value - high.astype(F32)).astype(BF16)
    return dot(high, ones) + dot(low, ones)


def low_half(rows):
    return lax.broadcasted_iota(jnp.int32, (rows, 128), 1) < HEAD_DIM


def stacked(value):
    mask = low_half(WIN)
    return jnp.concatenate([jnp.where(mask, value, 0.0), jnp.where(mask, 0.0, value)], 0).astype(BF16)


def unstacked(value):
    return jnp.where(low_half(WIN), value[:WIN], value[WIN:])


def normalized(rows):
    inv = lax.rsqrt(head_sum(rows * rows) + COSINE_EPS)
    return rows * inv, inv


def penalties(region_row, region_col):
    out = []
    for w in range(WINDOWS):
        same = region_row[w : w + 1, :] == region_col[w * WIN : (w + 1) * WIN, :]
        one = jnp.where(same, 0.0, -100.0).astype(F32)
        out.append(jnp.concatenate([one, one], 0))
    return out


def two_heads(scale_ref, head):
    top = lax.broadcasted_iota(jnp.int32, (2 * WIN, 1), 0) < WIN
    return jnp.where(top, scale_ref[head], scale_ref[head + 1])


def softmax_of(scores):
    exp_scores = [jnp.exp(one) for one in scores]
    sums = [jnp.sum(one, -1, keepdims=True) for one in exp_scores]
    return [one / total for one, total in zip(exp_scores, sums)]


SPANS = [slice(n * WIN, (n + 1) * WIN) for n in range(WINDOWS)]


HALF_ROWS = 12


def f32_rows(ref, start, count):
    return ref[...].astype(F32)[start : start + count]


def window_rows(own, east, west, low, grid, rows):
    for j in range(12):
        i = j % SHIFT_W
        if j < SHIFT_W:
            upper = own[SHIFT_W + i].astype(F32)[SHIFT_H : SHIFT_H + HALF_ROWS]
            lower = [f32_rows(west, i * HALF_ROWS, HALF_ROWS)]
        else:
            upper = f32_rows(east, i * HALF_ROWS, HALF_ROWS)
            lower = [own[i].astype(F32)[SHIFT_H + HALF_ROWS :], f32_rows(low, i * SHIFT_H, SHIFT_H)]
        column = jnp.concatenate([upper] + lower, 0)
        for t in range(12):
            grid[t, j * 24 : (j + 1) * 24, :] = column[:, t * 128 : (t + 1) * 128]
    for r in range(24):
        for t in range(12):
            rows[r * 12 : (r + 1) * 12, t * 128 : (t + 1) * 128] = grid[t, pl.ds(r, 12, stride=24), :]


def to_east_body(own, low, out):
    out[...] = jnp.concatenate(
        [
            piece
            for i in range(SHIFT_W)
            for piece in (
                own[i].astype(F32)[SHIFT_H + HALF_ROWS :],
                f32_rows(low, (SHIFT_W + i) * SHIFT_H, SHIFT_H),
            )
        ],
        0,
    ).astype(BF16)


def forward_body(
    scale, own, east, west, low, w, bias, pair_bias, row, col, x, projected, attended, grid, rows, wide, sems
):
    copies = []
    for g in range(3):
        for j in range(3):
            at = pl.ds(j * HC + g * 256, 256)
            copies.append(pltpu.make_async_copy(w.at[:, at], wide.at[:, at], sems.at[3 * g + j]))
            copies[-1].start()
    window_rows(own, east, west, low, grid, rows)
    x[...] = rows[...].astype(BF16)
    pens = penalties(row[...], col[...])
    for g in range(3):
        for j in range(3):
            lo = j * HC + g * 256
            copies[3 * g + j].wait()
            projected[:, lo : lo + 256] = dot(x[...], wide[:, lo : lo + 256]) + bias[:, lo : lo + 256]
        for half in range(2):
            lo = g * 256 + half * 128
            head = lo // HEAD_DIM
            factor = two_heads(scale, head)
            q = normalized(projected[:, lo : lo + 128])[0]
            k = normalized(projected[:, HC + lo : HC + lo + 128])[0]
            v = projected[:, 2 * HC + lo : 2 * HC + lo + 128]
            pb = pair_bias[head * WIN : (head + 2) * WIN, :]
            cosines = [dot(stacked(q[at]), k[at].astype(BF16), NT) for at in SPANS]
            attention = softmax_of([c * factor + pb + pen for c, pen in zip(cosines, pens)])
            outs = [dot(a.astype(BF16), v[at].astype(BF16)) for a, at in zip(attention, SPANS)]
            attended[:, lo : lo + 128] = jnp.concatenate([unstacked(o) for o in outs], 0).astype(BF16)


def norm_part(attended, rows, pw, gain, mixed_low, attended_grad, gain_part, mixed_all):
    for n in range(6):
        at = slice(n * 256, (n + 1) * 256)
        mixed_all[:, at] = dot(attended[...], pw[at, :], NT)
    total = jnp.zeros((1, C), F32)
    for r in range(6):
        at = slice(r * 48, (r + 1) * 48)
        mixed = mixed_all[at, :]
        center = mixed - jnp.mean(mixed, -1, keepdims=True)
        inv_std = lax.rsqrt(jnp.mean(center * center, -1, keepdims=True) + NORM_EPS)
        normed = center * inv_std
        up = rows[at, :]
        total = total + jnp.sum(up * normed, 0, keepdims=True)
        scaled = up * gain[...]
        grad = inv_std * (
            scaled
            - jnp.mean(scaled, -1, keepdims=True)
            - normed * jnp.mean(scaled * normed, -1, keepdims=True)
        )
        mixed_low[at, :] = grad.astype(BF16)
    gain_part[...] = total
    for n in range(3):
        at = slice(n * 256, (n + 1) * 256)
        attended_grad[:, at] = dot(mixed_low[...], pw[:, at]).astype(BF16).astype(F32)


def attention_pair(scale, head, q, k, v, da, pb, pens, gains):
    factor = two_heads(scale, head)
    q, q_inv = normalized(q)
    k, k_inv = normalized(k)
    qs = [stacked(q[at]) for at in SPANS]
    das = [stacked(da[at]) for at in SPANS]
    kb = [k[at].astype(BF16) for at in SPANS]
    vb = [v[at].astype(BF16) for at in SPANS]
    cosines = [dot(a, b, NT) for a, b in zip(qs, kb)]
    prob_grads = [dot(a, b, NT) for a, b in zip(das, vb)]
    attention = softmax_of([c * factor + pb + pen for c, pen in zip(cosines, pens)])
    v_grad = jnp.concatenate([dot(a.astype(BF16), b, TN) for a, b in zip(attention, das)], 0)
    means = [jnp.sum(a * p, -1, keepdims=True) for a, p in zip(attention, prob_grads)]
    score_grads = [a * (p - m) for a, p, m in zip(attention, prob_grads, means)]
    cosine_grads = [(s * factor).astype(BF16) for s in score_grads]
    gq = jnp.concatenate([unstacked(dot(c, b)) for c, b in zip(cosine_grads, kb)], 0)
    gk = jnp.concatenate([dot(c, b, TN) for c, b in zip(cosine_grads, qs)], 0)
    pair = (score_grads[0] + score_grads[1]) + (score_grads[2] + score_grads[3])
    scaled = sum(s * c for s, c in zip(score_grads, cosines))
    lane = lax.broadcasted_iota(jnp.int32, (1, 128), 1)
    scale_line = jnp.zeros((1, 128), F32)
    for i in range(2):
        one = jnp.sum(jnp.sum(scaled[i * WIN : (i + 1) * WIN], 0, keepdims=True), 1, keepdims=True)
        scale_line = scale_line + jnp.where(lane == i, one * scale[head + i], 0.0)
    q_grad = q_inv * (gq - q * head_sum(q * gq))
    k_grad = k_inv * (gk - k * head_sum(k * gk))
    lines = jnp.concatenate(
        [
            jnp.sum(q_grad, 0, keepdims=True),
            jnp.sum(v_grad, 0, keepdims=True),
            scale_line,
            gains[:, :128],
            gains[:, 128:],
            jnp.zeros((11, 128), F32),
        ],
        0,
    )
    return (q_grad, k_grad, v_grad), pair, lines


def store_pair(grads, small, at, parts, pair, lines):
    for i, part in enumerate(parts):
        grads[:, at * HALF + i * 128 : at * HALF + (i + 1) * 128] = part.astype(BF16)
    rows = slice(at * 48, (at + 1) * 48)
    for g in range(3):
        small[rows, g * 128 : g * 128 + WIN] = pair[g * 48 : (g + 1) * 48]
    small[at * 48 : at * 48 + 16, 384:] = lines


def attention_body(
    side, scale, q_ref, k_ref, v_ref, da_ref, pair_bias, row, col, gain_part, grads, small
):
    pens = penalties(row[...], col[...])
    head = side[0] * 6 + 2 * pl.program_id(0)
    small[...] = jnp.zeros_like(small)
    store_pair(
        grads,
        small,
        0,
        *attention_pair(
            scale, head, q_ref[...], k_ref[...], v_ref[...], da_ref[...], pair_bias[...], pens, gain_part[...]
        ),
    )


def backward_body(
    side,
    scale,
    attended,
    own,
    east,
    west,
    low,
    pw,
    gain,
    projected,
    pair_bias,
    row,
    col,
    mixed_low,
    attended_grad,
    gain_part,
    grads,
    small,
    grid,
    rows,
    mixed_all,
    weight,
    heads,
    sems,
):
    copies = [pltpu.make_async_copy(pw, weight, sems.at[0])]
    for j in range(3):
        at = pl.ds(pl.multiple_of(j * HC + side[0] * HALF, 128), HALF)
        copies.append(pltpu.make_async_copy(projected.at[:, at], heads.at[j], sems.at[1 + j]))
    for copy in copies:
        copy.start()
    window_rows(own, east, west, low, grid, rows)
    copies[0].wait()
    norm_part(attended, rows, weight, gain, mixed_low, attended_grad, gain_part, mixed_all)
    pens = penalties(row[...], col[...])
    small[...] = jnp.zeros_like(small)
    for copy in copies[1:]:
        copy.wait()
    for hp in range(3):
        cols = slice(hp * 128, (hp + 1) * 128)
        head = side[0] * 6 + 2 * hp
        gains = gain_part[:, pl.ds(pl.multiple_of(side[0] * HC + hp * 256, 128), 256)]
        store_pair(
            grads,
            small,
            hp,
            *attention_pair(
                scale,
                head,
                heads[0, :, cols],
                heads[1, :, cols],
                heads[2, :, cols],
                attended_grad[:, pl.ds(pl.multiple_of(side[0] * HALF + hp * 128, 128), 128)],
                pair_bias[pl.ds(pl.multiple_of(head * WIN, 8), 2 * WIN), :],
                pens,
                gains,
            ),
        )


def write_coded(value, lines, outs, base):
    high = lines.astype(BF16)
    low = (lines - high.astype(F32)).astype(BF16)
    for i, tail in enumerate((high, low)):
        block = jnp.concatenate([value[i][:, :384].astype(BF16), tail], 1)
        for out in outs:
            out[base + i] = block


def add_coded(keep, recv, outs, source, base):
    value = [keep[source + i].astype(F32) + recv[source + i].astype(F32) for i in range(EXTRA)]
    write_coded(value, value[0][:, 384:] + value[1][:, 384:], outs, base)


def row_of(place):
    y = place["y"]
    return 24 * ((y // 2) * 32 + place["x"] * 8 + place["z"] * 2 + y % 2)


def weight_body(order, x0, x1, p0, p1, m0, m1, a0, a1, s0, s1, *rest):
    outs, (left, grads, mixed, heads, total, sems) = rest[:6], rest[6:]
    pairs = ((x0, x1, left), (p0, p1, grads), (m0, m1, mixed), (a0, a1, heads))
    copies = []
    for i, (own, other, joined) in enumerate(pairs):
        for k, source in enumerate((own, other)):
            copies.append(
                pltpu.make_async_copy(source, joined.at[k * CELLS : (k + 1) * CELLS], sems.at[2 * i + k])
            )
            copies[-1].start()
    for copy in copies[:4]:
        copy.wait()
    for m in range(4):
        at = slice(m * 384, (m + 1) * 384)
        part = dot(left[:, at], grads[...], TN)
        for j in range(3):
            total[at, j * 512 : j * 512 + HALF] = part[:, j * HALF : (j + 1) * HALF]
    for copy in copies[4:]:
        copy.wait()
    for m in range(4):
        at = slice(m * 384, (m + 1) * 384)
        part = dot(mixed[:, at], heads[...], TN)
        for j in range(3):
            total[at, j * 512 + HALF : (j + 1) * 512] = part[:, j * 128 : (j + 1) * 128]
    for j in range(3):
        cols = slice(j * 512, (j + 1) * 512)
        for i in range(4):
            out = outs[2 * j + i // 2]
            for second in range(4):
                for third in range(4):
                    places = (order[4 * j + i], second, third)
                    start = row_of(dict(zip(ORDERS[j], places)))
                    rows = pl.ds(pl.multiple_of(start, 8), 24)
                    out[i % 2 * 16 + second * 4 + third] = total[rows, cols].astype(BF16)
        at = slice(j * 48, (j + 1) * 48)
        value = s0[at, :] + s1[at, :]
        write_coded([value[:24], value[24:]], value[:24, 384:], outs[2 * j : 2 * j + 2], 32)


def halve_body(count, size, order, *refs):
    ins, outs = refs[:6], refs[6:]
    for j in range(3):
        keep, recv = ins[2 * j : 2 * j + 2]
        for i in range(2 * count):
            out = outs[2 * j + i // count]
            for b in range(size):
                at = order[2 * count * j + i] * size + b
                out[i % count * size + b] = (keep[at].astype(F32) + recv[at].astype(F32)).astype(BF16)
        add_coded(keep, recv, outs[2 * j : 2 * j + 2], 2 * count * size, count * size)


def total_body(*refs):
    ins, out = refs[:6], refs[6]
    for j in range(3):
        keep, recv = ins[2 * j : 2 * j + 2]
        out[3 * j] = (keep[0].astype(F32) + recv[0].astype(F32)).astype(BF16)
        add_coded(keep, recv, [out], 1, 3 * j + 1)


def finish_body(core, own, other, qkv, proj, pair, gain, qb, vb, scale):
    which = core[0]
    for side in range(2):
        for j in range(3):
            def block(i):
                return jnp.where(which == side, own[3 * j + i].astype(F32), other[3 * j + i].astype(F32))

            rows = block(0)
            rows = jnp.where(which == 0, rows[:12], rows[12:])
            at = side * HALF + j * 128
            for t in range(3):
                qkv[:, t * HC + at : t * HC + at + 128] = rows[:, t * 128 : (t + 1) * 128]
            proj[:, at : at + 128] = rows[:, HALF:]
            top, bottom = block(1), block(2)
            for g in range(3):
                start = (side * 3 + j) * 144 + g * 48
                pair[start : start + 24, :] = top[:, g * 128 : g * 128 + WIN]
                pair[start + 24 : start + 48, :] = bottom[:, g * 128 : g * 128 + WIN]
            lines = top[:, 384:] + bottom[:, 384:]
            qb[at : at + 128] = lines[0]
            vb[at : at + 128] = lines[1]
            scale[side * 3 + j : side * 3 + j + 1, :] = lines[2:3]
            gain[side * HC + j * 256 : side * HC + j * 256 + 128] = lines[3]
            gain[side * HC + j * 256 + 128 : side * HC + j * 256 + 256] = lines[4]


def branch_body(side, w, own, theirs, to_east, to_west, stay_low, stay_high, grads, rows):
    which = side[0]

    @pl.when(pl.program_id(0) == 0)
    def _():
        for pair in range(3):
            for j in range(3):
                at = j * HC + pair * 128
                cols = slice(pair * HALF + j * 128, pair * HALF + (j + 1) * 128)
                grads[:, pl.ds(pl.multiple_of(at + which * HALF, 128), 128)] = own[:, cols]
                grads[:, pl.ds(pl.multiple_of(at + (1 - which) * HALF, 128), 128)] = theirs[:, cols]

    product = dot(grads[...], w[...], NT)
    for i in range(2):
        rows[i] = product[:, i * 128 : (i + 1) * 128]
    columns = [
        jnp.concatenate([rows[i, pl.ds(j, 24, stride=12), :] for i in range(2)], 1) for j in range(12)
    ]
    for out, cols, start in (
        (stay_low, columns[:SHIFT_W], 0),
        (to_east, columns[SHIFT_W:], 0),
        (to_west, columns[:SHIFT_W], HALF_ROWS),
        (stay_high, columns[SHIFT_W:], HALF_ROWS),
    ):
        out[...] = jnp.concatenate([one[start : start + HALF_ROWS] for one in cols], 0).astype(BF16)


def last_rows_body(stay_high, from_east, out):
    start = HALF_ROWS - SHIFT_H
    out[...] = jnp.concatenate(
        [
            f32_rows(half, i * HALF_ROWS + start, SHIFT_H)
            for half in (stay_high, from_east)
            for i in range(SHIFT_W)
        ],
        0,
    ).astype(BF16)


def merge_body(upstream, stay_low, stay_high, from_west, from_east, low, out):
    for j in range(12):
        i = j % SHIFT_W
        upper, lower = (from_west, stay_high) if j < SHIFT_W else (stay_low, from_east)
        back = jnp.concatenate(
            [
                f32_rows(low, j * SHIFT_H, SHIFT_H),
                f32_rows(upper, i * HALF_ROWS, HALF_ROWS),
                f32_rows(lower, i * HALF_ROWS, HALF_ROWS - SHIFT_H),
            ],
            0,
        )
        out[j] = (upstream[j].astype(F32) + back).astype(BF16)


def permuted(value, axes, target):
    sizes = [lax.axis_size(a) for a in axes]
    pairs = []
    for source in range(int(np.prod(sizes))):
        place = np.unravel_index(source, sizes)
        to = target(*[int(v) for v in place])
        pairs.append((source, int(np.ravel_multi_index(to, sizes))))
    return lax.ppermute(value, axes, pairs)


def lon_step(value, steps):
    return permuted(value, LON, lambda *at: np.unravel_index((np.ravel_multi_index(at, (2, 4, 4)) + steps) % 32, (2, 4, 4)))


def lat_step(value, steps):
    return permuted(value, LAT, lambda *at: np.unravel_index((np.ravel_multi_index(at, (2, 2)) + steps) % 4, (2, 2)))


def core_swap(value):
    return permuted(value, ("c",), lambda c: (1 - c,))


def ring_swap(value, axis, step):
    def partner(place, c):
        return place ^ 1 if (step == 0) == (c == 0) else 3 - place

    if axis == "y":
        def target(yh, yl, c):
            to = partner(yh * 2 + yl, c)
            return (to // 2, to % 2, c)
    else:
        def target(place, c):
            return (partner(place, c), c)

    return permuted(value, AXES[axis] + ("c",), target)


def first_messages(grid):
    upper = grid[:SHIFT_W, SHIFT_H : SHIFT_H + HALF_ROWS]
    return grid[:, :SHIFT_H].reshape(-1, C), upper.reshape(-1, C)


def halo(grid, low, upper):
    low = lat_step(low, -1)
    east = lon_step(upper, -1)
    (lower,) = call(
        to_east_body, [shape((72, C), BF16)], [grid[SHIFT_W:], low], scalars=0, name="to_east"
    )
    return east, lon_step(lower, 1), low


def shards(
    features,
    upstream,
    region_ids,
    qkv_weight,
    query_bias,
    value_bias,
    logit_scale,
    pair_bias,
    proj_weight,
    norm_gain,
):
    core = lax.axis_index("c")
    place = {"x": lax.axis_index("x"), "z": lax.axis_index("z"), "y": lax.axis_index("yh") * 2 + lax.axis_index("yl")}
    mine = core.astype(jnp.int32).reshape(1)
    theirs = 1 - mine
    scale = jnp.exp(logit_scale)
    bias = jnp.concatenate([query_bias, jnp.zeros_like(query_bias), value_bias]).reshape(1, -1)
    pair_rows = pair_bias.reshape(HEADS * WIN, WIN)
    lower_ids = lon_step(region_ids[HALF_ROWS:], 1)
    region_ids = jnp.concatenate([region_ids[:HALF_ROWS], lower_ids], 0)
    region_row = region_ids.reshape(WINDOWS, WIN)
    region_col = region_ids.reshape(-1, 1)
    gain = norm_gain.reshape(1, C)

    features = features.transpose(1, 0, 2)
    upstream = upstream.transpose(1, 0, 2)
    came = halo(features, *first_messages(features))
    late, low = lax.optimization_barrier((first_messages(upstream), came[2]))
    came = (*came[:2], low)
    came_late = halo(upstream, *late)
    x, projected, attended = call(
        forward_body,
        [shape((CELLS, C), BF16), shape((CELLS, 3 * HC), F32), shape((CELLS, HC), BF16)],
        [scale, features, *came, qkv_weight, bias, pair_rows, region_row, region_col],
        scratch=[
            pltpu.VMEM((12, CELLS, 128), F32),
            pltpu.VMEM((CELLS, C), F32),
            pltpu.VMEM((C, 3 * HC), BF16),
            pltpu.SemaphoreType.DMA((9,)),
        ],
        flops=2 * CELLS * C * 3 * HC,
        far=(5,),
        name="forward",
    )
    x_other = core_swap(x)
    mixed_low, attended_grad, gain_part, grads_theirs, small_theirs = call(
        backward_body,
        [
            shape((CELLS, C), BF16),
            shape((CELLS, HC), F32),
            shape((1, C), F32),
            shape((CELLS, 3 * HALF), BF16),
            shape((144, 512), F32),
        ],
        [
            theirs,
            scale,
            attended,
            upstream,
            *came_late,
            proj_weight,
            gain,
            projected,
            pair_rows,
            region_row,
            region_col,
        ],
        scalars=2,
        scratch=[
            pltpu.VMEM((12, CELLS, 128), F32),
            pltpu.VMEM((CELLS, C), F32),
            pltpu.VMEM((CELLS, C), F32),
            pltpu.VMEM((C, HC), BF16),
            pltpu.VMEM((3, CELLS, HALF), F32),
            pltpu.SemaphoreType.DMA((4,)),
        ],
        far=(7,),
        near=(9,),
        flops=4 * CELLS * C * HC + 2 * CELLS * WIN * 128 * 18,
        name="backward",
    )
    mixed_other = core_swap(mixed_low)
    attended_theirs = lax.dynamic_slice(attended, (0, theirs[0] * HALF), (CELLS, HALF))
    attended_mine = lax.dynamic_slice(attended, (0, mine[0] * HALF), (CELLS, HALF))
    attended_other = core_swap(attended_theirs)

    def attention(side):
        def cols(base):
            return lambda i, side, scale: (0, base + side[0] * 3 + i)

        whole = lambda i, side, scale: (0, 0)
        block = (CELLS, 128)
        return grid_call(
            attention_body,
            (3,),
            [side, scale],
            [
                (projected, block, cols(0)),
                (projected, block, cols(6)),
                (projected, block, cols(12)),
                (attended_grad, block, cols(0)),
                (pair_rows, (2 * WIN, WIN), lambda i, side, scale: (side[0] * 3 + i, 0)),
                (region_row, (WINDOWS, WIN), whole),
                (region_col, (CELLS, 1), whole),
                (gain_part, (1, 256), cols(0)),
            ],
            [
                (shape((CELLS, 3 * HALF), BF16), (CELLS, HALF), lambda i, side, scale: (0, i)),
                (shape((144, 512), F32), (48, 512), lambda i, side, scale: (i, 0)),
            ],
            flops=2 * CELLS * WIN * 128 * 6 * 3,
            name="attention",
        )

    def tables(values, step):
        return jnp.concatenate([jnp.asarray(values)[core, place[names[step]]] for names in ORDERS])

    grads_other = core_swap(grads_theirs)
    small_other = core_swap(small_theirs)
    grads_mine, small_mine = attention(mine)

    parts = call(
        weight_body,
        [shape((32 + EXTRA,) + BLOCK, BF16)] * 6,
        [
            tables(FIRST, 0),
            x,
            x_other,
            grads_mine,
            grads_other,
            mixed_low,
            mixed_other,
            attended_mine,
            attended_other,
            small_mine,
            small_other,
        ],
        scratch=[
            pltpu.VMEM((2 * CELLS, C), BF16),
            pltpu.VMEM((2 * CELLS, 3 * HALF), BF16),
            pltpu.VMEM((2 * CELLS, C), BF16),
            pltpu.VMEM((2 * CELLS, HALF), BF16),
            pltpu.VMEM((C, C), F32),
            pltpu.SemaphoreType.DMA((8,)),
        ],
        near=tuple(range(1, 9)),
        flops=4 * CELLS * C * C,
        name="weights",
    )
    side, parts = lax.optimization_barrier((mine, parts))
    whole = lambda i, side: (0, 0)
    to_east, to_west, stay_low, stay_high = grid_call(
        branch_body,
        (6,),
        [side],
        [
            (qkv_weight, (256, 3 * HC), lambda i, side: (i, 0)),
            (grads_mine, (CELLS, 3 * HALF), whole),
            (grads_theirs, (CELLS, 3 * HALF), whole),
        ],
        [(shape((72, C), BF16), (72, 256), lambda i, side: (0, i))] * 4,
        scratch=[pltpu.VMEM((CELLS, 3 * HC), BF16), pltpu.VMEM((2, CELLS, 128), F32)],
        flops=2 * CELLS * C * 3 * HC,
        name="branch",
    )
    from_west = lon_step(to_east, 1)
    from_east = lon_step(to_west, -1)
    (last,) = call(
        last_rows_body, [shape((36, C), BF16)], [stay_high, from_east], scalars=0, name="last_rows"
    )
    (input_grad,) = call(
        merge_body,
        [shape((12, 24, C), BF16)],
        [upstream, stay_low, stay_high, from_west, from_east, lat_step(last, 1)],
        scalars=0,
        name="merge",
    )
    for step in range(6):
        terms = []
        for j, names in enumerate(ORDERS):
            terms += [parts[2 * j], ring_swap(parts[2 * j + 1], names[step // 2], step % 2)]
        if step == 5:
            break
        left = 32 >> step
        if step % 2 == 0:
            body = functools.partial(halve_body, 1, left // 2)
            order = tables(SECOND, step // 2)
        else:
            body = functools.partial(halve_body, 2, left // 4)
            order = tables(FIRST, step // 2 + 1)
        if step == 0:
            order, stay_low = lax.optimization_barrier((order, stay_low))
        if step == 1:
            order, last = lax.optimization_barrier((order, last))
        parts = call(body, [shape((left // 2 + EXTRA,) + BLOCK, BF16)] * 6, [order, *terms], name="halve")
    terms, input_grad = lax.optimization_barrier((terms, input_grad))
    (sums,) = call(total_body, [shape((9,) + BLOCK, BF16)], terms, scalars=0, name="total")
    sums_other = core_swap(sums)
    qkv_weight_grad, proj_weight_grad, pair_grad, gain_grad, query_bias_grad, value_bias_grad, scale_grad = call(
        finish_body,
        [
            shape((12, 3 * HC), F32),
            shape((12, HC), F32),
            shape((HEADS * WIN, WIN), F32),
            shape((C,), F32),
            shape((HC,), F32),
            shape((HC,), F32),
            shape((6, 128), F32),
        ],
        [mine, sums, sums_other],
        name="finish",
    )
    pair_grad = pair_grad.reshape(HEADS, WIN, WIN)
    scale_grad = scale_grad[:, :2].reshape(HEADS)

    return (
        input_grad.transpose(1, 0, 2),
        qkv_weight_grad,
        proj_weight_grad,
        gain_grad,
        query_bias_grad,
        value_bias_grad,
        scale_grad,
        pair_grad,
    )


def solution(mesh):
    fine = Mesh(mesh.devices.reshape(2, 4, 4, 2, 2), ("yh", "x", "z", "yl", "c"))
    every = LON + LAT
    return jax.shard_map(
        shards,
        mesh=fine,
        in_specs=(P(LAT, LON, None), P(LAT, LON, None), P(LAT, LON)) + (P(),) * 7,
        out_specs=(P(LAT, LON, None), P(every, None), P(every, None)) + (P(),) * 5,
        check_vma=False,
    )
```

```python
import functools

import jax
import jax.numpy as jnp
import numpy as np
from jax import lax
from jax.experimental import pallas as pl
from jax.experimental.pallas import tpu as pltpu
from jax.sharding import Mesh
from jax.sharding import PartitionSpec as P

HEADS = 12
HEAD_DIM = 64
WIN_H = 6
WIN_W = 12
SHIFT_H = 3
SHIFT_W = 6
WIN = 72
C = 1536
HC = 768
HALF = 384
CELLS = 288
WINDOWS = 4
COSINE_EPS = 1e-06
NORM_EPS = 1e-05

F32 = jnp.float32
BF16 = jnp.bfloat16
LON = ("yh", "x", "z")
LAT = ("yl", "c")
Y = ("yh", "yl")
ORDERS = (("x", "y", "z"), ("y", "z", "x"), ("z", "x", "y"))
AXES = {"x": ("x",), "y": Y, "z": ("z",)}
KEEP = np.array([[[0, 3], [1, 2], [1, 2], [0, 3]], [[0, 1], [0, 1], [2, 3], [2, 3]]], np.int32)
SEND = np.array([[[1, 2], [0, 3], [0, 3], [1, 2]], [[2, 3], [2, 3], [0, 1], [0, 1]]], np.int32)
FIRST = np.concatenate([KEEP, SEND], -1)
SECOND = np.array([[[0, 1], [0, 1], [1, 0], [1, 0]], [[0, 1], [1, 0], [0, 1], [1, 0]]], np.int32)
BLOCK = (24, 512)
EXTRA = 2
NT = (((1,), (1,)), ((), ()))
TN = (((0,), (0,)), ((), ()))
NN = (((1,), (0,)), ((), ()))
VMEM = pl.BlockSpec(memory_space=pltpu.VMEM)
HBM = pl.BlockSpec(memory_space=pltpu.HBM)
ANY = pl.BlockSpec(memory_space=pl.ANY)
SMEM = pl.BlockSpec(memory_space=pltpu.SMEM)


def dot(left, right, dims=NN):
    return lax.dot_general(left, right, dims, preferred_element_type=F32)


def cost(outs, operands, flops):
    moved = sum(int(np.prod(o.shape)) * o.dtype.itemsize for o in (*outs, *operands))
    return pl.CostEstimate(flops=flops, bytes_accessed=moved, transcendentals=0)


def call(body, outs, operands, scalars=1, scratch=(), flops=0, vmem=50, far=(), near=(), name=None):
    specs = [SMEM] * scalars + [VMEM] * (len(operands) - scalars)
    for i in far:
        specs[i] = HBM
    for i in near:
        specs[i] = ANY
    return pl.pallas_call(
        body,
        out_shape=list(outs),
        in_specs=specs,
        out_specs=[VMEM] * len(outs),
        scratch_shapes=list(scratch),
        compiler_params=pltpu.CompilerParams(vmem_limit_bytes=vmem * 2**20),
        cost_estimate=cost(outs, operands, flops),
        name=name,
    )(*operands)


def grid_call(body, grid, scalars, ins, outs, scratch=(), flops=0, vmem=50, name=None):
    operands = [array for array, _, _ in ins]
    results = [result for result, _, _ in outs]
    spec = pltpu.PrefetchScalarGridSpec(
        num_scalar_prefetch=len(scalars),
        grid=grid,
        in_specs=[pl.BlockSpec(block, at) for _, block, at in ins],
        out_specs=[pl.BlockSpec(block, at) for _, block, at in outs],
        scratch_shapes=list(scratch),
    )
    return pl.pallas_call(
        body,
        grid_spec=spec,
        out_shape=results,
        compiler_params=pltpu.CompilerParams(vmem_limit_bytes=vmem * 2**20),
        cost_estimate=cost(results, operands, flops),
        name=name,
    )(*scalars, *operands)


def shape(dims, dtype):
    return jax.ShapeDtypeStruct(dims, dtype)


def head_sum(value):
    rows = lax.broadcasted_iota(jnp.int32, (128, 128), 0) // HEAD_DIM
    cols = lax.broadcasted_iota(jnp.int32, (128, 128), 1) // HEAD_DIM
    ones = (rows == cols).astype(F32).astype(BF16)
    high = value.astype(BF16)
    low = (value - high.astype(F32)).astype(BF16)
    return dot(high, ones) + dot(low, ones)


def low_half(rows):
    return lax.broadcasted_iota(jnp.int32, (rows, 128), 1) < HEAD_DIM


def stacked(value):
    mask = low_half(WIN)
    return jnp.concatenate([jnp.where(mask, value, 0.0), jnp.where(mask, 0.0, value)], 0).astype(BF16)


def unstacked(value):
    return jnp.where(low_half(WIN), value[:WIN], value[WIN:])


def normalized(rows):
    inv = lax.rsqrt(head_sum(rows * rows) + COSINE_EPS)
    return rows * inv, inv


def penalties(region_row, region_col):
    out = []
    for w in range(WINDOWS):
        same = region_row[w : w + 1, :] == region_col[w * WIN : (w + 1) * WIN, :]
        one = jnp.where(same, 0.0, -100.0).astype(F32)
        out.append(jnp.concatenate([one, one], 0))
    return out


def two_heads(scale_ref, head):
    top = lax.broadcasted_iota(jnp.int32, (2 * WIN, 1), 0) < WIN
    return jnp.where(top, scale_ref[head], scale_ref[head + 1])


def softmax_of(scores):
    exp_scores = [jnp.exp(one) for one in scores]
    sums = [jnp.sum(one, -1, keepdims=True) for one in exp_scores]
    return [one / total for one, total in zip(exp_scores, sums)]


SPANS = [slice(n * WIN, (n + 1) * WIN) for n in range(WINDOWS)]


HALF_ROWS = 12


def f32_rows(ref, start, count):
    return ref[...].astype(F32)[start : start + count]


def window_rows(own, east, west, low, grid, rows):
    for j in range(12):
        i = j % SHIFT_W
        if j < SHIFT_W:
            upper = own[SHIFT_W + i].astype(F32)[SHIFT_H : SHIFT_H + HALF_ROWS]
            lower = [f32_rows(west, i * HALF_ROWS, HALF_ROWS)]
        else:
            upper = f32_rows(east, i * HALF_ROWS, HALF_ROWS)
            lower = [own[i].astype(F32)[SHIFT_H + HALF_ROWS :], f32_rows(low, i * SHIFT_H, SHIFT_H)]
        column = jnp.concatenate([upper] + lower, 0)
        for t in range(12):
            grid[t, j * 24 : (j + 1) * 24, :] = column[:, t * 128 : (t + 1) * 128]
    for r in range(24):
        for t in range(12):
            rows[r * 12 : (r + 1) * 12, t * 128 : (t + 1) * 128] = grid[t, pl.ds(r, 12, stride=24), :]


def first_body(own, low, upper):
    low[...] = jnp.concatenate([own[j].astype(F32)[:SHIFT_H] for j in range(12)], 0).astype(BF16)
    upper[...] = jnp.concatenate(
        [own[j].astype(F32)[SHIFT_H : SHIFT_H + HALF_ROWS] for j in range(SHIFT_W)], 0
    ).astype(BF16)


def to_east_body(own, low, out):
    out[...] = jnp.concatenate(
        [
            piece
            for i in range(SHIFT_W)
            for piece in (
                own[SHIFT_W + i].astype(F32)[SHIFT_H + HALF_ROWS :],
                f32_rows(low, (SHIFT_W + i) * SHIFT_H, SHIFT_H),
            )
        ],
        0,
    ).astype(BF16)


def forward_body(
    scale, own, east, west, low, w, bias, pair_bias, row, col, x, projected, attended, grid, rows, wide, sems
):
    copies = []
    for g in range(3):
        for j in range(3):
            at = pl.ds(j * HC + g * 256, 256)
            copies.append(pltpu.make_async_copy(w.at[:, at], wide.at[:, at], sems.at[3 * g + j]))
            copies[-1].start()
    window_rows(own, east, west, low, grid, rows)
    x[...] = rows[...].astype(BF16)
    pens = penalties(row[...], col[...])
    for g in range(3):
        for j in range(3):
            lo = j * HC + g * 256
            copies[3 * g + j].wait()
            projected[:, lo : lo + 256] = dot(x[...], wide[:, lo : lo + 256]) + bias[:, lo : lo + 256]
        for half in range(2):
            lo = g * 256 + half * 128
            head = lo // HEAD_DIM
            factor = two_heads(scale, head)
            q = normalized(projected[:, lo : lo + 128])[0]
            k = normalized(projected[:, HC + lo : HC + lo + 128])[0]
            v = projected[:, 2 * HC + lo : 2 * HC + lo + 128]
            pb = pair_bias[head * WIN : (head + 2) * WIN, :]
            cosines = [dot(stacked(q[at]), k[at].astype(BF16), NT) for at in SPANS]
            attention = softmax_of([c * factor + pb + pen for c, pen in zip(cosines, pens)])
            outs = [dot(a.astype(BF16), v[at].astype(BF16)) for a, at in zip(attention, SPANS)]
            attended[:, lo : lo + 128] = jnp.concatenate([unstacked(o) for o in outs], 0).astype(BF16)


def norm_part(attended, rows, pw, gain, mixed_low, attended_grad, gain_part, mixed_all):
    for n in range(6):
        at = slice(n * 256, (n + 1) * 256)
        mixed_all[:, at] = dot(attended[...], pw[at, :], NT)
    total = jnp.zeros((1, C), F32)
    for r in range(6):
        at = slice(r * 48, (r + 1) * 48)
        mixed = mixed_all[at, :]
        center = mixed - jnp.mean(mixed, -1, keepdims=True)
        inv_std = lax.rsqrt(jnp.mean(center * center, -1, keepdims=True) + NORM_EPS)
        normed = center * inv_std
        up = rows[at, :]
        total = total + jnp.sum(up * normed, 0, keepdims=True)
        scaled = up * gain[...]
        grad = inv_std * (
            scaled
            - jnp.mean(scaled, -1, keepdims=True)
            - normed * jnp.mean(scaled * normed, -1, keepdims=True)
        )
        mixed_low[at, :] = grad.astype(BF16)
    gain_part[...] = total
    for n in range(3):
        at = slice(n * 256, (n + 1) * 256)
        attended_grad[:, at] = dot(mixed_low[...], pw[:, at]).astype(BF16).astype(F32)


def attention_pair(scale, head, q, k, v, da, pb, pens, gains):
    factor = two_heads(scale, head)
    q, q_inv = normalized(q)
    k, k_inv = normalized(k)
    qs = [stacked(q[at]) for at in SPANS]
    das = [stacked(da[at]) for at in SPANS]
    kb = [k[at].astype(BF16) for at in SPANS]
    vb = [v[at].astype(BF16) for at in SPANS]
    cosines = [dot(a, b, NT) for a, b in zip(qs, kb)]
    prob_grads = [dot(a, b, NT) for a, b in zip(das, vb)]
    attention = softmax_of([c * factor + pb + pen for c, pen in zip(cosines, pens)])
    v_grad = jnp.concatenate([dot(a.astype(BF16), b, TN) for a, b in zip(attention, das)], 0)
    means = [jnp.sum(a * p, -1, keepdims=True) for a, p in zip(attention, prob_grads)]
    score_grads = [a * (p - m) for a, p, m in zip(attention, prob_grads, means)]
    cosine_grads = [(s * factor).astype(BF16) for s in score_grads]
    gq = jnp.concatenate([unstacked(dot(c, b)) for c, b in zip(cosine_grads, kb)], 0)
    gk = jnp.concatenate([dot(c, b, TN) for c, b in zip(cosine_grads, qs)], 0)
    pair = (score_grads[0] + score_grads[1]) + (score_grads[2] + score_grads[3])
    scaled = sum(s * c for s, c in zip(score_grads, cosines))
    lane = lax.broadcasted_iota(jnp.int32, (1, 128), 1)
    scale_line = jnp.zeros((1, 128), F32)
    for i in range(2):
        one = jnp.sum(jnp.sum(scaled[i * WIN : (i + 1) * WIN], 0, keepdims=True), 1, keepdims=True)
        scale_line = scale_line + jnp.where(lane == head + i, one * scale[head + i], 0.0)
    q_grad = q_inv * (gq - q * head_sum(q * gq))
    k_grad = k_inv * (gk - k * head_sum(k * gk))
    lines = jnp.concatenate(
        [
            jnp.sum(q_grad, 0, keepdims=True),
            jnp.sum(v_grad, 0, keepdims=True),
            scale_line,
            gains[:, :128],
            gains[:, 128:],
            jnp.zeros((11, 128), F32),
        ],
        0,
    )
    return (q_grad, k_grad, v_grad), pair, lines


def store_pair(grads, small, at, parts, pair, lines):
    for i, part in enumerate(parts):
        grads[:, at * HALF + i * 128 : at * HALF + (i + 1) * 128] = part.astype(BF16)
    rows = slice(at * 48, (at + 1) * 48)
    for g in range(3):
        small[rows, g * 128 : g * 128 + WIN] = pair[g * 48 : (g + 1) * 48]
    small[at * 48 : at * 48 + 16, 384:] = lines


def attention_body(
    side, scale, q_ref, k_ref, v_ref, da_ref, pair_bias, row, col, gain_part, grads, small
):
    pens = penalties(row[...], col[...])
    head = side[0] * 6 + 2 * pl.program_id(0)
    small[...] = jnp.zeros_like(small)
    store_pair(
        grads,
        small,
        0,
        *attention_pair(
            scale, head, q_ref[...], k_ref[...], v_ref[...], da_ref[...], pair_bias[...], pens, gain_part[...]
        ),
    )


def backward_body(
    side,
    scale,
    attended,
    own,
    east,
    west,
    low,
    pw,
    gain,
    projected,
    pair_bias,
    row,
    col,
    mixed_low,
    attended_grad,
    gain_part,
    grads,
    small,
    grid,
    rows,
    mixed_all,
    weight,
    heads,
    sems,
):
    copies = [pltpu.make_async_copy(pw, weight, sems.at[0])]
    for j in range(3):
        at = pl.ds(pl.multiple_of(j * HC + side[0] * HALF, 128), HALF)
        copies.append(pltpu.make_async_copy(projected.at[:, at], heads.at[j], sems.at[1 + j]))
    for copy in copies:
        copy.start()
    window_rows(own, east, west, low, grid, rows)
    copies[0].wait()
    norm_part(attended, rows, weight, gain, mixed_low, attended_grad, gain_part, mixed_all)
    pens = penalties(row[...], col[...])
    small[...] = jnp.zeros_like(small)
    for copy in copies[1:]:
        copy.wait()
    for hp in range(3):
        cols = slice(hp * 128, (hp + 1) * 128)
        head = side[0] * 6 + 2 * hp
        gains = gain_part[:, pl.ds(pl.multiple_of(side[0] * HC + hp * 256, 128), 256)]
        store_pair(
            grads,
            small,
            hp,
            *attention_pair(
                scale,
                head,
                heads[0, :, cols],
                heads[1, :, cols],
                heads[2, :, cols],
                attended_grad[:, pl.ds(pl.multiple_of(side[0] * HALF + hp * 128, 128), 128)],
                pair_bias[pl.ds(pl.multiple_of(head * WIN, 8), 2 * WIN), :],
                pens,
                gains,
            ),
        )


def write_coded(value, lines, outs, base):
    high = lines.astype(BF16)
    low = (lines - high.astype(F32)).astype(BF16)
    for i, tail in enumerate((high, low)):
        block = jnp.concatenate([value[i][:, :384].astype(BF16), tail], 1)
        for out in outs:
            out[base + i] = block


def add_coded(keep, recv, outs, source, base):
    value = [keep[source + i].astype(F32) + recv[source + i].astype(F32) for i in range(EXTRA)]
    write_coded(value, value[0][:, 384:] + value[1][:, 384:], outs, base)


def row_of(place):
    y = place["y"]
    return 24 * ((y // 2) * 32 + place["x"] * 8 + place["z"] * 2 + y % 2)


def weight_body(order, x0, x1, p0, p1, m0, m1, a0, a1, s0, s1, *rest):
    outs, (left, grads, mixed, heads, total, sems) = rest[:6], rest[6:]
    pairs = ((x0, x1, left), (p0, p1, grads), (m0, m1, mixed), (a0, a1, heads))
    copies = []
    for i, (own, other, joined) in enumerate(pairs):
        for k, source in enumerate((own, other)):
            copies.append(
                pltpu.make_async_copy(source, joined.at[k * CELLS : (k + 1) * CELLS], sems.at[2 * i + k])
            )
            copies[-1].start()
    for copy in copies[:4]:
        copy.wait()
    for m in range(4):
        at = slice(m * 384, (m + 1) * 384)
        part = dot(left[:, at], grads[...], TN)
        for j in range(3):
            total[at, j * 512 : j * 512 + HALF] = part[:, j * HALF : (j + 1) * HALF]
    for copy in copies[4:]:
        copy.wait()
    for m in range(4):
        at = slice(m * 384, (m + 1) * 384)
        part = dot(mixed[:, at], heads[...], TN)
        for j in range(3):
            total[at, j * 512 + HALF : (j + 1) * 512] = part[:, j * 128 : (j + 1) * 128]
    for j in range(3):
        cols = slice(j * 512, (j + 1) * 512)
        for i in range(4):
            out = outs[2 * j + i // 2]
            for second in range(4):
                for third in range(4):
                    places = (order[4 * j + i], second, third)
                    start = row_of(dict(zip(ORDERS[j], places)))
                    rows = pl.ds(pl.multiple_of(start, 8), 24)
                    out[i % 2 * 16 + second * 4 + third] = total[rows, cols].astype(BF16)
        at = slice(j * 48, (j + 1) * 48)
        value = s0[at, :] + s1[at, :]
        write_coded([value[:24], value[24:]], value[:24, 384:], outs[2 * j : 2 * j + 2], 32)


def halve_body(count, size, order, *refs):
    ins, outs = refs[:6], refs[6:]
    for j in range(3):
        keep, recv = ins[2 * j : 2 * j + 2]
        for i in range(2 * count):
            out = outs[2 * j + i // count]
            for b in range(size):
                at = order[2 * count * j + i] * size + b
                out[i % count * size + b] = (keep[at].astype(F32) + recv[at].astype(F32)).astype(BF16)
        add_coded(keep, recv, outs[2 * j : 2 * j + 2], 2 * count * size, count * size)


def total_body(*refs):
    ins, out = refs[:6], refs[6]
    for j in range(3):
        keep, recv = ins[2 * j : 2 * j + 2]
        out[3 * j] = (keep[0].astype(F32) + recv[0].astype(F32)).astype(BF16)
        add_coded(keep, recv, [out], 1, 3 * j + 1)


def finish_body(core, own, other, qkv, proj, pair, gain, qb, vb, scale):
    which = core[0]
    scales = jnp.zeros((128,), F32)
    for side in range(2):
        for j in range(3):
            def block(i):
                return jnp.where(which == side, own[3 * j + i].astype(F32), other[3 * j + i].astype(F32))

            rows = block(0)
            rows = jnp.where(which == 0, rows[:12], rows[12:])
            at = side * HALF + j * 128
            for t in range(3):
                qkv[:, t * HC + at : t * HC + at + 128] = rows[:, t * 128 : (t + 1) * 128]
            proj[:, at : at + 128] = rows[:, HALF:]
            top, bottom = block(1), block(2)
            for g in range(3):
                start = (side * 3 + j) * 144 + g * 48
                pair[start : start + 24, :] = top[:, g * 128 : g * 128 + WIN]
                pair[start + 24 : start + 48, :] = bottom[:, g * 128 : g * 128 + WIN]
            lines = top[:, 384:] + bottom[:, 384:]
            qb[at : at + 128] = lines[0]
            vb[at : at + 128] = lines[1]
            scales = scales + lines[2]
            gain[side * HC + j * 256 : side * HC + j * 256 + 128] = lines[3]
            gain[side * HC + j * 256 + 128 : side * HC + j * 256 + 256] = lines[4]
    scale[...] = scales[:HEADS]


def branch_body(side, w, own, theirs, to_east, to_west, stay_low, stay_high, grads, rows):
    which = side[0]

    @pl.when(pl.program_id(0) == 0)
    def _():
        for pair in range(3):
            for j in range(3):
                at = j * HC + pair * 128
                cols = slice(pair * HALF + j * 128, pair * HALF + (j + 1) * 128)
                grads[:, pl.ds(pl.multiple_of(at + which * HALF, 128), 128)] = own[:, cols]
                grads[:, pl.ds(pl.multiple_of(at + (1 - which) * HALF, 128), 128)] = theirs[:, cols]

    product = dot(grads[...], w[...], NT)
    for i in range(2):
        rows[i] = product[:, i * 128 : (i + 1) * 128]
    columns = [
        jnp.concatenate([rows[i, pl.ds(j, 24, stride=12), :] for i in range(2)], 1) for j in range(12)
    ]
    for out, cols, start in (
        (stay_low, columns[:SHIFT_W], 0),
        (to_east, columns[SHIFT_W:], 0),
        (to_west, columns[:SHIFT_W], HALF_ROWS),
        (stay_high, columns[SHIFT_W:], HALF_ROWS),
    ):
        out[...] = jnp.concatenate([one[start : start + HALF_ROWS] for one in cols], 0).astype(BF16)


def last_rows_body(stay_high, from_east, out):
    start = HALF_ROWS - SHIFT_H
    out[...] = jnp.concatenate(
        [
            f32_rows(half, i * HALF_ROWS + start, SHIFT_H)
            for half in (stay_high, from_east)
            for i in range(SHIFT_W)
        ],
        0,
    ).astype(BF16)


def merge_body(upstream, stay_low, stay_high, from_west, from_east, low, out):
    for j in range(12):
        i = j % SHIFT_W
        upper, lower = (from_west, stay_high) if j < SHIFT_W else (stay_low, from_east)
        back = jnp.concatenate(
            [
                f32_rows(low, j * SHIFT_H, SHIFT_H),
                f32_rows(upper, i * HALF_ROWS, HALF_ROWS),
                f32_rows(lower, i * HALF_ROWS, HALF_ROWS - SHIFT_H),
            ],
            0,
        )
        out[j] = (upstream[j].astype(F32) + back).astype(BF16)


def permuted(value, axes, target):
    sizes = [lax.axis_size(a) for a in axes]
    pairs = []
    for source in range(int(np.prod(sizes))):
        place = np.unravel_index(source, sizes)
        to = target(*[int(v) for v in place])
        pairs.append((source, int(np.ravel_multi_index(to, sizes))))
    return lax.ppermute(value, axes, pairs)


def lon_step(value, steps):
    return permuted(value, LON, lambda *at: np.unravel_index((np.ravel_multi_index(at, (2, 4, 4)) + steps) % 32, (2, 4, 4)))


def lat_step(value, steps):
    return permuted(value, LAT, lambda *at: np.unravel_index((np.ravel_multi_index(at, (2, 2)) + steps) % 4, (2, 2)))


def core_swap(value):
    return permuted(value, ("c",), lambda c: (1 - c,))


def ring_swap(value, axis, step):
    def partner(place, c):
        return place ^ 1 if (step == 0) == (c == 0) else 3 - place

    if axis == "y":
        def target(yh, yl, c):
            to = partner(yh * 2 + yl, c)
            return (to // 2, to % 2, c)
    else:
        def target(place, c):
            return (partner(place, c), c)

    return permuted(value, AXES[axis] + ("c",), target)


def first_messages(grid):
    return call(
        first_body, [shape((36, C), BF16), shape((72, C), BF16)], [grid], scalars=0, name="first"
    )


def halo(grid):
    low, upper = first_messages(grid)
    low = lat_step(low, -1)
    east = lon_step(upper, -1)
    (lower,) = call(
        to_east_body, [shape((72, C), BF16)], [grid, low], scalars=0, name="to_east"
    )
    return east, low, lower


def shards(
    features,
    upstream,
    region_ids,
    qkv_weight,
    query_bias,
    value_bias,
    logit_scale,
    pair_bias,
    proj_weight,
    norm_gain,
):
    core = lax.axis_index("c")
    place = {"x": lax.axis_index("x"), "z": lax.axis_index("z"), "y": lax.axis_index("yh") * 2 + lax.axis_index("yl")}
    mine = core.astype(jnp.int32).reshape(1)
    theirs = 1 - mine
    scale = jnp.exp(logit_scale)
    bias = jnp.concatenate([query_bias, jnp.zeros_like(query_bias), value_bias]).reshape(1, -1)
    pair_rows = pair_bias.reshape(HEADS * WIN, WIN)
    gain = norm_gain.reshape(1, C)

    features = features.transpose(1, 0, 2)
    upstream = upstream.transpose(1, 0, 2)
    east, low, lower = halo(features)
    late, region_ids, lower = lax.optimization_barrier((upstream, region_ids, lower))
    came = east, lon_step(lower, 1), low
    lower_ids = lon_step(region_ids[HALF_ROWS:], 1)
    region_ids = jnp.concatenate([region_ids[:HALF_ROWS], lower_ids], 0)
    region_row = region_ids.reshape(WINDOWS, WIN)
    region_col = region_ids.reshape(-1, 1)
    east, low, lower = halo(late)
    came_late = east, lon_step(lower, 1), low
    x, projected, attended = call(
        forward_body,
        [shape((CELLS, C), BF16), shape((CELLS, 3 * HC), F32), shape((CELLS, HC), BF16)],
        [scale, features, *came, qkv_weight, bias, pair_rows, region_row, region_col],
        scratch=[
            pltpu.VMEM((12, CELLS, 128), F32),
            pltpu.VMEM((CELLS, C), F32),
            pltpu.VMEM((C, 3 * HC), BF16),
            pltpu.SemaphoreType.DMA((9,)),
        ],
        flops=2 * CELLS * C * 3 * HC,
        far=(5,),
        name="forward",
    )
    x_other = core_swap(x)
    mixed_low, attended_grad, gain_part, grads_theirs, small_theirs = call(
        backward_body,
        [
            shape((CELLS, C), BF16),
            shape((CELLS, HC), F32),
            shape((1, C), F32),
            shape((CELLS, 3 * HALF), BF16),
            shape((144, 512), F32),
        ],
        [
            theirs,
            scale,
            attended,
            upstream,
            *came_late,
            proj_weight,
            gain,
            projected,
            pair_rows,
            region_row,
            region_col,
        ],
        scalars=2,
        scratch=[
            pltpu.VMEM((12, CELLS, 128), F32),
            pltpu.VMEM((CELLS, C), F32),
            pltpu.VMEM((CELLS, C), F32),
            pltpu.VMEM((C, HC), BF16),
            pltpu.VMEM((3, CELLS, HALF), F32),
            pltpu.SemaphoreType.DMA((4,)),
        ],
        far=(7,),
        near=(9,),
        flops=4 * CELLS * C * HC + 2 * CELLS * WIN * 128 * 18,
        name="backward",
    )
    mixed_other = core_swap(mixed_low)
    attended_theirs = lax.dynamic_slice(attended, (0, theirs[0] * HALF), (CELLS, HALF))
    attended_mine = lax.dynamic_slice(attended, (0, mine[0] * HALF), (CELLS, HALF))
    attended_other = core_swap(attended_theirs)

    def attention(side):
        def cols(base):
            return lambda i, side, scale: (0, base + side[0] * 3 + i)

        whole = lambda i, side, scale: (0, 0)
        block = (CELLS, 128)
        return grid_call(
            attention_body,
            (3,),
            [side, scale],
            [
                (projected, block, cols(0)),
                (projected, block, cols(6)),
                (projected, block, cols(12)),
                (attended_grad, block, cols(0)),
                (pair_rows, (2 * WIN, WIN), lambda i, side, scale: (side[0] * 3 + i, 0)),
                (region_row, (WINDOWS, WIN), whole),
                (region_col, (CELLS, 1), whole),
                (gain_part, (1, 256), cols(0)),
            ],
            [
                (shape((CELLS, 3 * HALF), BF16), (CELLS, HALF), lambda i, side, scale: (0, i)),
                (shape((144, 512), F32), (48, 512), lambda i, side, scale: (i, 0)),
            ],
            flops=2 * CELLS * WIN * 128 * 6 * 3,
            name="attention",
        )

    def tables(values, step):
        return jnp.concatenate([jnp.asarray(values)[core, place[names[step]]] for names in ORDERS])

    grads_other = core_swap(grads_theirs)
    small_other = core_swap(small_theirs)
    grads_mine, small_mine = attention(mine)

    parts = call(
        weight_body,
        [shape((32 + EXTRA,) + BLOCK, BF16)] * 6,
        [
            tables(FIRST, 0),
            x,
            x_other,
            grads_mine,
            grads_other,
            mixed_low,
            mixed_other,
            attended_mine,
            attended_other,
            small_mine,
            small_other,
        ],
        scratch=[
            pltpu.VMEM((2 * CELLS, C), BF16),
            pltpu.VMEM((2 * CELLS, 3 * HALF), BF16),
            pltpu.VMEM((2 * CELLS, C), BF16),
            pltpu.VMEM((2 * CELLS, HALF), BF16),
            pltpu.VMEM((C, C), F32),
            pltpu.SemaphoreType.DMA((8,)),
        ],
        near=tuple(range(1, 9)),
        flops=4 * CELLS * C * C,
        name="weights",
    )
    side, parts = lax.optimization_barrier((mine, parts))
    whole = lambda i, side: (0, 0)
    to_east, to_west, stay_low, stay_high = grid_call(
        branch_body,
        (6,),
        [side],
        [
            (qkv_weight, (256, 3 * HC), lambda i, side: (i, 0)),
            (grads_mine, (CELLS, 3 * HALF), whole),
            (grads_theirs, (CELLS, 3 * HALF), whole),
        ],
        [(shape((72, C), BF16), (72, 256), lambda i, side: (0, i))] * 4,
        scratch=[pltpu.VMEM((CELLS, 3 * HC), BF16), pltpu.VMEM((2, CELLS, 128), F32)],
        flops=2 * CELLS * C * 3 * HC,
        name="branch",
    )
    from_west = lon_step(to_east, 1)
    from_east = lon_step(to_west, -1)
    (last,) = call(
        last_rows_body, [shape((36, C), BF16)], [stay_high, from_east], scalars=0, name="last_rows"
    )
    (input_grad,) = call(
        merge_body,
        [shape((12, 24, C), BF16)],
        [upstream, stay_low, stay_high, from_west, from_east, lat_step(last, 1)],
        scalars=0,
        name="merge",
    )
    for step in range(6):
        terms = []
        for j, names in enumerate(ORDERS):
            terms += [parts[2 * j], ring_swap(parts[2 * j + 1], names[step // 2], step % 2)]
        if step == 5:
            break
        left = 32 >> step
        if step % 2 == 0:
            body = functools.partial(halve_body, 1, left // 2)
            order = tables(SECOND, step // 2)
        else:
            body = functools.partial(halve_body, 2, left // 4)
            order = tables(FIRST, step // 2 + 1)
        if step == 0:
            order, stay_low = lax.optimization_barrier((order, stay_low))
        if step == 3:
            order, last = lax.optimization_barrier((order, last))
        parts = call(body, [shape((left // 2 + EXTRA,) + BLOCK, BF16)] * 6, [order, *terms], name="halve")
    terms, input_grad = lax.optimization_barrier((terms, input_grad))
    (sums,) = call(total_body, [shape((9,) + BLOCK, BF16)], terms, scalars=0, name="total")
    sums_other = core_swap(sums)
    qkv_weight_grad, proj_weight_grad, pair_grad, gain_grad, query_bias_grad, value_bias_grad, scale_grad = call(
        finish_body,
        [
            shape((12, 3 * HC), F32),
            shape((12, HC), F32),
            shape((HEADS * WIN, WIN), F32),
            shape((C,), F32),
            shape((HC,), F32),
            shape((HC,), F32),
            shape((HEADS,), F32),
        ],
        [mine, sums, sums_other],
        name="finish",
    )
    pair_grad = pair_grad.reshape(HEADS, WIN, WIN)

    return (
        input_grad.transpose(1, 0, 2),
        qkv_weight_grad,
        proj_weight_grad,
        gain_grad,
        query_bias_grad,
        value_bias_grad,
        scale_grad,
        pair_grad,
    )


def solution(mesh):
    fine = Mesh(mesh.devices.reshape(2, 4, 4, 2, 2), ("yh", "x", "z", "yl", "c"))
    every = LON + LAT
    return jax.shard_map(
        shards,
        mesh=fine,
        in_specs=(P(LAT, LON, None), P(LAT, LON, None), P(LAT, LON)) + (P(),) * 7,
        out_specs=(P(LAT, LON, None), P(every, None), P(every, None)) + (P(),) * 5,
        check_vma=False,
    )
```

```python
import functools

import jax
import jax.numpy as jnp
import numpy as np
from jax import lax
from jax.experimental import pallas as pl
from jax.experimental.pallas import tpu as pltpu
from jax.sharding import Mesh
from jax.sharding import PartitionSpec as P

HEADS = 12
HEAD_DIM = 64
WIN_H = 6
WIN_W = 12
SHIFT_H = 3
SHIFT_W = 6
WIN = 72
C = 1536
HC = 768
HALF = 384
CELLS = 288
WINDOWS = 4
COSINE_EPS = 1e-06
NORM_EPS = 1e-05

F32 = jnp.float32
BF16 = jnp.bfloat16
LON = ("yh", "x", "z")
LAT = ("yl", "c")
Y = ("yh", "yl")
ORDERS = (("x", "y", "z"), ("y", "z", "x"), ("z", "x", "y"))
AXES = {"x": ("x",), "y": Y, "z": ("z",)}
BLOCK = (24, 512)
EXTRA = 2
NT = (((1,), (1,)), ((), ()))
TN = (((0,), (0,)), ((), ()))
NN = (((1,), (0,)), ((), ()))
VMEM = pl.BlockSpec(memory_space=pltpu.VMEM)
HBM = pl.BlockSpec(memory_space=pltpu.HBM)
ANY = pl.BlockSpec(memory_space=pl.ANY)
SMEM = pl.BlockSpec(memory_space=pltpu.SMEM)


def dot(left, right, dims=NN):
    return lax.dot_general(left, right, dims, preferred_element_type=F32)


def cost(outs, operands, flops):
    moved = sum(int(np.prod(o.shape)) * o.dtype.itemsize for o in (*outs, *operands))
    return pl.CostEstimate(flops=flops, bytes_accessed=moved, transcendentals=0)


def call(body, outs, operands, scalars=1, scratch=(), flops=0, vmem=50, far=(), near=(), name=None):
    specs = [SMEM] * scalars + [VMEM] * (len(operands) - scalars)
    for i in far:
        specs[i] = HBM
    for i in near:
        specs[i] = ANY
    return pl.pallas_call(
        body,
        out_shape=list(outs),
        in_specs=specs,
        out_specs=[VMEM] * len(outs),
        scratch_shapes=list(scratch),
        compiler_params=pltpu.CompilerParams(vmem_limit_bytes=vmem * 2**20),
        cost_estimate=cost(outs, operands, flops),
        name=name,
    )(*operands)


def grid_call(body, grid, scalars, ins, outs, scratch=(), flops=0, vmem=50, name=None):
    operands = [array for array, _, _ in ins]
    results = [result for result, _, _ in outs]
    spec = pltpu.PrefetchScalarGridSpec(
        num_scalar_prefetch=len(scalars),
        grid=grid,
        in_specs=[pl.BlockSpec(block, at) for _, block, at in ins],
        out_specs=[pl.BlockSpec(block, at) for _, block, at in outs],
        scratch_shapes=list(scratch),
    )
    return pl.pallas_call(
        body,
        grid_spec=spec,
        out_shape=results,
        compiler_params=pltpu.CompilerParams(vmem_limit_bytes=vmem * 2**20),
        cost_estimate=cost(results, operands, flops),
        name=name,
    )(*scalars, *operands)


def shape(dims, dtype):
    return jax.ShapeDtypeStruct(dims, dtype)


def head_sum(value):
    rows = lax.broadcasted_iota(jnp.int32, (128, 128), 0) // HEAD_DIM
    cols = lax.broadcasted_iota(jnp.int32, (128, 128), 1) // HEAD_DIM
    ones = (rows == cols).astype(F32).astype(BF16)
    high = value.astype(BF16)
    low = (value - high.astype(F32)).astype(BF16)
    return dot(high, ones) + dot(low, ones)


def low_half(rows):
    return lax.broadcasted_iota(jnp.int32, (rows, 128), 1) < HEAD_DIM


def stacked(value):
    mask = low_half(WIN)
    return jnp.concatenate([jnp.where(mask, value, 0.0), jnp.where(mask, 0.0, value)], 0).astype(BF16)


def unstacked(value):
    return jnp.where(low_half(WIN), value[:WIN], value[WIN:])


def normalized(rows):
    inv = lax.rsqrt(head_sum(rows * rows) + COSINE_EPS)
    return rows * inv, inv


def penalties(region_row, region_col):
    out = []
    for w in range(WINDOWS):
        same = region_row[w : w + 1, :] == region_col[w * WIN : (w + 1) * WIN, :]
        one = jnp.where(same, 0.0, -100.0).astype(F32)
        out.append(jnp.concatenate([one, one], 0))
    return out


def two_heads(scale_ref, head):
    top = lax.broadcasted_iota(jnp.int32, (2 * WIN, 1), 0) < WIN
    return jnp.exp(jnp.where(top, scale_ref[head], scale_ref[head + 1]))


def softmax_of(scores):
    exp_scores = [jnp.exp(one) for one in scores]
    sums = [jnp.sum(one, -1, keepdims=True) for one in exp_scores]
    return [one / total for one, total in zip(exp_scores, sums)]


SPANS = [slice(n * WIN, (n + 1) * WIN) for n in range(WINDOWS)]


HALF_ROWS = 12


def f32_rows(ref, start, count):
    return ref[...].astype(F32)[start : start + count]


def window_rows(own, east, west, low, grid, rows):
    for j in range(12):
        i = j % SHIFT_W
        if j < SHIFT_W:
            upper = own[SHIFT_W + i].astype(F32)[SHIFT_H : SHIFT_H + HALF_ROWS]
            lower = [f32_rows(west, i * HALF_ROWS, HALF_ROWS)]
        else:
            upper = f32_rows(east, i * HALF_ROWS, HALF_ROWS)
            lower = [own[i].astype(F32)[SHIFT_H + HALF_ROWS :], f32_rows(low, i * SHIFT_H, SHIFT_H)]
        column = jnp.concatenate([upper] + lower, 0)
        for t in range(12):
            grid[t, j * 24 : (j + 1) * 24, :] = column[:, t * 128 : (t + 1) * 128]
    for r in range(24):
        for t in range(12):
            rows[r * 12 : (r + 1) * 12, t * 128 : (t + 1) * 128] = grid[t, pl.ds(r, 12, stride=24), :]


def first_body(own, low, upper, part, sem):
    copy = pltpu.make_async_copy(own.at[:, :16], part, sem)
    copy.start()
    copy.wait()
    low[...] = jnp.concatenate([part[j].astype(F32)[:SHIFT_H] for j in range(12)], 0).astype(BF16)
    upper[...] = jnp.concatenate(
        [part[j].astype(F32)[SHIFT_H : SHIFT_H + HALF_ROWS] for j in range(SHIFT_W)], 0
    ).astype(BF16)


def to_east_body(own, low, out, part, sem):
    copy = pltpu.make_async_copy(own.at[SHIFT_W:, 8:], part, sem)
    copy.start()
    copy.wait()
    out[...] = jnp.concatenate(
        [
            piece
            for i in range(SHIFT_W)
            for piece in (
                part[i].astype(F32)[SHIFT_H + HALF_ROWS - 8 :],
                f32_rows(low, (SHIFT_W + i) * SHIFT_H, SHIFT_H),
            )
        ],
        0,
    ).astype(BF16)


def forward_body(
    scale, own, east, west, low, w, query_bias, value_bias, pair_bias, row, col, x, projected, attended, grid, rows, wide, sems
):
    copies = []
    for g in range(3):
        for j in range(3):
            at = pl.ds(j * HC + g * 256, 256)
            copies.append(pltpu.make_async_copy(w.at[:, at], wide.at[:, at], sems.at[3 * g + j]))
            copies[-1].start()
    window_rows(own, east, west, low, grid, rows)
    x[...] = rows[...].astype(BF16)
    pens = penalties(row[...], col[...])
    for g in range(3):
        for j in range(3):
            lo = j * HC + g * 256
            copies[3 * g + j].wait()
            product = dot(x[...], wide[:, lo : lo + 256])
            if j != 1:
                product = product + (query_bias, None, value_bias)[j][:, g * 256 : (g + 1) * 256]
            projected[:, lo : lo + 256] = product
        for half in range(2):
            lo = g * 256 + half * 128
            head = lo // HEAD_DIM
            factor = two_heads(scale, head)
            q = normalized(projected[:, lo : lo + 128])[0]
            k = normalized(projected[:, HC + lo : HC + lo + 128])[0]
            v = projected[:, 2 * HC + lo : 2 * HC + lo + 128]
            pb = pair_bias[head * WIN : (head + 2) * WIN, :]
            cosines = [dot(stacked(q[at]), k[at].astype(BF16), NT) for at in SPANS]
            attention = softmax_of([c * factor + pb + pen for c, pen in zip(cosines, pens)])
            outs = [dot(a.astype(BF16), v[at].astype(BF16)) for a, at in zip(attention, SPANS)]
            attended[:, lo : lo + 128] = jnp.concatenate([unstacked(o) for o in outs], 0).astype(BF16)


def norm_part(attended, rows, pw, gain, mixed_low, attended_grad, gain_part, mixed_all):
    for n in range(6):
        at = slice(n * 256, (n + 1) * 256)
        mixed_all[:, at] = dot(attended[...], pw[at, :], NT)
    total = jnp.zeros((1, C), F32)
    for r in range(6):
        at = slice(r * 48, (r + 1) * 48)
        mixed = mixed_all[at, :]
        center = mixed - jnp.mean(mixed, -1, keepdims=True)
        inv_std = lax.rsqrt(jnp.mean(center * center, -1, keepdims=True) + NORM_EPS)
        normed = center * inv_std
        up = rows[at, :]
        total = total + jnp.sum(up * normed, 0, keepdims=True)
        scaled = up * gain[...]
        grad = inv_std * (
            scaled
            - jnp.mean(scaled, -1, keepdims=True)
            - normed * jnp.mean(scaled * normed, -1, keepdims=True)
        )
        mixed_low[at, :] = grad.astype(BF16)
    gain_part[...] = total
    for n in range(3):
        at = slice(n * 256, (n + 1) * 256)
        attended_grad[:, at] = dot(mixed_low[...], pw[:, at]).astype(BF16).astype(F32)


def attention_pair(scale, head, q, k, v, da, pb, pens, gains):
    factor = two_heads(scale, head)
    q, q_inv = normalized(q)
    k, k_inv = normalized(k)
    qs = [stacked(q[at]) for at in SPANS]
    das = [stacked(da[at]) for at in SPANS]
    kb = [k[at].astype(BF16) for at in SPANS]
    vb = [v[at].astype(BF16) for at in SPANS]
    cosines = [dot(a, b, NT) for a, b in zip(qs, kb)]
    prob_grads = [dot(a, b, NT) for a, b in zip(das, vb)]
    attention = softmax_of([c * factor + pb + pen for c, pen in zip(cosines, pens)])
    v_grad = jnp.concatenate([dot(a.astype(BF16), b, TN) for a, b in zip(attention, das)], 0)
    means = [jnp.sum(a * p, -1, keepdims=True) for a, p in zip(attention, prob_grads)]
    score_grads = [a * (p - m) for a, p, m in zip(attention, prob_grads, means)]
    cosine_grads = [(s * factor).astype(BF16) for s in score_grads]
    gq = jnp.concatenate([unstacked(dot(c, b)) for c, b in zip(cosine_grads, kb)], 0)
    gk = jnp.concatenate([dot(c, b, TN) for c, b in zip(cosine_grads, qs)], 0)
    pair = (score_grads[0] + score_grads[1]) + (score_grads[2] + score_grads[3])
    scaled = sum(s * c for s, c in zip(score_grads, cosines))
    lane = lax.broadcasted_iota(jnp.int32, (1, 128), 1)
    scale_line = jnp.zeros((1, 128), F32)
    for i in range(2):
        one = jnp.sum(jnp.sum(scaled[i * WIN : (i + 1) * WIN], 0, keepdims=True), 1, keepdims=True)
        scale_line = scale_line + jnp.where(lane == head + i, one * factor[i * WIN : i * WIN + 1], 0.0)
    q_grad = q_inv * (gq - q * head_sum(q * gq))
    k_grad = k_inv * (gk - k * head_sum(k * gk))
    lines = jnp.concatenate(
        [
            jnp.sum(q_grad, 0, keepdims=True),
            jnp.sum(v_grad, 0, keepdims=True),
            scale_line,
            gains[:, :128],
            gains[:, 128:],
            jnp.zeros((11, 128), F32),
        ],
        0,
    )
    return (q_grad, k_grad, v_grad), pair, lines


def store_pair(grads, small, at, parts, pair, lines):
    for i, part in enumerate(parts):
        grads[:, at * HALF + i * 128 : at * HALF + (i + 1) * 128] = part.astype(BF16)
    rows = slice(at * 48, (at + 1) * 48)
    for g in range(3):
        small[rows, g * 128 : g * 128 + WIN] = pair[g * 48 : (g + 1) * 48]
    small[at * 48 : at * 48 + 16, 384:] = lines


def attention_body(
    side, scale, q_ref, k_ref, v_ref, da_ref, pair_bias, row, col, gain_part, grads, small
):
    pens = penalties(row[...], col[...])
    head = side[0] * 6 + 2 * pl.program_id(0)
    small[...] = jnp.zeros_like(small)
    store_pair(
        grads,
        small,
        0,
        *attention_pair(
            scale, head, q_ref[...], k_ref[...], v_ref[...], da_ref[...], pair_bias[...], pens, gain_part[...]
        ),
    )


def backward_body(
    side,
    scale,
    attended,
    own,
    east,
    west,
    low,
    pw,
    gain,
    projected,
    pair_bias,
    row,
    col,
    mixed_low,
    attended_grad,
    gain_part,
    grads,
    small,
    grid,
    rows,
    mixed_all,
    weight,
    heads,
    sems,
):
    copies = [pltpu.make_async_copy(pw, weight, sems.at[0])]
    for j in range(3):
        at = pl.ds(pl.multiple_of(j * HC + side[0] * HALF, 128), HALF)
        copies.append(pltpu.make_async_copy(projected.at[:, at], heads.at[j], sems.at[1 + j]))
    for copy in copies:
        copy.start()
    window_rows(own, east, west, low, grid, rows)
    copies[0].wait()
    norm_part(attended, rows, weight, gain, mixed_low, attended_grad, gain_part, mixed_all)
    pens = penalties(row[...], col[...])
    small[...] = jnp.zeros_like(small)
    for copy in copies[1:]:
        copy.wait()
    for hp in range(3):
        cols = slice(hp * 128, (hp + 1) * 128)
        head = side[0] * 6 + 2 * hp
        gains = gain_part[:, pl.ds(pl.multiple_of(side[0] * HC + hp * 256, 128), 256)]
        store_pair(
            grads,
            small,
            hp,
            *attention_pair(
                scale,
                head,
                heads[0, :, cols],
                heads[1, :, cols],
                heads[2, :, cols],
                attended_grad[:, pl.ds(pl.multiple_of(side[0] * HALF + hp * 128, 128), 128)],
                pair_bias[pl.ds(pl.multiple_of(head * WIN, 8), 2 * WIN), :],
                pens,
                gains,
            ),
        )


def write_coded(value, lines, outs, base):
    high = lines.astype(BF16)
    low = (lines - high.astype(F32)).astype(BF16)
    for i, tail in enumerate((high, low)):
        block = jnp.concatenate([value[i][:, :384].astype(BF16), tail], 1)
        for out in outs:
            out[base + i] = block


def add_coded(keep, recv, outs, source, base):
    value = [keep[source + i].astype(F32) + recv[source + i].astype(F32) for i in range(EXTRA)]
    write_coded(value, value[0][:, 384:] + value[1][:, 384:], outs, base)


def row_of(place):
    y = place["y"]
    return 24 * ((y // 2) * 32 + place["x"] * 8 + place["z"] * 2 + y % 2)


def first_order(core, at):
    end, left = (at == 0) | (at == 3), at < 2
    zero = [jnp.where(end, a, b) for a, b in ((0, 1), (3, 2), (1, 0), (2, 3))]
    one = [jnp.where(left, a, b) for a, b in ((0, 2), (1, 3), (2, 0), (3, 1))]
    return [jnp.where(core == 0, a, b) for a, b in zip(zero, one)]


def second_order(core, at):
    kept = jnp.where(core == 0, at // 2, at % 2)
    return [kept, 1 - kept]


def order_of(place, j, axis, second):
    at = place[1 + "xyz".index(ORDERS[j][axis])]
    return (second_order if second else first_order)(place[0], at)


def weight_body(place, x0, x1, p0, p1, m0, m1, a0, a1, s0, s1, *rest):
    outs, (left, grads, mixed, heads, total, sems) = rest[:6], rest[6:]
    pairs = ((x0, x1, left), (p0, p1, grads), (m0, m1, mixed), (a0, a1, heads))
    copies = []
    for i, (own, other, joined) in enumerate(pairs):
        for k, source in enumerate((own, other)):
            copies.append(
                pltpu.make_async_copy(source, joined.at[k * CELLS : (k + 1) * CELLS], sems.at[2 * i + k])
            )
            copies[-1].start()
    for copy in copies[:4]:
        copy.wait()
    for m in range(4):
        at = slice(m * 384, (m + 1) * 384)
        part = dot(left[:, at], grads[...], TN)
        for j in range(3):
            total[at, j * 512 : j * 512 + HALF] = part[:, j * HALF : (j + 1) * HALF]
    for copy in copies[4:]:
        copy.wait()
    for m in range(4):
        at = slice(m * 384, (m + 1) * 384)
        part = dot(mixed[:, at], heads[...], TN)
        for j in range(3):
            total[at, j * 512 + HALF : (j + 1) * 512] = part[:, j * 128 : (j + 1) * 128]
    for j in range(3):
        cols = slice(j * 512, (j + 1) * 512)
        order = order_of(place, j, 0, False)
        for i in range(4):
            out = outs[2 * j + i // 2]
            for second in range(4):
                for third in range(4):
                    places = (order[i], second, third)
                    start = row_of(dict(zip(ORDERS[j], places)))
                    rows = pl.ds(pl.multiple_of(start, 8), 24)
                    out[i % 2 * 16 + second * 4 + third] = total[rows, cols].astype(BF16)
        at = slice(j * 48, (j + 1) * 48)
        value = s0[at, :] + s1[at, :]
        write_coded([value[:24], value[24:]], value[:24, 384:], outs[2 * j : 2 * j + 2], 32)


def halve_body(count, size, axis, place, *refs):
    ins, outs = refs[:6], refs[6:]
    for j in range(3):
        keep, recv = ins[2 * j : 2 * j + 2]
        order = order_of(place, j, axis, count == 1)
        for i in range(2 * count):
            out = outs[2 * j + i // count]
            for b in range(size):
                at = order[i] * size + b
                out[i % count * size + b] = (keep[at].astype(F32) + recv[at].astype(F32)).astype(BF16)
        add_coded(keep, recv, outs[2 * j : 2 * j + 2], 2 * count * size, count * size)


def total_body(*refs):
    ins, out = refs[:6], refs[6]
    for j in range(3):
        keep, recv = ins[2 * j : 2 * j + 2]
        out[3 * j] = (keep[0].astype(F32) + recv[0].astype(F32)).astype(BF16)
        add_coded(keep, recv, [out], 1, 3 * j + 1)


def finish_body(core, own, other, qkv, proj, pair, gain, qb, vb, scale):
    which = core[0]
    scales = jnp.zeros((128,), F32)
    for side in range(2):
        for j in range(3):
            def block(i):
                return jnp.where(which == side, own[3 * j + i].astype(F32), other[3 * j + i].astype(F32))

            rows = block(0)
            rows = jnp.where(which == 0, rows[:12], rows[12:])
            at = side * HALF + j * 128
            for t in range(3):
                qkv[:, t * HC + at : t * HC + at + 128] = rows[:, t * 128 : (t + 1) * 128]
            proj[:, at : at + 128] = rows[:, HALF:]
            top, bottom = block(1), block(2)
            for g in range(3):
                start = (side * 3 + j) * 144 + g * 48
                pair[start : start + 24, :] = top[:, g * 128 : g * 128 + WIN]
                pair[start + 24 : start + 48, :] = bottom[:, g * 128 : g * 128 + WIN]
            lines = top[:, 384:] + bottom[:, 384:]
            qb[at : at + 128] = lines[0]
            vb[at : at + 128] = lines[1]
            scales = scales + lines[2]
            gain[side * HC + j * 256 : side * HC + j * 256 + 128] = lines[3]
            gain[side * HC + j * 256 + 128 : side * HC + j * 256 + 256] = lines[4]
    scale[...] = scales[:HEADS]


def branch_body(side, w, own, theirs, to_east, to_west, stay_low, stay_high, grads, rows):
    which = side[0]

    @pl.when(pl.program_id(0) == 0)
    def _():
        for pair in range(3):
            for j in range(3):
                at = j * HC + pair * 128
                cols = slice(pair * HALF + j * 128, pair * HALF + (j + 1) * 128)
                grads[:, pl.ds(pl.multiple_of(at + which * HALF, 128), 128)] = own[:, cols]
                grads[:, pl.ds(pl.multiple_of(at + (1 - which) * HALF, 128), 128)] = theirs[:, cols]

    product = dot(grads[...], w[...], NT)
    for i in range(2):
        rows[i] = product[:, i * 128 : (i + 1) * 128]
    columns = [
        jnp.concatenate([rows[i, pl.ds(j, 24, stride=12), :] for i in range(2)], 1) for j in range(12)
    ]
    for out, cols, start in (
        (stay_low, columns[:SHIFT_W], 0),
        (to_east, columns[SHIFT_W:], 0),
        (to_west, columns[:SHIFT_W], HALF_ROWS),
        (stay_high, columns[SHIFT_W:], HALF_ROWS),
    ):
        out[...] = jnp.concatenate([one[start : start + HALF_ROWS] for one in cols], 0).astype(BF16)


def last_rows_body(stay_high, from_east, out):
    start = HALF_ROWS - SHIFT_H
    out[...] = jnp.concatenate(
        [
            f32_rows(half, i * HALF_ROWS + start, SHIFT_H)
            for half in (stay_high, from_east)
            for i in range(SHIFT_W)
        ],
        0,
    ).astype(BF16)


def merge_body(upstream, stay_low, stay_high, from_west, from_east, low, out):
    for j in range(12):
        i = j % SHIFT_W
        upper, lower = (from_west, stay_high) if j < SHIFT_W else (stay_low, from_east)
        back = jnp.concatenate(
            [
                f32_rows(low, j * SHIFT_H, SHIFT_H),
                f32_rows(upper, i * HALF_ROWS, HALF_ROWS),
                f32_rows(lower, i * HALF_ROWS, HALF_ROWS - SHIFT_H),
            ],
            0,
        )
        out[j] = (upstream[j].astype(F32) + back).astype(BF16)


def permuted(value, axes, target):
    sizes = [lax.axis_size(a) for a in axes]
    pairs = []
    for source in range(int(np.prod(sizes))):
        place = np.unravel_index(source, sizes)
        to = target(*[int(v) for v in place])
        pairs.append((source, int(np.ravel_multi_index(to, sizes))))
    return lax.ppermute(value, axes, pairs)


def lon_step(value, steps):
    return permuted(value, LON, lambda *at: np.unravel_index((np.ravel_multi_index(at, (2, 4, 4)) + steps) % 32, (2, 4, 4)))


def lat_step(value, steps):
    return permuted(value, LAT, lambda *at: np.unravel_index((np.ravel_multi_index(at, (2, 2)) + steps) % 4, (2, 2)))


def core_swap(value):
    return permuted(value, ("c",), lambda c: (1 - c,))


def ring_swap(value, axis, step):
    def partner(place, c):
        return place ^ 1 if (step == 0) == (c == 0) else 3 - place

    if axis == "y":
        def target(yh, yl, c):
            to = partner(yh * 2 + yl, c)
            return (to // 2, to % 2, c)
    else:
        def target(place, c):
            return (partner(place, c), c)

    return permuted(value, AXES[axis] + ("c",), target)


def first_messages(grid):
    return call(
        first_body,
        [shape((36, C), BF16), shape((72, C), BF16)],
        [grid],
        scalars=0,
        scratch=[pltpu.VMEM((12, 16, C), BF16), pltpu.SemaphoreType.DMA],
        vmem=60,
        far=(0,),
        name="first",
    )


def halo(grid):
    low, upper = first_messages(grid)
    low = lat_step(low, -1)
    east = lon_step(upper, -1)
    (lower,) = call(
        to_east_body,
        [shape((72, C), BF16)],
        [grid, low],
        scalars=0,
        scratch=[pltpu.VMEM((SHIFT_W, 16, C), BF16), pltpu.SemaphoreType.DMA],
        vmem=60,
        far=(0,),
        name="to_east",
    )
    return east, low, lower


def shards(
    features,
    upstream,
    region_ids,
    qkv_weight,
    query_bias,
    value_bias,
    logit_scale,
    pair_bias,
    proj_weight,
    norm_gain,
):
    core = lax.axis_index("c")
    place = jnp.stack(
        [core, lax.axis_index("x"), lax.axis_index("yh") * 2 + lax.axis_index("yl"), lax.axis_index("z")]
    ).astype(jnp.int32)
    mine = core.astype(jnp.int32).reshape(1)
    theirs = 1 - mine
    scale = logit_scale
    query_row, value_row = query_bias.reshape(1, HC), value_bias.reshape(1, HC)
    pair_rows = pair_bias.reshape(HEADS * WIN, WIN)
    gain = norm_gain.reshape(1, C)

    features = features.transpose(1, 0, 2)
    upstream = upstream.transpose(1, 0, 2)
    east, low, lower = halo(features)
    late, region_ids, lower = lax.optimization_barrier((upstream, region_ids, lower))
    came = east, lon_step(lower, 1), low
    lower_ids = lon_step(region_ids[HALF_ROWS:], 1)
    region_ids = jnp.concatenate([region_ids[:HALF_ROWS], lower_ids], 0)
    region_row = region_ids.reshape(WINDOWS, WIN)
    region_col = region_ids.reshape(-1, 1)
    east, low, lower = halo(late)
    came_late = east, lon_step(lower, 1), low
    x, projected, attended = call(
        forward_body,
        [shape((CELLS, C), BF16), shape((CELLS, 3 * HC), F32), shape((CELLS, HC), BF16)],
        [scale, features, *came, qkv_weight, query_row, value_row, pair_rows, region_row, region_col],
        scratch=[
            pltpu.VMEM((12, CELLS, 128), F32),
            pltpu.VMEM((CELLS, C), F32),
            pltpu.VMEM((C, 3 * HC), BF16),
            pltpu.SemaphoreType.DMA((9,)),
        ],
        flops=2 * CELLS * C * 3 * HC,
        far=(5,),
        name="forward",
    )
    x_other = core_swap(x)
    mixed_low, attended_grad, gain_part, grads_theirs, small_theirs = call(
        backward_body,
        [
            shape((CELLS, C), BF16),
            shape((CELLS, HC), F32),
            shape((1, C), F32),
            shape((CELLS, 3 * HALF), BF16),
            shape((144, 512), F32),
        ],
        [
            theirs,
            scale,
            attended,
            upstream,
            *came_late,
            proj_weight,
            gain,
            projected,
            pair_rows,
            region_row,
            region_col,
        ],
        scalars=2,
        scratch=[
            pltpu.VMEM((12, CELLS, 128), F32),
            pltpu.VMEM((CELLS, C), F32),
            pltpu.VMEM((CELLS, C), F32),
            pltpu.VMEM((C, HC), BF16),
            pltpu.VMEM((3, CELLS, HALF), F32),
            pltpu.SemaphoreType.DMA((4,)),
        ],
        far=(7,),
        near=(9,),
        flops=4 * CELLS * C * HC + 2 * CELLS * WIN * 128 * 18,
        name="backward",
    )
    mixed_other = core_swap(mixed_low)
    attended_theirs = lax.dynamic_slice(attended, (0, theirs[0] * HALF), (CELLS, HALF))
    attended_mine = lax.dynamic_slice(attended, (0, mine[0] * HALF), (CELLS, HALF))
    attended_other = core_swap(attended_theirs)

    def attention(side):
        def cols(base):
            return lambda i, side, scale: (0, base + side[0] * 3 + i)

        whole = lambda i, side, scale: (0, 0)
        block = (CELLS, 128)
        return grid_call(
            attention_body,
            (3,),
            [side, scale],
            [
                (projected, block, cols(0)),
                (projected, block, cols(6)),
                (projected, block, cols(12)),
                (attended_grad, block, cols(0)),
                (pair_rows, (2 * WIN, WIN), lambda i, side, scale: (side[0] * 3 + i, 0)),
                (region_row, (WINDOWS, WIN), whole),
                (region_col, (CELLS, 1), whole),
                (gain_part, (1, 256), cols(0)),
            ],
            [
                (shape((CELLS, 3 * HALF), BF16), (CELLS, HALF), lambda i, side, scale: (0, i)),
                (shape((144, 512), F32), (48, 512), lambda i, side, scale: (i, 0)),
            ],
            flops=2 * CELLS * WIN * 128 * 6 * 3,
            vmem=16,
            name="attention",
        )

    grads_other = core_swap(grads_theirs)
    small_other = core_swap(small_theirs)
    grads_mine, small_mine = attention(mine)

    parts = call(
        weight_body,
        [shape((32 + EXTRA,) + BLOCK, BF16)] * 6,
        [
            place,
            x,
            x_other,
            grads_mine,
            grads_other,
            mixed_low,
            mixed_other,
            attended_mine,
            attended_other,
            small_mine,
            small_other,
        ],
        scratch=[
            pltpu.VMEM((2 * CELLS, C), BF16),
            pltpu.VMEM((2 * CELLS, 3 * HALF), BF16),
            pltpu.VMEM((2 * CELLS, C), BF16),
            pltpu.VMEM((2 * CELLS, HALF), BF16),
            pltpu.VMEM((C, C), F32),
            pltpu.SemaphoreType.DMA((8,)),
        ],
        near=tuple(range(1, 9)),
        flops=4 * CELLS * C * C,
        vmem=26,
        name="weights",
    )
    side, parts = lax.optimization_barrier((mine, parts))
    order = place
    whole = lambda i, side: (0, 0)
    to_east, to_west, stay_low, stay_high = grid_call(
        branch_body,
        (6,),
        [side],
        [
            (qkv_weight, (256, 3 * HC), lambda i, side: (i, 0)),
            (grads_mine, (CELLS, 3 * HALF), whole),
            (grads_theirs, (CELLS, 3 * HALF), whole),
        ],
        [(shape((72, C), BF16), (72, 256), lambda i, side: (0, i))] * 4,
        scratch=[pltpu.VMEM((CELLS, 3 * HC), BF16), pltpu.VMEM((2, CELLS, 128), F32)],
        flops=2 * CELLS * C * 3 * HC,
        vmem=16,
        name="branch",
    )
    from_west = lon_step(to_east, 1)
    from_east = lon_step(to_west, -1)
    (last,) = call(
        last_rows_body, [shape((36, C), BF16)], [stay_high, from_east], scalars=0, vmem=6, name="last_rows"
    )
    (input_grad,) = call(
        merge_body,
        [shape((12, 24, C), BF16)],
        [upstream, stay_low, stay_high, from_west, from_east, lat_step(last, 1)],
        scalars=0,
        vmem=10,
        name="merge",
    )
    for step in range(6):
        terms = []
        for j, names in enumerate(ORDERS):
            terms += [parts[2 * j], ring_swap(parts[2 * j + 1], names[step // 2], step % 2)]
        if step == 5:
            break
        left = 32 >> step
        if step % 2 == 0:
            body = functools.partial(halve_body, 1, left // 2, step // 2)
        else:
            body = functools.partial(halve_body, 2, left // 4, step // 2 + 1)
        if step == 0:
            order, stay_low = lax.optimization_barrier((order, stay_low))
        if step == 3:
            order, last = lax.optimization_barrier((order, last))
        parts = call(body, [shape((left // 2 + EXTRA,) + BLOCK, BF16)] * 6, [order, *terms], vmem=10, name="halve")
    terms, input_grad = lax.optimization_barrier((terms, input_grad))
    (sums,) = call(total_body, [shape((9,) + BLOCK, BF16)], terms, scalars=0, vmem=6, name="total")
    sums_other = core_swap(sums)
    qkv_weight_grad, proj_weight_grad, pair_grad, gain_grad, query_bias_grad, value_bias_grad, scale_grad = call(
        finish_body,
        [
            shape((12, 3 * HC), F32),
            shape((12, HC), F32),
            shape((HEADS * WIN, WIN), F32),
            shape((C,), F32),
            shape((HC,), F32),
            shape((HC,), F32),
            shape((HEADS,), F32),
        ],
        [mine, sums, sums_other],
        vmem=8,
        name="finish",
    )
    pair_grad = pair_grad.reshape(HEADS, WIN, WIN)

    return (
        input_grad.transpose(1, 0, 2),
        qkv_weight_grad,
        proj_weight_grad,
        gain_grad,
        query_bias_grad,
        value_bias_grad,
        scale_grad,
        pair_grad,
    )


def solution(mesh):
    fine = Mesh(mesh.devices.reshape(2, 4, 4, 2, 2), ("yh", "x", "z", "yl", "c"))
    every = LON + LAT
    return jax.shard_map(
        shards,
        mesh=fine,
        in_specs=(P(LAT, LON, None), P(LAT, LON, None), P(LAT, LON)) + (P(),) * 7,
        out_specs=(P(LAT, LON, None), P(every, None), P(every, None)) + (P(),) * 5,
        check_vma=False,
    )
```

```python
import functools

import jax
import jax.numpy as jnp
import numpy as np
from jax import lax
from jax.experimental import pallas as pl
from jax.experimental.pallas import tpu as pltpu
from jax.sharding import Mesh
from jax.sharding import PartitionSpec as P

HEADS = 12
HEAD_DIM = 64
WIN_H = 6
WIN_W = 12
SHIFT_H = 3
SHIFT_W = 6
WIN = 72
C = 1536
HC = 768
HALF = 384
CELLS = 288
WINDOWS = 4
COSINE_EPS = 1e-06
NORM_EPS = 1e-05

F32 = jnp.float32
BF16 = jnp.bfloat16
LON = ("yh", "x", "z")
LAT = ("yl", "c")
Y = ("yh", "yl")
ORDERS = (("x", "y", "z"), ("y", "z", "x"), ("z", "x", "y"))
AXES = {"x": ("x",), "y": Y, "z": ("z",)}
BLOCK = (24, 512)
EXTRA = 2
NT = (((1,), (1,)), ((), ()))
TN = (((0,), (0,)), ((), ()))
NN = (((1,), (0,)), ((), ()))
VMEM = pl.BlockSpec(memory_space=pltpu.VMEM)
HBM = pl.BlockSpec(memory_space=pltpu.HBM)
ANY = pl.BlockSpec(memory_space=pl.ANY)
SMEM = pl.BlockSpec(memory_space=pltpu.SMEM)


def dot(left, right, dims=NN):
    return lax.dot_general(left, right, dims, preferred_element_type=F32)


def cost(outs, operands, flops):
    moved = sum(int(np.prod(o.shape)) * o.dtype.itemsize for o in (*outs, *operands))
    return pl.CostEstimate(flops=flops, bytes_accessed=moved, transcendentals=0)


def call(body, outs, operands, scalars=1, scratch=(), flops=0, vmem=50, far=(), near=(), name=None):
    specs = [SMEM] * scalars + [VMEM] * (len(operands) - scalars)
    for i in far:
        specs[i] = HBM
    for i in near:
        specs[i] = ANY
    return pl.pallas_call(
        body,
        out_shape=list(outs),
        in_specs=specs,
        out_specs=[VMEM] * len(outs),
        scratch_shapes=list(scratch),
        compiler_params=pltpu.CompilerParams(vmem_limit_bytes=vmem * 2**20),
        cost_estimate=cost(outs, operands, flops),
        name=name,
    )(*operands)


def grid_call(body, grid, scalars, ins, outs, scratch=(), flops=0, vmem=50, name=None):
    operands = [array for array, _, _ in ins]
    results = [result for result, _, _ in outs]
    spec = pltpu.PrefetchScalarGridSpec(
        num_scalar_prefetch=len(scalars),
        grid=grid,
        in_specs=[pl.BlockSpec(block, at) for _, block, at in ins],
        out_specs=[pl.BlockSpec(block, at) for _, block, at in outs],
        scratch_shapes=list(scratch),
    )
    return pl.pallas_call(
        body,
        grid_spec=spec,
        out_shape=results,
        compiler_params=pltpu.CompilerParams(vmem_limit_bytes=vmem * 2**20),
        cost_estimate=cost(results, operands, flops),
        name=name,
    )(*scalars, *operands)


def shape(dims, dtype):
    return jax.ShapeDtypeStruct(dims, dtype)


def head_sum(value):
    rows = lax.broadcasted_iota(jnp.int32, (128, 128), 0) // HEAD_DIM
    cols = lax.broadcasted_iota(jnp.int32, (128, 128), 1) // HEAD_DIM
    ones = (rows == cols).astype(F32).astype(BF16)
    high = value.astype(BF16)
    low = (value - high.astype(F32)).astype(BF16)
    return dot(high, ones) + dot(low, ones)


def low_half(rows):
    return lax.broadcasted_iota(jnp.int32, (rows, 128), 1) < HEAD_DIM


def stacked(value):
    mask = low_half(WIN)
    return jnp.concatenate([jnp.where(mask, value, 0.0), jnp.where(mask, 0.0, value)], 0).astype(BF16)


def unstacked(value):
    return jnp.where(low_half(WIN), value[:WIN], value[WIN:])


def normalized(rows):
    inv = lax.rsqrt(head_sum(rows * rows) + COSINE_EPS)
    return rows * inv, inv


def penalties(region_row, region_col):
    out = []
    for w in range(WINDOWS):
        same = region_row[w : w + 1, :] == region_col[w * WIN : (w + 1) * WIN, :]
        one = jnp.where(same, 0.0, -100.0).astype(F32)
        out.append(jnp.concatenate([one, one], 0))
    return out


def two_heads(scale_ref, head):
    top = lax.broadcasted_iota(jnp.int32, (2 * WIN, 1), 0) < WIN
    return jnp.exp(jnp.where(top, scale_ref[head], scale_ref[head + 1]))


def softmax_of(scores):
    exp_scores = [jnp.exp(one) for one in scores]
    sums = [jnp.sum(one, -1, keepdims=True) for one in exp_scores]
    return [one / total for one, total in zip(exp_scores, sums)]


SPANS = [slice(n * WIN, (n + 1) * WIN) for n in range(WINDOWS)]


HALF_ROWS = 12


def f32_rows(ref, start, count):
    return ref[...].astype(F32)[start : start + count]


def window_rows(own, east, west, low, grid, rows):
    for j in range(12):
        i = j % SHIFT_W
        if j < SHIFT_W:
            upper = own[SHIFT_W + i].astype(F32)[SHIFT_H : SHIFT_H + HALF_ROWS]
            lower = [f32_rows(west, i * HALF_ROWS, HALF_ROWS)]
        else:
            upper = f32_rows(east, i * HALF_ROWS, HALF_ROWS)
            lower = [own[i].astype(F32)[SHIFT_H + HALF_ROWS :], f32_rows(low, i * SHIFT_H, SHIFT_H)]
        column = jnp.concatenate([upper] + lower, 0)
        for t in range(12):
            grid[t, j * 24 : (j + 1) * 24, :] = column[:, t * 128 : (t + 1) * 128]
    for r in range(24):
        for t in range(12):
            rows[r * 12 : (r + 1) * 12, t * 128 : (t + 1) * 128] = grid[t, pl.ds(r, 12, stride=24), :]


def first_body(own, low, upper):
    low[...] = jnp.concatenate([own[j].astype(F32)[:SHIFT_H] for j in range(12)], 0).astype(BF16)
    upper[...] = jnp.concatenate(
        [own[j].astype(F32)[SHIFT_H : SHIFT_H + HALF_ROWS] for j in range(SHIFT_W)], 0
    ).astype(BF16)


def to_east_body(own, low, out):
    out[...] = jnp.concatenate(
        [
            piece
            for i in range(SHIFT_W)
            for piece in (
                own[SHIFT_W + i].astype(F32)[SHIFT_H + HALF_ROWS :],
                f32_rows(low, (SHIFT_W + i) * SHIFT_H, SHIFT_H),
            )
        ],
        0,
    ).astype(BF16)


def forward_body(
    scale, own, east, west, low, w, query_bias, value_bias, pair_bias, row, col, x, projected, attended, grid, rows, wide, sems
):
    copies = []
    for g in range(3):
        for j in range(3):
            at = pl.ds(j * HC + g * 256, 256)
            copies.append(pltpu.make_async_copy(w.at[:, at], wide.at[:, at], sems.at[3 * g + j]))
            copies[-1].start()
    window_rows(own, east, west, low, grid, rows)
    x[...] = rows[...].astype(BF16)
    pens = penalties(row[...], col[...])
    for g in range(3):
        for j in range(3):
            lo = j * HC + g * 256
            copies[3 * g + j].wait()
            product = dot(x[...], wide[:, lo : lo + 256])
            if j != 1:
                product = product + (query_bias, None, value_bias)[j][:, g * 256 : (g + 1) * 256]
            projected[:, lo : lo + 256] = product
        for half in range(2):
            lo = g * 256 + half * 128
            head = lo // HEAD_DIM
            factor = two_heads(scale, head)
            q = normalized(projected[:, lo : lo + 128])[0]
            k = normalized(projected[:, HC + lo : HC + lo + 128])[0]
            v = projected[:, 2 * HC + lo : 2 * HC + lo + 128]
            pb = pair_bias[head * WIN : (head + 2) * WIN, :]
            cosines = [dot(stacked(q[at]), k[at].astype(BF16), NT) for at in SPANS]
            attention = softmax_of([c * factor + pb + pen for c, pen in zip(cosines, pens)])
            outs = [dot(a.astype(BF16), v[at].astype(BF16)) for a, at in zip(attention, SPANS)]
            attended[:, lo : lo + 128] = jnp.concatenate([unstacked(o) for o in outs], 0).astype(BF16)


def norm_part(attended, rows, pw, gain, mixed_low, attended_grad, gain_part, mixed_all):
    for n in range(6):
        at = slice(n * 256, (n + 1) * 256)
        mixed_all[:, at] = dot(attended[...], pw[at, :], NT)
    total = jnp.zeros((1, C), F32)
    for r in range(6):
        at = slice(r * 48, (r + 1) * 48)
        mixed = mixed_all[at, :]
        center = mixed - jnp.mean(mixed, -1, keepdims=True)
        inv_std = lax.rsqrt(jnp.mean(center * center, -1, keepdims=True) + NORM_EPS)
        normed = center * inv_std
        up = rows[at, :]
        total = total + jnp.sum(up * normed, 0, keepdims=True)
        scaled = up * gain[...]
        grad = inv_std * (
            scaled
            - jnp.mean(scaled, -1, keepdims=True)
            - normed * jnp.mean(scaled * normed, -1, keepdims=True)
        )
        mixed_low[at, :] = grad.astype(BF16)
    gain_part[...] = total
    for n in range(3):
        at = slice(n * 256, (n + 1) * 256)
        attended_grad[:, at] = dot(mixed_low[...], pw[:, at]).astype(BF16).astype(F32)


def attention_pair(scale, head, q, k, v, da, pb, pens, gains):
    factor = two_heads(scale, head)
    q, q_inv = normalized(q)
    k, k_inv = normalized(k)
    qs = [stacked(q[at]) for at in SPANS]
    das = [stacked(da[at]) for at in SPANS]
    kb = [k[at].astype(BF16) for at in SPANS]
    vb = [v[at].astype(BF16) for at in SPANS]
    cosines = [dot(a, b, NT) for a, b in zip(qs, kb)]
    prob_grads = [dot(a, b, NT) for a, b in zip(das, vb)]
    attention = softmax_of([c * factor + pb + pen for c, pen in zip(cosines, pens)])
    v_grad = jnp.concatenate([dot(a.astype(BF16), b, TN) for a, b in zip(attention, das)], 0)
    means = [jnp.sum(a * p, -1, keepdims=True) for a, p in zip(attention, prob_grads)]
    score_grads = [a * (p - m) for a, p, m in zip(attention, prob_grads, means)]
    cosine_grads = [(s * factor).astype(BF16) for s in score_grads]
    gq = jnp.concatenate([unstacked(dot(c, b)) for c, b in zip(cosine_grads, kb)], 0)
    gk = jnp.concatenate([dot(c, b, TN) for c, b in zip(cosine_grads, qs)], 0)
    pair = (score_grads[0] + score_grads[1]) + (score_grads[2] + score_grads[3])
    scaled = sum(s * c for s, c in zip(score_grads, cosines))
    lane = lax.broadcasted_iota(jnp.int32, (1, 128), 1)
    scale_line = jnp.zeros((1, 128), F32)
    for i in range(2):
        one = jnp.sum(jnp.sum(scaled[i * WIN : (i + 1) * WIN], 0, keepdims=True), 1, keepdims=True)
        scale_line = scale_line + jnp.where(lane == head + i, one * factor[i * WIN : i * WIN + 1], 0.0)
    q_grad = q_inv * (gq - q * head_sum(q * gq))
    k_grad = k_inv * (gk - k * head_sum(k * gk))
    lines = jnp.concatenate(
        [
            jnp.sum(q_grad, 0, keepdims=True),
            jnp.sum(v_grad, 0, keepdims=True),
            scale_line,
            gains[:, :128],
            gains[:, 128:],
            jnp.zeros((11, 128), F32),
        ],
        0,
    )
    return (q_grad, k_grad, v_grad), pair, lines


def store_pair(grads, small, at, parts, pair, lines):
    for i, part in enumerate(parts):
        grads[:, at * HALF + i * 128 : at * HALF + (i + 1) * 128] = part.astype(BF16)
    rows = slice(at * 48, (at + 1) * 48)
    for g in range(3):
        small[rows, g * 128 : g * 128 + WIN] = pair[g * 48 : (g + 1) * 48]
    small[at * 48 : at * 48 + 16, 384:] = lines


def attention_body(
    side, scale, q_ref, k_ref, v_ref, da_ref, pair_bias, row, col, gain_part, grads, small
):
    pens = penalties(row[...], col[...])
    head = side[0] * 6 + 2 * pl.program_id(0)
    small[...] = jnp.zeros_like(small)
    store_pair(
        grads,
        small,
        0,
        *attention_pair(
            scale, head, q_ref[...], k_ref[...], v_ref[...], da_ref[...], pair_bias[...], pens, gain_part[...]
        ),
    )


def backward_body(
    side,
    scale,
    attended,
    own,
    east,
    west,
    low,
    pw,
    gain,
    projected,
    pair_bias,
    row,
    col,
    mixed_low,
    grad_other,
    gain_part,
    grads,
    small,
    attended_near,
    attended_far,
    grid,
    rows,
    mixed_all,
    weight,
    heads,
    attended_grad,
    sems,
):
    copies = [pltpu.make_async_copy(pw, weight, sems.at[0])]
    for j in range(3):
        at = pl.ds(pl.multiple_of(j * HC + side[0] * HALF, 128), HALF)
        copies.append(pltpu.make_async_copy(projected.at[:, at], heads.at[j], sems.at[1 + j]))
    for copy in copies:
        copy.start()
    window_rows(own, east, west, low, grid, rows)
    copies[0].wait()
    norm_part(attended, rows, weight, gain, mixed_low, attended_grad, gain_part, mixed_all)
    pens = penalties(row[...], col[...])
    near = pl.ds(pl.multiple_of((1 - side[0]) * HALF, 128), HALF)
    far = pl.ds(pl.multiple_of(side[0] * HALF, 128), HALF)
    grad_other[...] = attended_grad[:, near]
    attended_near[...] = attended[:, near]
    attended_far[...] = attended[:, far]
    small[...] = jnp.zeros_like(small)
    for copy in copies[1:]:
        copy.wait()
    for hp in range(3):
        cols = slice(hp * 128, (hp + 1) * 128)
        head = side[0] * 6 + 2 * hp
        gains = gain_part[:, pl.ds(pl.multiple_of(side[0] * HC + hp * 256, 128), 256)]
        store_pair(
            grads,
            small,
            hp,
            *attention_pair(
                scale,
                head,
                heads[0, :, cols],
                heads[1, :, cols],
                heads[2, :, cols],
                attended_grad[:, pl.ds(pl.multiple_of(side[0] * HALF + hp * 128, 128), 128)],
                pair_bias[pl.ds(pl.multiple_of(head * WIN, 8), 2 * WIN), :],
                pens,
                gains,
            ),
        )


def write_coded(value, lines, outs, base):
    high = lines.astype(BF16)
    low = (lines - high.astype(F32)).astype(BF16)
    for i, tail in enumerate((high, low)):
        block = jnp.concatenate([value[i][:, :384].astype(BF16), tail], 1)
        for out in outs:
            out[base + i] = block


def add_coded(keep, recv, outs, source, base):
    value = [keep[source + i].astype(F32) + recv[source + i].astype(F32) for i in range(EXTRA)]
    write_coded(value, value[0][:, 384:] + value[1][:, 384:], outs, base)


def row_of(place):
    y = place["y"]
    return 24 * ((y // 2) * 32 + place["x"] * 8 + place["z"] * 2 + y % 2)


def first_order(core, at):
    end, left = (at == 0) | (at == 3), at < 2
    zero = [jnp.where(end, a, b) for a, b in ((0, 1), (3, 2), (1, 0), (2, 3))]
    one = [jnp.where(left, a, b) for a, b in ((0, 2), (1, 3), (2, 0), (3, 1))]
    return [jnp.where(core == 0, a, b) for a, b in zip(zero, one)]


def second_order(core, at):
    kept = jnp.where(core == 0, at // 2, at % 2)
    return [kept, 1 - kept]


def order_of(place, j, axis, second):
    at = place[1 + "xyz".index(ORDERS[j][axis])]
    return (second_order if second else first_order)(place[0], at)


def weight_body(place, x0, x1, p0, p1, m0, m1, a0, a1, s0, s1, *rest):
    outs, (left, grads, mixed, heads, total, sems) = rest[:6], rest[6:]
    pairs = ((x0, x1, left), (p0, p1, grads), (m0, m1, mixed), (a0, a1, heads))
    copies = []
    for i, (own, other, joined) in enumerate(pairs):
        for k, source in enumerate((own, other)):
            copies.append(
                pltpu.make_async_copy(source, joined.at[k * CELLS : (k + 1) * CELLS], sems.at[2 * i + k])
            )
            copies[-1].start()
    for copy in copies[:4]:
        copy.wait()
    for m in range(4):
        at = slice(m * 384, (m + 1) * 384)
        part = dot(left[:, at], grads[...], TN)
        for j in range(3):
            total[at, j * 512 : j * 512 + HALF] = part[:, j * HALF : (j + 1) * HALF]
    for copy in copies[4:]:
        copy.wait()
    for m in range(4):
        at = slice(m * 384, (m + 1) * 384)
        part = dot(mixed[:, at], heads[...], TN)
        for j in range(3):
            total[at, j * 512 + HALF : (j + 1) * 512] = part[:, j * 128 : (j + 1) * 128]
    for j in range(3):
        cols = slice(j * 512, (j + 1) * 512)
        order = order_of(place, j, 0, False)
        for i in range(4):
            out = outs[2 * j + i // 2]
            for second in range(4):
                for third in range(4):
                    places = (order[i], second, third)
                    start = row_of(dict(zip(ORDERS[j], places)))
                    rows = pl.ds(pl.multiple_of(start, 8), 24)
                    out[i % 2 * 16 + second * 4 + third] = total[rows, cols].astype(BF16)
        at = slice(j * 48, (j + 1) * 48)
        value = s0[at, :] + s1[at, :]
        write_coded([value[:24], value[24:]], value[:24, 384:], outs[2 * j : 2 * j + 2], 32)


def halve_body(count, size, axis, place, *refs):
    ins, outs = refs[:6], refs[6:]
    for j in range(3):
        keep, recv = ins[2 * j : 2 * j + 2]
        order = order_of(place, j, axis, count == 1)
        for i in range(2 * count):
            out = outs[2 * j + i // count]
            for b in range(size):
                at = order[i] * size + b
                out[i % count * size + b] = (keep[at].astype(F32) + recv[at].astype(F32)).astype(BF16)
        add_coded(keep, recv, outs[2 * j : 2 * j + 2], 2 * count * size, count * size)


def total_body(*refs):
    ins, out = refs[:6], refs[6]
    for j in range(3):
        keep, recv = ins[2 * j : 2 * j + 2]
        out[3 * j] = (keep[0].astype(F32) + recv[0].astype(F32)).astype(BF16)
        add_coded(keep, recv, [out], 1, 3 * j + 1)


def finish_body(core, own, other, qkv, proj, pair, gain, qb, vb, scale):
    which = core[0]
    scales = jnp.zeros((128,), F32)
    for side in range(2):
        for j in range(3):
            def block(i):
                return jnp.where(which == side, own[3 * j + i].astype(F32), other[3 * j + i].astype(F32))

            rows = block(0)
            rows = jnp.where(which == 0, rows[:12], rows[12:])
            at = side * HALF + j * 128
            for t in range(3):
                qkv[:, t * HC + at : t * HC + at + 128] = rows[:, t * 128 : (t + 1) * 128]
            proj[:, at : at + 128] = rows[:, HALF:]
            top, bottom = block(1), block(2)
            for g in range(3):
                start = (side * 3 + j) * 144 + g * 48
                pair[start : start + 24, :] = top[:, g * 128 : g * 128 + WIN]
                pair[start + 24 : start + 48, :] = bottom[:, g * 128 : g * 128 + WIN]
            lines = top[:, 384:] + bottom[:, 384:]
            qb[at : at + 128] = lines[0]
            vb[at : at + 128] = lines[1]
            scales = scales + lines[2]
            gain[side * HC + j * 256 : side * HC + j * 256 + 128] = lines[3]
            gain[side * HC + j * 256 + 128 : side * HC + j * 256 + 256] = lines[4]
    scale[...] = scales[:HEADS]


def branch_body(side, w, own, theirs, to_east, to_west, stay_low, stay_high, grads, rows):
    which = side[0]

    @pl.when(pl.program_id(0) == 0)
    def _():
        for pair in range(3):
            for j in range(3):
                at = j * HC + pair * 128
                cols = slice(pair * HALF + j * 128, pair * HALF + (j + 1) * 128)
                grads[:, pl.ds(pl.multiple_of(at + which * HALF, 128), 128)] = own[:, cols]
                grads[:, pl.ds(pl.multiple_of(at + (1 - which) * HALF, 128), 128)] = theirs[:, cols]

    product = dot(grads[...], w[...], NT)
    for i in range(2):
        rows[i] = product[:, i * 128 : (i + 1) * 128]
    columns = [
        jnp.concatenate([rows[i, pl.ds(j, 24, stride=12), :] for i in range(2)], 1) for j in range(12)
    ]
    for out, cols, start in (
        (stay_low, columns[:SHIFT_W], 0),
        (to_east, columns[SHIFT_W:], 0),
        (to_west, columns[:SHIFT_W], HALF_ROWS),
        (stay_high, columns[SHIFT_W:], HALF_ROWS),
    ):
        out[...] = jnp.concatenate([one[start : start + HALF_ROWS] for one in cols], 0).astype(BF16)


def last_rows_body(stay_high, from_east, out):
    start = HALF_ROWS - SHIFT_H
    out[...] = jnp.concatenate(
        [
            f32_rows(half, i * HALF_ROWS + start, SHIFT_H)
            for half in (stay_high, from_east)
            for i in range(SHIFT_W)
        ],
        0,
    ).astype(BF16)


def merge_body(upstream, stay_low, stay_high, from_west, from_east, low, out):
    for j in range(12):
        i = j % SHIFT_W
        upper, lower = (from_west, stay_high) if j < SHIFT_W else (stay_low, from_east)
        back = jnp.concatenate(
            [
                f32_rows(low, j * SHIFT_H, SHIFT_H),
                f32_rows(upper, i * HALF_ROWS, HALF_ROWS),
                f32_rows(lower, i * HALF_ROWS, HALF_ROWS - SHIFT_H),
            ],
            0,
        )
        out[j] = (upstream[j].astype(F32) + back).astype(BF16)


def permuted(value, axes, target):
    sizes = [lax.axis_size(a) for a in axes]
    pairs = []
    for source in range(int(np.prod(sizes))):
        place = np.unravel_index(source, sizes)
        to = target(*[int(v) for v in place])
        pairs.append((source, int(np.ravel_multi_index(to, sizes))))
    return lax.ppermute(value, axes, pairs)


def lon_step(value, steps):
    return permuted(value, LON, lambda *at: np.unravel_index((np.ravel_multi_index(at, (2, 4, 4)) + steps) % 32, (2, 4, 4)))


def lat_step(value, steps):
    return permuted(value, LAT, lambda *at: np.unravel_index((np.ravel_multi_index(at, (2, 2)) + steps) % 4, (2, 2)))


def core_swap(value):
    return permuted(value, ("c",), lambda c: (1 - c,))


def ring_swap(value, axis, step):
    def partner(place, c):
        return place ^ 1 if (step == 0) == (c == 0) else 3 - place

    if axis == "y":
        def target(yh, yl, c):
            to = partner(yh * 2 + yl, c)
            return (to // 2, to % 2, c)
    else:
        def target(place, c):
            return (partner(place, c), c)

    return permuted(value, AXES[axis] + ("c",), target)


def first_messages(grid):
    return call(
        first_body, [shape((36, C), BF16), shape((72, C), BF16)], [grid], scalars=0, name="first"
    )


def halo(grid):
    low, upper = first_messages(grid)
    low = lat_step(low, -1)
    east = lon_step(upper, -1)
    (lower,) = call(
        to_east_body, [shape((72, C), BF16)], [grid, low], scalars=0, name="to_east"
    )
    return east, low, lower


def shards(
    features,
    upstream,
    region_ids,
    qkv_weight,
    query_bias,
    value_bias,
    logit_scale,
    pair_bias,
    proj_weight,
    norm_gain,
):
    core = lax.axis_index("c")
    place = jnp.stack(
        [core, lax.axis_index("x"), lax.axis_index("yh") * 2 + lax.axis_index("yl"), lax.axis_index("z")]
    ).astype(jnp.int32)
    mine = core.astype(jnp.int32).reshape(1)
    theirs = 1 - mine
    scale = logit_scale
    query_row, value_row = query_bias.reshape(1, HC), value_bias.reshape(1, HC)
    pair_rows = pair_bias.reshape(HEADS * WIN, WIN)
    gain = norm_gain.reshape(1, C)

    features = features.transpose(1, 0, 2)
    upstream = upstream.transpose(1, 0, 2)
    east, low, lower = halo(features)
    late, region_ids, lower = lax.optimization_barrier((upstream, region_ids, lower))
    came = east, lon_step(lower, 1), low
    lower_ids = lon_step(region_ids[HALF_ROWS:], 1)
    region_ids = jnp.concatenate([region_ids[:HALF_ROWS], lower_ids], 0)
    region_row = region_ids.reshape(WINDOWS, WIN)
    region_col = region_ids.reshape(-1, 1)
    east, low, lower = halo(late)
    came_late = east, lon_step(lower, 1), low
    x, projected, attended = call(
        forward_body,
        [shape((CELLS, C), BF16), shape((CELLS, 3 * HC), F32), shape((CELLS, HC), BF16)],
        [scale, features, *came, qkv_weight, query_row, value_row, pair_rows, region_row, region_col],
        scratch=[
            pltpu.VMEM((12, CELLS, 128), F32),
            pltpu.VMEM((CELLS, C), F32),
            pltpu.VMEM((C, 3 * HC), BF16),
            pltpu.SemaphoreType.DMA((9,)),
        ],
        flops=2 * CELLS * C * 3 * HC,
        far=(5,),
        name="forward",
    )
    x_other = core_swap(x)
    mixed_low, attended_grad, gain_part, grads_theirs, small_theirs, attended_mine, attended_theirs = call(
        backward_body,
        [
            shape((CELLS, C), BF16),
            shape((CELLS, HALF), F32),
            shape((1, C), F32),
            shape((CELLS, 3 * HALF), BF16),
            shape((144, 512), F32),
            shape((CELLS, HALF), BF16),
            shape((CELLS, HALF), BF16),
        ],
        [
            theirs,
            scale,
            attended,
            upstream,
            *came_late,
            proj_weight,
            gain,
            projected,
            pair_rows,
            region_row,
            region_col,
        ],
        scalars=2,
        scratch=[
            pltpu.VMEM((12, CELLS, 128), F32),
            pltpu.VMEM((CELLS, C), F32),
            pltpu.VMEM((CELLS, C), F32),
            pltpu.VMEM((C, HC), BF16),
            pltpu.VMEM((3, CELLS, HALF), F32),
            pltpu.VMEM((CELLS, HC), F32),
            pltpu.SemaphoreType.DMA((4,)),
        ],
        far=(7,),
        near=(9,),
        flops=4 * CELLS * C * HC + 2 * CELLS * WIN * 128 * 18,
        name="backward",
    )
    mixed_other = core_swap(mixed_low)
    attended_other = core_swap(attended_theirs)

    def attention(side):
        def cols(base):
            return lambda i, side, scale: (0, base + side[0] * 3 + i)

        whole = lambda i, side, scale: (0, 0)
        block = (CELLS, 128)
        return grid_call(
            attention_body,
            (3,),
            [side, scale],
            [
                (projected, block, cols(0)),
                (projected, block, cols(6)),
                (projected, block, cols(12)),
                (attended_grad, block, lambda i, side, scale: (0, i)),
                (pair_rows, (2 * WIN, WIN), lambda i, side, scale: (side[0] * 3 + i, 0)),
                (region_row, (WINDOWS, WIN), whole),
                (region_col, (CELLS, 1), whole),
                (gain_part, (1, 256), cols(0)),
            ],
            [
                (shape((CELLS, 3 * HALF), BF16), (CELLS, HALF), lambda i, side, scale: (0, i)),
                (shape((144, 512), F32), (48, 512), lambda i, side, scale: (i, 0)),
            ],
            flops=2 * CELLS * WIN * 128 * 6 * 3,
            vmem=16,
            name="attention",
        )

    grads_other = core_swap(grads_theirs)
    small_other = core_swap(small_theirs)
    grads_mine, small_mine = attention(mine)

    parts = call(
        weight_body,
        [shape((32 + EXTRA,) + BLOCK, BF16)] * 6,
        [
            place,
            x,
            x_other,
            grads_mine,
            grads_other,
            mixed_low,
            mixed_other,
            attended_mine,
            attended_other,
            small_mine,
            small_other,
        ],
        scratch=[
            pltpu.VMEM((2 * CELLS, C), BF16),
            pltpu.VMEM((2 * CELLS, 3 * HALF), BF16),
            pltpu.VMEM((2 * CELLS, C), BF16),
            pltpu.VMEM((2 * CELLS, HALF), BF16),
            pltpu.VMEM((C, C), F32),
            pltpu.SemaphoreType.DMA((8,)),
        ],
        near=tuple(range(1, 9)),
        flops=4 * CELLS * C * C,
        vmem=26,
        name="weights",
    )
    side, parts = lax.optimization_barrier((mine, parts))
    order = place
    whole = lambda i, side: (0, 0)
    to_east, to_west, stay_low, stay_high = grid_call(
        branch_body,
        (6,),
        [side],
        [
            (qkv_weight, (256, 3 * HC), lambda i, side: (i, 0)),
            (grads_mine, (CELLS, 3 * HALF), whole),
            (grads_theirs, (CELLS, 3 * HALF), whole),
        ],
        [(shape((72, C), BF16), (72, 256), lambda i, side: (0, i))] * 4,
        scratch=[pltpu.VMEM((CELLS, 3 * HC), BF16), pltpu.VMEM((2, CELLS, 128), F32)],
        flops=2 * CELLS * C * 3 * HC,
        vmem=16,
        name="branch",
    )
    from_west = lon_step(to_east, 1)
    from_east = lon_step(to_west, -1)
    (last,) = call(
        last_rows_body, [shape((36, C), BF16)], [stay_high, from_east], scalars=0, vmem=6, name="last_rows"
    )
    low = lat_step(last, 1)
    for step in range(6):
        terms = []
        for j, names in enumerate(ORDERS):
            terms += [parts[2 * j], ring_swap(parts[2 * j + 1], names[step // 2], step % 2)]
        if step == 5:
            break
        left = 32 >> step
        if step % 2 == 0:
            body = functools.partial(halve_body, 1, left // 2, step // 2)
        else:
            body = functools.partial(halve_body, 2, left // 4, step // 2 + 1)
        if step == 0:
            order, stay_low = lax.optimization_barrier((order, stay_low))
        if step == 3:
            order, from_west = lax.optimization_barrier((order, from_west))
        if step == 4:
            order, low = lax.optimization_barrier((order, low))
        if step == 2:
            order, last = lax.optimization_barrier((order, last))
        parts = call(body, [shape((left // 2 + EXTRA,) + BLOCK, BF16)] * 6, [order, *terms], vmem=10, name="halve")
    (input_grad,) = call(
        merge_body,
        [shape((12, 24, C), BF16)],
        [upstream, stay_low, stay_high, from_west, from_east, low],
        scalars=0,
        vmem=10,
        name="merge",
    )
    terms, input_grad = lax.optimization_barrier((terms, input_grad))
    (sums,) = call(total_body, [shape((9,) + BLOCK, BF16)], terms, scalars=0, vmem=6, name="total")
    sums_other = core_swap(sums)
    qkv_weight_grad, proj_weight_grad, pair_grad, gain_grad, query_bias_grad, value_bias_grad, scale_grad = call(
        finish_body,
        [
            shape((12, 3 * HC), F32),
            shape((12, HC), F32),
            shape((HEADS * WIN, WIN), F32),
            shape((C,), F32),
            shape((HC,), F32),
            shape((HC,), F32),
            shape((HEADS,), F32),
        ],
        [mine, sums, sums_other],
        vmem=8,
        name="finish",
    )
    pair_grad = pair_grad.reshape(HEADS, WIN, WIN)

    return (
        input_grad.transpose(1, 0, 2),
        qkv_weight_grad,
        proj_weight_grad,
        gain_grad,
        query_bias_grad,
        value_bias_grad,
        scale_grad,
        pair_grad,
    )


def solution(mesh):
    fine = Mesh(mesh.devices.reshape(2, 4, 4, 2, 2), ("yh", "x", "z", "yl", "c"))
    every = LON + LAT
    return jax.shard_map(
        shards,
        mesh=fine,
        in_specs=(P(LAT, LON, None), P(LAT, LON, None), P(LAT, LON)) + (P(),) * 7,
        out_specs=(P(LAT, LON, None), P(every, None), P(every, None)) + (P(),) * 5,
        check_vma=False,
    )
```

```python
import functools

import jax
import jax.numpy as jnp
import numpy as np
from jax import lax
from jax.experimental import pallas as pl
from jax.experimental.pallas import tpu as pltpu
from jax.sharding import Mesh
from jax.sharding import PartitionSpec as P

HEADS = 12
HEAD_DIM = 64
WIN_H = 6
WIN_W = 12
SHIFT_H = 3
SHIFT_W = 6
WIN = 72
C = 1536
HC = 768
HALF = 384
CELLS = 288
WINDOWS = 4
COSINE_EPS = 1e-06
NORM_EPS = 1e-05

F32 = jnp.float32
BF16 = jnp.bfloat16
LON = ("yh", "x", "z")
LAT = ("yl", "c")
Y = ("yh", "yl")
ORDERS = (("x", "y", "z"), ("y", "z", "x"), ("z", "x", "y"))
AXES = {"x": ("x",), "y": Y, "z": ("z",)}
BLOCK = (24, 512)
EXTRA = 2
NT = (((1,), (1,)), ((), ()))
TN = (((0,), (0,)), ((), ()))
NN = (((1,), (0,)), ((), ()))
VMEM = pl.BlockSpec(memory_space=pltpu.VMEM)
HBM = pl.BlockSpec(memory_space=pltpu.HBM)
ANY = pl.BlockSpec(memory_space=pl.ANY)
SMEM = pl.BlockSpec(memory_space=pltpu.SMEM)


def dot(left, right, dims=NN):
    return lax.dot_general(left, right, dims, preferred_element_type=F32)


def cost(outs, operands, flops):
    moved = sum(int(np.prod(o.shape)) * o.dtype.itemsize for o in (*outs, *operands))
    return pl.CostEstimate(flops=flops, bytes_accessed=moved, transcendentals=0)


def call(body, outs, operands, scalars=1, scratch=(), flops=0, vmem=50, far=(), near=(), name=None):
    specs = [SMEM] * scalars + [VMEM] * (len(operands) - scalars)
    for i in far:
        specs[i] = HBM
    for i in near:
        specs[i] = ANY
    return pl.pallas_call(
        body,
        out_shape=list(outs),
        in_specs=specs,
        out_specs=[VMEM] * len(outs),
        scratch_shapes=list(scratch),
        compiler_params=pltpu.CompilerParams(vmem_limit_bytes=vmem * 2**20),
        cost_estimate=cost(outs, operands, flops),
        name=name,
    )(*operands)


def grid_call(body, grid, scalars, ins, outs, scratch=(), flops=0, vmem=50, name=None):
    operands = [array for array, _, _ in ins]
    results = [result for result, _, _ in outs]
    spec = pltpu.PrefetchScalarGridSpec(
        num_scalar_prefetch=len(scalars),
        grid=grid,
        in_specs=[pl.BlockSpec(block, at) for _, block, at in ins],
        out_specs=[pl.BlockSpec(block, at) for _, block, at in outs],
        scratch_shapes=list(scratch),
    )
    return pl.pallas_call(
        body,
        grid_spec=spec,
        out_shape=results,
        compiler_params=pltpu.CompilerParams(vmem_limit_bytes=vmem * 2**20),
        cost_estimate=cost(results, operands, flops),
        name=name,
    )(*scalars, *operands)


def shape(dims, dtype):
    return jax.ShapeDtypeStruct(dims, dtype)


def head_sum(value):
    rows = lax.broadcasted_iota(jnp.int32, (128, 128), 0) // HEAD_DIM
    cols = lax.broadcasted_iota(jnp.int32, (128, 128), 1) // HEAD_DIM
    ones = (rows == cols).astype(F32).astype(BF16)
    high = value.astype(BF16)
    low = (value - high.astype(F32)).astype(BF16)
    return dot(high, ones) + dot(low, ones)


def low_half(rows):
    return lax.broadcasted_iota(jnp.int32, (rows, 128), 1) < HEAD_DIM


def stacked(value):
    mask = low_half(WIN)
    return jnp.concatenate([jnp.where(mask, value, 0.0), jnp.where(mask, 0.0, value)], 0).astype(BF16)


def unstacked(value):
    return jnp.where(low_half(WIN), value[:WIN], value[WIN:])


def normalized(rows):
    inv = lax.rsqrt(head_sum(rows * rows) + COSINE_EPS)
    return rows * inv, inv


def penalties(region_row, region_col):
    out = []
    for w in range(WINDOWS):
        same = region_row[w : w + 1, :] == region_col[w * WIN : (w + 1) * WIN, :]
        one = jnp.where(same, 0.0, -100.0).astype(F32)
        out.append(jnp.concatenate([one, one], 0))
    return out


def two_heads(scale_ref, head):
    top = lax.broadcasted_iota(jnp.int32, (2 * WIN, 1), 0) < WIN
    return jnp.exp(jnp.where(top, scale_ref[head], scale_ref[head + 1]))


def softmax_of(scores):
    exp_scores = [jnp.exp(one) for one in scores]
    sums = [jnp.sum(one, -1, keepdims=True) for one in exp_scores]
    return [one / total for one, total in zip(exp_scores, sums)]


SPANS = [slice(n * WIN, (n + 1) * WIN) for n in range(WINDOWS)]


HALF_ROWS = 12


def f32_rows(ref, start, count):
    return ref[...].astype(F32)[start : start + count]


def window_rows(own, east, west, low, grid, rows):
    for j in range(12):
        i = j % SHIFT_W
        if j < SHIFT_W:
            upper = own[SHIFT_W + i].astype(F32)[SHIFT_H : SHIFT_H + HALF_ROWS]
            lower = [f32_rows(west, i * HALF_ROWS, HALF_ROWS)]
        else:
            upper = f32_rows(east, i * HALF_ROWS, HALF_ROWS)
            lower = [own[i].astype(F32)[SHIFT_H + HALF_ROWS :], f32_rows(low, i * SHIFT_H, SHIFT_H)]
        column = jnp.concatenate([upper] + lower, 0)
        for t in range(12):
            grid[t, j * 24 : (j + 1) * 24, :] = column[:, t * 128 : (t + 1) * 128]
    for r in range(24):
        for t in range(12):
            rows[r * 12 : (r + 1) * 12, t * 128 : (t + 1) * 128] = grid[t, pl.ds(r, 12, stride=24), :]


def first_body(own, low, upper, lower):
    low[...] = jnp.concatenate([own[j].astype(F32)[:SHIFT_H] for j in range(12)], 0).astype(BF16)
    upper[...] = jnp.concatenate(
        [own[j].astype(F32)[SHIFT_H : SHIFT_H + HALF_ROWS] for j in range(SHIFT_W)], 0
    ).astype(BF16)
    lower[...] = jnp.concatenate(
        [own[SHIFT_W + i].astype(F32)[SHIFT_H + HALF_ROWS :] for i in range(SHIFT_W)], 0
    ).astype(BF16)


def to_east_body(lower, low, out):
    count = HALF_ROWS - SHIFT_H
    out[...] = jnp.concatenate(
        [
            piece
            for i in range(SHIFT_W)
            for piece in (
                f32_rows(lower, i * count, count),
                f32_rows(low, (SHIFT_W + i) * SHIFT_H, SHIFT_H),
            )
        ],
        0,
    ).astype(BF16)


def forward_body(
    scale, own, east, west, low, w, query_bias, value_bias, pair_bias, row, col, x, projected, attended, grid, rows, wide, sems
):
    copies = []
    for g in range(3):
        for j in range(3):
            at = pl.ds(j * HC + g * 256, 256)
            copies.append(pltpu.make_async_copy(w.at[:, at], wide.at[:, at], sems.at[3 * g + j]))
            copies[-1].start()
    window_rows(own, east, west, low, grid, rows)
    x[...] = rows[...].astype(BF16)
    pens = penalties(row[...], col[...])
    for g in range(3):
        for j in range(3):
            lo = j * HC + g * 256
            copies[3 * g + j].wait()
            product = dot(x[...], wide[:, lo : lo + 256])
            if j != 1:
                product = product + (query_bias, None, value_bias)[j][g * 256 : (g + 1) * 256].reshape(1, 256)
            projected[:, lo : lo + 256] = product
        for half in range(2):
            lo = g * 256 + half * 128
            head = lo // HEAD_DIM
            factor = two_heads(scale, head)
            q = normalized(projected[:, lo : lo + 128])[0]
            k = normalized(projected[:, HC + lo : HC + lo + 128])[0]
            v = projected[:, 2 * HC + lo : 2 * HC + lo + 128]
            pb = pair_bias[head * WIN : (head + 2) * WIN, :]
            cosines = [dot(stacked(q[at]), k[at].astype(BF16), NT) for at in SPANS]
            attention = softmax_of([c * factor + pb + pen for c, pen in zip(cosines, pens)])
            outs = [dot(a.astype(BF16), v[at].astype(BF16)) for a, at in zip(attention, SPANS)]
            attended[:, lo : lo + 128] = jnp.concatenate([unstacked(o) for o in outs], 0).astype(BF16)


def norm_part(attended, rows, pw, gain, mixed_low, attended_grad, gain_part, mixed_all):
    for n in range(6):
        at = slice(n * 256, (n + 1) * 256)
        mixed_all[:, at] = dot(attended[...], pw[at, :], NT)
    total = jnp.zeros((1, C), F32)
    for r in range(6):
        at = slice(r * 48, (r + 1) * 48)
        mixed = mixed_all[at, :]
        center = mixed - jnp.mean(mixed, -1, keepdims=True)
        inv_std = lax.rsqrt(jnp.mean(center * center, -1, keepdims=True) + NORM_EPS)
        normed = center * inv_std
        up = rows[at, :]
        total = total + jnp.sum(up * normed, 0, keepdims=True)
        scaled = up * gain[...].reshape(1, C)
        grad = inv_std * (
            scaled
            - jnp.mean(scaled, -1, keepdims=True)
            - normed * jnp.mean(scaled * normed, -1, keepdims=True)
        )
        mixed_low[at, :] = grad.astype(BF16)
    gain_part[...] = total
    for n in range(3):
        at = slice(n * 256, (n + 1) * 256)
        attended_grad[:, at] = dot(mixed_low[...], pw[:, at]).astype(BF16).astype(F32)


def attention_pair(scale, head, q, k, v, da, pb, pens, gains):
    factor = two_heads(scale, head)
    q, q_inv = normalized(q)
    k, k_inv = normalized(k)
    qs = [stacked(q[at]) for at in SPANS]
    das = [stacked(da[at]) for at in SPANS]
    kb = [k[at].astype(BF16) for at in SPANS]
    vb = [v[at].astype(BF16) for at in SPANS]
    cosines = [dot(a, b, NT) for a, b in zip(qs, kb)]
    prob_grads = [dot(a, b, NT) for a, b in zip(das, vb)]
    attention = softmax_of([c * factor + pb + pen for c, pen in zip(cosines, pens)])
    v_grad = jnp.concatenate([dot(a.astype(BF16), b, TN) for a, b in zip(attention, das)], 0)
    means = [jnp.sum(a * p, -1, keepdims=True) for a, p in zip(attention, prob_grads)]
    score_grads = [a * (p - m) for a, p, m in zip(attention, prob_grads, means)]
    cosine_grads = [(s * factor).astype(BF16) for s in score_grads]
    gq = jnp.concatenate([unstacked(dot(c, b)) for c, b in zip(cosine_grads, kb)], 0)
    gk = jnp.concatenate([dot(c, b, TN) for c, b in zip(cosine_grads, qs)], 0)
    pair = (score_grads[0] + score_grads[1]) + (score_grads[2] + score_grads[3])
    scaled = sum(s * c for s, c in zip(score_grads, cosines))
    lane = lax.broadcasted_iota(jnp.int32, (1, 128), 1)
    scale_line = jnp.zeros((1, 128), F32)
    for i in range(2):
        one = jnp.sum(jnp.sum(scaled[i * WIN : (i + 1) * WIN], 0, keepdims=True), 1, keepdims=True)
        scale_line = scale_line + jnp.where(lane == head + i, one * factor[i * WIN : i * WIN + 1], 0.0)
    q_grad = q_inv * (gq - q * head_sum(q * gq))
    k_grad = k_inv * (gk - k * head_sum(k * gk))
    lines = jnp.concatenate(
        [
            jnp.sum(q_grad, 0, keepdims=True),
            jnp.sum(v_grad, 0, keepdims=True),
            scale_line,
            gains[:, :128],
            gains[:, 128:],
            jnp.zeros((11, 128), F32),
        ],
        0,
    )
    return (q_grad, k_grad, v_grad), pair, lines


def store_pair(grads, small, at, parts, pair, lines):
    for i, part in enumerate(parts):
        grads[:, at * HALF + i * 128 : at * HALF + (i + 1) * 128] = part.astype(BF16)
    rows = slice(at * 48, (at + 1) * 48)
    for g in range(3):
        small[rows, g * 128 : g * 128 + WIN] = pair[g * 48 : (g + 1) * 48]
    small[at * 48 : at * 48 + 16, 384:] = lines


def attention_body(side, scale, projected, da, pair_bias, row, col, gain_part, grads, small, heads, sems):
    copies = []
    for hp in range(3):
        for j in range(4):
            lane = hp * 128 if j == 3 else pl.multiple_of(j * HC + side[0] * HALF + hp * 128, 128)
            source = (da if j == 3 else projected).at[:, pl.ds(lane, 128)]
            copies.append(pltpu.make_async_copy(source, heads.at[hp, j], sems.at[4 * hp + j]))
            copies[-1].start()
    pens = penalties(row[...], col[...])
    small[...] = jnp.zeros_like(small)
    for hp in range(3):
        for copy in copies[4 * hp : 4 * hp + 4]:
            copy.wait()
        head = side[0] * 6 + 2 * hp
        store_pair(
            grads,
            small,
            hp,
            *attention_pair(
                scale,
                head,
                *(heads[hp, j] for j in range(4)),
                pair_bias[pl.ds(pl.multiple_of(head * WIN, 8), 2 * WIN), :],
                pens,
                gain_part[:, pl.ds(pl.multiple_of(side[0] * HC + hp * 256, 128), 256)],
            ),
        )


def backward_body(
    side,
    scale,
    attended,
    own,
    east,
    west,
    low,
    pw,
    gain,
    projected,
    pair_bias,
    row,
    col,
    mixed_low,
    grad_other,
    gain_part,
    grads,
    small,
    attended_near,
    attended_far,
    grid,
    rows,
    mixed_all,
    weight,
    heads,
    attended_grad,
    sems,
):
    copies = [pltpu.make_async_copy(pw, weight, sems.at[0])]
    for j in range(3):
        at = pl.ds(pl.multiple_of(j * HC + side[0] * HALF, 128), HALF)
        copies.append(pltpu.make_async_copy(projected.at[:, at], heads.at[j], sems.at[1 + j]))
    for copy in copies:
        copy.start()
    window_rows(own, east, west, low, grid, rows)
    copies[0].wait()
    norm_part(attended, rows, weight, gain, mixed_low, attended_grad, gain_part, mixed_all)
    pens = penalties(row[...], col[...])
    near = pl.ds(pl.multiple_of((1 - side[0]) * HALF, 128), HALF)
    far = pl.ds(pl.multiple_of(side[0] * HALF, 128), HALF)
    grad_other[...] = attended_grad[:, near]
    attended_near[...] = attended[:, near]
    attended_far[...] = attended[:, far]
    small[...] = jnp.zeros_like(small)
    for copy in copies[1:]:
        copy.wait()
    for hp in range(3):
        cols = slice(hp * 128, (hp + 1) * 128)
        head = side[0] * 6 + 2 * hp
        gains = gain_part[:, pl.ds(pl.multiple_of(side[0] * HC + hp * 256, 128), 256)]
        store_pair(
            grads,
            small,
            hp,
            *attention_pair(
                scale,
                head,
                heads[0, :, cols],
                heads[1, :, cols],
                heads[2, :, cols],
                attended_grad[:, pl.ds(pl.multiple_of(side[0] * HALF + hp * 128, 128), 128)],
                pair_bias[pl.ds(pl.multiple_of(head * WIN, 8), 2 * WIN), :],
                pens,
                gains,
            ),
        )


def write_coded(value, lines, outs, base):
    high = lines.astype(BF16)
    low = (lines - high.astype(F32)).astype(BF16)
    for i, tail in enumerate((high, low)):
        block = jnp.concatenate([value[i][:, :384].astype(BF16), tail], 1)
        for out in outs:
            out[base + i] = block


def add_coded(keep, recv, outs, source, base):
    value = [keep[source + i].astype(F32) + recv[source + i].astype(F32) for i in range(EXTRA)]
    write_coded(value, value[0][:, 384:] + value[1][:, 384:], outs, base)


def row_of(place):
    y = place["y"]
    return 24 * ((y // 2) * 32 + place["x"] * 8 + place["z"] * 2 + y % 2)


def first_order(core, at):
    end, left = (at == 0) | (at == 3), at < 2
    zero = [jnp.where(end, a, b) for a, b in ((0, 1), (3, 2), (1, 0), (2, 3))]
    one = [jnp.where(left, a, b) for a, b in ((0, 2), (1, 3), (2, 0), (3, 1))]
    return [jnp.where(core == 0, a, b) for a, b in zip(zero, one)]


def second_order(core, at):
    kept = jnp.where(core == 0, at // 2, at % 2)
    return [kept, 1 - kept]


def order_of(place, j, axis, second):
    at = place[1 + "xyz".index(ORDERS[j][axis])]
    return (second_order if second else first_order)(place[0], at)


def weight_body(place, x0, x1, p0, p1, m0, m1, a0, a1, s0, s1, *rest):
    outs, (left, grads, mixed, heads, total, sems) = rest[:6], rest[6:]
    pairs = ((x0, x1, left), (p0, p1, grads), (m0, m1, mixed), (a0, a1, heads))
    copies = []
    for i, (own, other, joined) in enumerate(pairs):
        for k, source in enumerate((own, other)):
            copies.append(
                pltpu.make_async_copy(source, joined.at[k * CELLS : (k + 1) * CELLS], sems.at[2 * i + k])
            )
            copies[-1].start()
    for copy in copies[:4]:
        copy.wait()
    for m in range(4):
        at = slice(m * 384, (m + 1) * 384)
        part = dot(left[:, at], grads[...], TN)
        for j in range(3):
            total[at, j * 512 : j * 512 + HALF] = part[:, j * HALF : (j + 1) * HALF]
    for copy in copies[4:]:
        copy.wait()
    for m in range(4):
        at = slice(m * 384, (m + 1) * 384)
        part = dot(mixed[:, at], heads[...], TN)
        for j in range(3):
            total[at, j * 512 + HALF : (j + 1) * 512] = part[:, j * 128 : (j + 1) * 128]
    for j in range(3):
        cols = slice(j * 512, (j + 1) * 512)
        order = order_of(place, j, 0, False)
        for i in range(4):
            out = outs[2 * j + i // 2]
            for second in range(4):
                for third in range(4):
                    places = (order[i], second, third)
                    start = row_of(dict(zip(ORDERS[j], places)))
                    rows = pl.ds(pl.multiple_of(start, 8), 24)
                    out[i % 2 * 16 + second * 4 + third] = total[rows, cols].astype(BF16)
        at = slice(j * 48, (j + 1) * 48)
        value = s0[at, :] + s1[at, :]
        write_coded([value[:24], value[24:]], value[:24, 384:], outs[2 * j : 2 * j + 2], 32)


def halve_body(count, size, axis, place, *refs):
    ins, outs = refs[:6], refs[6:]
    for j in range(3):
        keep, recv = ins[2 * j : 2 * j + 2]
        order = order_of(place, j, axis, count == 1)
        for i in range(2 * count):
            out = outs[2 * j + i // count]
            for b in range(size):
                at = order[i] * size + b
                out[i % count * size + b] = (keep[at].astype(F32) + recv[at].astype(F32)).astype(BF16)
        add_coded(keep, recv, outs[2 * j : 2 * j + 2], 2 * count * size, count * size)


def total_body(*refs):
    ins, out = refs[:6], refs[6]
    for j in range(3):
        keep, recv = ins[2 * j : 2 * j + 2]
        out[3 * j] = (keep[0].astype(F32) + recv[0].astype(F32)).astype(BF16)
        add_coded(keep, recv, [out], 1, 3 * j + 1)


def finish_body(core, own, other, qkv, proj, pair, gain, qb, vb, scale):
    which = core[0]
    scales = jnp.zeros((128,), F32)
    for side in range(2):
        for j in range(3):
            def block(i):
                return jnp.where(which == side, own[3 * j + i].astype(F32), other[3 * j + i].astype(F32))

            rows = block(0)
            rows = jnp.where(which == 0, rows[:12], rows[12:])
            at = side * HALF + j * 128
            for t in range(3):
                qkv[:, t * HC + at : t * HC + at + 128] = rows[:, t * 128 : (t + 1) * 128]
            proj[:, at : at + 128] = rows[:, HALF:]
            top, bottom = block(1), block(2)
            for g in range(3):
                start = (side * 3 + j) * 144 + g * 48
                pair[start : start + 24, :] = top[:, g * 128 : g * 128 + WIN]
                pair[start + 24 : start + 48, :] = bottom[:, g * 128 : g * 128 + WIN]
            lines = top[:, 384:] + bottom[:, 384:]
            qb[at : at + 128] = lines[0]
            vb[at : at + 128] = lines[1]
            scales = scales + lines[2]
            gain[side * HC + j * 256 : side * HC + j * 256 + 128] = lines[3]
            gain[side * HC + j * 256 + 128 : side * HC + j * 256 + 256] = lines[4]
    scale[...] = scales[:HEADS]


def branch_body(side, w, own, theirs, to_east, to_west, stay_low, stay_high, grads, rows):
    which = side[0]

    @pl.when(pl.program_id(0) == 0)
    def _():
        for pair in range(3):
            for j in range(3):
                at = j * HC + pair * 128
                cols = slice(pair * HALF + j * 128, pair * HALF + (j + 1) * 128)
                grads[:, pl.ds(pl.multiple_of(at + which * HALF, 128), 128)] = own[:, cols]
                grads[:, pl.ds(pl.multiple_of(at + (1 - which) * HALF, 128), 128)] = theirs[:, cols]

    product = dot(grads[...], w[...], NT)
    for i in range(2):
        rows[i] = product[:, i * 128 : (i + 1) * 128]
    columns = [
        jnp.concatenate([rows[i, pl.ds(j, 24, stride=12), :] for i in range(2)], 1) for j in range(12)
    ]
    for out, cols, start in (
        (stay_low, columns[:SHIFT_W], 0),
        (to_east, columns[SHIFT_W:], 0),
        (to_west, columns[:SHIFT_W], HALF_ROWS),
        (stay_high, columns[SHIFT_W:], HALF_ROWS),
    ):
        out[...] = jnp.concatenate([one[start : start + HALF_ROWS] for one in cols], 0).astype(BF16)


def last_rows_body(stay_high, from_east, out):
    start = HALF_ROWS - SHIFT_H
    out[...] = jnp.concatenate(
        [
            f32_rows(half, i * HALF_ROWS + start, SHIFT_H)
            for half in (stay_high, from_east)
            for i in range(SHIFT_W)
        ],
        0,
    ).astype(BF16)


def merge_body(upstream, stay_low, stay_high, from_west, from_east, low, out):
    for j in range(12):
        i = j % SHIFT_W
        upper, lower = (from_west, stay_high) if j < SHIFT_W else (stay_low, from_east)
        back = jnp.concatenate(
            [
                f32_rows(low, j * SHIFT_H, SHIFT_H),
                f32_rows(upper, i * HALF_ROWS, HALF_ROWS),
                f32_rows(lower, i * HALF_ROWS, HALF_ROWS - SHIFT_H),
            ],
            0,
        )
        out[j] = (upstream[j].astype(F32) + back).astype(BF16)


def permuted(value, axes, target):
    sizes = [lax.axis_size(a) for a in axes]
    pairs = []
    for source in range(int(np.prod(sizes))):
        place = np.unravel_index(source, sizes)
        to = target(*[int(v) for v in place])
        pairs.append((source, int(np.ravel_multi_index(to, sizes))))
    return lax.ppermute(value, axes, pairs)


def lon_step(value, steps):
    return permuted(value, LON, lambda *at: np.unravel_index((np.ravel_multi_index(at, (2, 4, 4)) + steps) % 32, (2, 4, 4)))


def lat_step(value, steps):
    return permuted(value, LAT, lambda *at: np.unravel_index((np.ravel_multi_index(at, (2, 2)) + steps) % 4, (2, 2)))


def core_swap(value):
    return permuted(value, ("c",), lambda c: (1 - c,))


def ring_swap(value, axis, step):
    def partner(place, c):
        return place ^ 1 if (step == 0) == (c == 0) else 3 - place

    if axis == "y":
        def target(yh, yl, c):
            to = partner(yh * 2 + yl, c)
            return (to // 2, to % 2, c)
    else:
        def target(place, c):
            return (partner(place, c), c)

    return permuted(value, AXES[axis] + ("c",), target)


def first_messages(grid):
    return call(
        first_body,
        [shape((36, C), BF16), shape((72, C), BF16), shape((54, C), BF16)],
        [grid],
        scalars=0,
        name="first",
    )


def halo(low, upper, lower):
    low = lat_step(low, -1)
    east = lon_step(upper, -1)
    (lower,) = call(to_east_body, [shape((72, C), BF16)], [lower, low], scalars=0, name="to_east")
    return east, low, lower


def shards(
    features,
    upstream,
    region_ids,
    qkv_weight,
    query_bias,
    value_bias,
    logit_scale,
    pair_bias,
    proj_weight,
    norm_gain,
):
    core = lax.axis_index("c")
    place = jnp.stack(
        [core, lax.axis_index("x"), lax.axis_index("yh") * 2 + lax.axis_index("yl"), lax.axis_index("z")]
    ).astype(jnp.int32)
    mine = core.astype(jnp.int32).reshape(1)
    theirs = 1 - mine
    scale = logit_scale
    pair_rows = pair_bias.reshape(HEADS * WIN, WIN)
    gain = norm_gain

    features = features.transpose(1, 0, 2)
    upstream = upstream.transpose(1, 0, 2)
    late = first_messages(upstream)
    east, low, lower = halo(*first_messages(features))
    late, region_ids, lower = lax.optimization_barrier((late, region_ids, lower))
    came = east, lon_step(lower, 1), low
    lower_ids = lon_step(region_ids[HALF_ROWS:], 1)
    region_ids = jnp.concatenate([region_ids[:HALF_ROWS], lower_ids], 0)
    region_row = region_ids.reshape(WINDOWS, WIN)
    region_col = region_ids.reshape(-1, 1)
    east, low, lower = halo(*late)
    came_late = east, lon_step(lower, 1), low
    x, projected, attended = call(
        forward_body,
        [shape((CELLS, C), BF16), shape((CELLS, 3 * HC), F32), shape((CELLS, HC), BF16)],
        [scale, features, *came, qkv_weight, query_bias, value_bias, pair_rows, region_row, region_col],
        scratch=[
            pltpu.VMEM((12, CELLS, 128), F32),
            pltpu.VMEM((CELLS, C), F32),
            pltpu.VMEM((C, 3 * HC), BF16),
            pltpu.SemaphoreType.DMA((9,)),
        ],
        flops=2 * CELLS * C * 3 * HC,
        far=(5,),
        name="forward",
    )
    x_other = core_swap(x)
    mixed_low, grad_mine, gain_part, grads_theirs, small_theirs, attended_mine, attended_theirs = call(
        backward_body,
        [
            shape((CELLS, C), BF16),
            shape((CELLS, HALF), F32),
            shape((1, C), F32),
            shape((CELLS, 3 * HALF), BF16),
            shape((144, 512), F32),
            shape((CELLS, HALF), BF16),
            shape((CELLS, HALF), BF16),
        ],
        [
            theirs,
            scale,
            attended,
            upstream,
            *came_late,
            proj_weight,
            gain,
            projected,
            pair_rows,
            region_row,
            region_col,
        ],
        scalars=2,
        scratch=[
            pltpu.VMEM((12, CELLS, 128), F32),
            pltpu.VMEM((CELLS, C), F32),
            pltpu.VMEM((CELLS, C), F32),
            pltpu.VMEM((C, HC), BF16),
            pltpu.VMEM((3, CELLS, HALF), F32),
            pltpu.VMEM((CELLS, HC), F32),
            pltpu.SemaphoreType.DMA((4,)),
        ],
        far=(7,),
        near=(9,),
        flops=4 * CELLS * C * HC + 2 * CELLS * WIN * 128 * 18,
        name="backward",
    )
    mixed_other = core_swap(mixed_low)
    attended_other = core_swap(attended_theirs)

    grads_other = core_swap(grads_theirs)
    small_other = core_swap(small_theirs)
    grads_mine, small_mine = call(
        attention_body,
        [shape((CELLS, 3 * HALF), BF16), shape((144, 512), F32)],
        [mine, scale, projected, grad_mine, pair_rows, region_row, region_col, gain_part],
        scalars=2,
        scratch=[pltpu.VMEM((3, 4, CELLS, 128), F32), pltpu.SemaphoreType.DMA((12,))],
        flops=2 * CELLS * WIN * 128 * 6 * 3,
        vmem=16,
        near=(2, 3),
        name="attention",
    )

    parts = call(
        weight_body,
        [shape((32 + EXTRA,) + BLOCK, BF16)] * 6,
        [
            place,
            x,
            x_other,
            grads_mine,
            grads_other,
            mixed_low,
            mixed_other,
            attended_mine,
            attended_other,
            small_mine,
            small_other,
        ],
        scratch=[
            pltpu.VMEM((2 * CELLS, C), BF16),
            pltpu.VMEM((2 * CELLS, 3 * HALF), BF16),
            pltpu.VMEM((2 * CELLS, C), BF16),
            pltpu.VMEM((2 * CELLS, HALF), BF16),
            pltpu.VMEM((C, C), F32),
            pltpu.SemaphoreType.DMA((8,)),
        ],
        near=tuple(range(1, 9)),
        flops=4 * CELLS * C * C,
        vmem=26,
        name="weights",
    )
    side, parts = lax.optimization_barrier((mine, parts))
    order = place
    whole = lambda i, side: (0, 0)
    to_east, to_west, stay_low, stay_high = grid_call(
        branch_body,
        (6,),
        [side],
        [
            (qkv_weight, (256, 3 * HC), lambda i, side: (i, 0)),
            (grads_mine, (CELLS, 3 * HALF), whole),
            (grads_theirs, (CELLS, 3 * HALF), whole),
        ],
        [(shape((72, C), BF16), (72, 256), lambda i, side: (0, i))] * 4,
        scratch=[pltpu.VMEM((CELLS, 3 * HC), BF16), pltpu.VMEM((2, CELLS, 128), F32)],
        flops=2 * CELLS * C * 3 * HC,
        vmem=16,
        name="branch",
    )
    from_west = lon_step(to_east, 1)
    from_east = lon_step(to_west, -1)
    (last,) = call(
        last_rows_body, [shape((36, C), BF16)], [stay_high, from_east], scalars=0, vmem=6, name="last_rows"
    )
    low = lat_step(last, 1)
    for step in range(6):
        terms = []
        for j, names in enumerate(ORDERS):
            terms += [parts[2 * j], ring_swap(parts[2 * j + 1], names[step // 2], step % 2)]
        if step == 5:
            break
        left = 32 >> step
        if step % 2 == 0:
            body = functools.partial(halve_body, 1, left // 2, step // 2)
        else:
            body = functools.partial(halve_body, 2, left // 4, step // 2 + 1)
        if step == 0:
            order, stay_low = lax.optimization_barrier((order, stay_low))
        if step == 3:
            order, last = lax.optimization_barrier((order, last))
        parts = call(body, [shape((left // 2 + EXTRA,) + BLOCK, BF16)] * 6, [order, *terms], vmem=10, name="halve")
    (input_grad,) = call(
        merge_body,
        [shape((12, 24, C), BF16)],
        [upstream, stay_low, stay_high, from_west, from_east, low],
        scalars=0,
        vmem=10,
        name="merge",
    )
    terms, input_grad = lax.optimization_barrier((terms, input_grad))
    (sums,) = call(total_body, [shape((9,) + BLOCK, BF16)], terms, scalars=0, vmem=6, name="total")
    sums_other = core_swap(sums)
    qkv_weight_grad, proj_weight_grad, pair_grad, gain_grad, query_bias_grad, value_bias_grad, scale_grad = call(
        finish_body,
        [
            shape((12, 3 * HC), F32),
            shape((12, HC), F32),
            shape((HEADS * WIN, WIN), F32),
            shape((C,), F32),
            shape((HC,), F32),
            shape((HC,), F32),
            shape((HEADS,), F32),
        ],
        [mine, sums, sums_other],
        vmem=8,
        name="finish",
    )
    pair_grad = pair_grad.reshape(HEADS, WIN, WIN)

    return (
        input_grad.transpose(1, 0, 2),
        qkv_weight_grad,
        proj_weight_grad,
        gain_grad,
        query_bias_grad,
        value_bias_grad,
        scale_grad,
        pair_grad,
    )


def solution(mesh):
    fine = Mesh(mesh.devices.reshape(2, 4, 4, 2, 2), ("yh", "x", "z", "yl", "c"))
    every = LON + LAT
    return jax.shard_map(
        shards,
        mesh=fine,
        in_specs=(P(LAT, LON, None), P(LAT, LON, None), P(LAT, LON)) + (P(),) * 7,
        out_specs=(P(LAT, LON, None), P(every, None), P(every, None)) + (P(),) * 5,
        check_vma=False,
    )
```

```python
import functools

import jax
import jax.numpy as jnp
import numpy as np
from jax import lax
from jax.experimental import pallas as pl
from jax.experimental.pallas import tpu as pltpu
from jax.sharding import Mesh
from jax.sharding import PartitionSpec as P

HEADS = 12
HEAD_DIM = 64
WIN_H = 6
WIN_W = 12
SHIFT_H = 3
SHIFT_W = 6
WIN = 72
C = 1536
HC = 768
HALF = 384
CELLS = 288
WINDOWS = 4
COSINE_EPS = 1e-06
NORM_EPS = 1e-05

F32 = jnp.float32
BF16 = jnp.bfloat16
LON = ("yh", "x", "z")
LAT = ("yl", "c")
Y = ("yh", "yl")
ORDERS = (("x", "y", "z"), ("y", "z", "x"), ("z", "x", "y"))
AXES = {"x": ("x",), "y": Y, "z": ("z",)}
BLOCK = (24, 512)
EXTRA = 2
NT = (((1,), (1,)), ((), ()))
TN = (((0,), (0,)), ((), ()))
NN = (((1,), (0,)), ((), ()))
VMEM = pl.BlockSpec(memory_space=pltpu.VMEM)
HBM = pl.BlockSpec(memory_space=pltpu.HBM)
ANY = pl.BlockSpec(memory_space=pl.ANY)
SMEM = pl.BlockSpec(memory_space=pltpu.SMEM)


def dot(left, right, dims=NN):
    return lax.dot_general(left, right, dims, preferred_element_type=F32)


def cost(outs, operands, flops):
    moved = sum(int(np.prod(o.shape)) * o.dtype.itemsize for o in (*outs, *operands))
    return pl.CostEstimate(flops=flops, bytes_accessed=moved, transcendentals=0)


def call(body, outs, operands, scalars=1, scratch=(), flops=0, vmem=50, far=(), near=(), name=None):
    specs = [SMEM] * scalars + [VMEM] * (len(operands) - scalars)
    for i in far:
        specs[i] = HBM
    for i in near:
        specs[i] = ANY
    return pl.pallas_call(
        body,
        out_shape=list(outs),
        in_specs=specs,
        out_specs=[VMEM] * len(outs),
        scratch_shapes=list(scratch),
        compiler_params=pltpu.CompilerParams(vmem_limit_bytes=vmem * 2**20),
        cost_estimate=cost(outs, operands, flops),
        name=name,
    )(*operands)


def grid_call(body, grid, scalars, ins, outs, scratch=(), flops=0, vmem=50, name=None):
    operands = [array for array, _, _ in ins]
    results = [result for result, _, _ in outs]
    spec = pltpu.PrefetchScalarGridSpec(
        num_scalar_prefetch=len(scalars),
        grid=grid,
        in_specs=[pl.BlockSpec(block, at) for _, block, at in ins],
        out_specs=[pl.BlockSpec(block, at) for _, block, at in outs],
        scratch_shapes=list(scratch),
    )
    return pl.pallas_call(
        body,
        grid_spec=spec,
        out_shape=results,
        compiler_params=pltpu.CompilerParams(vmem_limit_bytes=vmem * 2**20),
        cost_estimate=cost(results, operands, flops),
        name=name,
    )(*scalars, *operands)


def shape(dims, dtype):
    return jax.ShapeDtypeStruct(dims, dtype)


def head_sum(value):
    rows = lax.broadcasted_iota(jnp.int32, (128, 128), 0) // HEAD_DIM
    cols = lax.broadcasted_iota(jnp.int32, (128, 128), 1) // HEAD_DIM
    ones = (rows == cols).astype(F32).astype(BF16)
    high = value.astype(BF16)
    low = (value - high.astype(F32)).astype(BF16)
    return dot(high, ones) + dot(low, ones)


def low_half(rows):
    return lax.broadcasted_iota(jnp.int32, (rows, 128), 1) < HEAD_DIM


def stacked(value):
    mask = low_half(WIN)
    return jnp.concatenate([jnp.where(mask, value, 0.0), jnp.where(mask, 0.0, value)], 0).astype(BF16)


def unstacked(value):
    return jnp.where(low_half(WIN), value[:WIN], value[WIN:])


def normalized(rows):
    inv = lax.rsqrt(head_sum(rows * rows) + COSINE_EPS)
    return rows * inv, inv


def penalties(region_row, region_col):
    out = []
    for w in range(WINDOWS):
        same = region_row[w : w + 1, :] == region_col[w * WIN : (w + 1) * WIN, :]
        one = jnp.where(same, 0.0, -100.0).astype(F32)
        out.append(jnp.concatenate([one, one], 0))
    return out


def two_heads(scale_ref, head):
    top = lax.broadcasted_iota(jnp.int32, (2 * WIN, 1), 0) < WIN
    return jnp.exp(jnp.where(top, scale_ref[head], scale_ref[head + 1]))


def softmax_of(scores):
    exp_scores = [jnp.exp(one) for one in scores]
    sums = [jnp.sum(one, -1, keepdims=True) for one in exp_scores]
    return [one / total for one, total in zip(exp_scores, sums)]


SPANS = [slice(n * WIN, (n + 1) * WIN) for n in range(WINDOWS)]


HALF_ROWS = 12


def f32_rows(ref, start, count):
    return ref[...].astype(F32)[start : start + count]


def window_rows(own, east, west, low, grid, rows):
    for j in range(12):
        i = j % SHIFT_W
        if j < SHIFT_W:
            upper = own[SHIFT_W + i].astype(F32)[SHIFT_H : SHIFT_H + HALF_ROWS]
            lower = [f32_rows(west, i * HALF_ROWS, HALF_ROWS)]
        else:
            upper = f32_rows(east, i * HALF_ROWS, HALF_ROWS)
            lower = [own[i].astype(F32)[SHIFT_H + HALF_ROWS :], f32_rows(low, i * SHIFT_H, SHIFT_H)]
        column = jnp.concatenate([upper] + lower, 0)
        for t in range(12):
            grid[t, j * 24 : (j + 1) * 24, :] = column[:, t * 128 : (t + 1) * 128]
    for r in range(24):
        for t in range(12):
            rows[r * 12 : (r + 1) * 12, t * 128 : (t + 1) * 128] = grid[t, pl.ds(r, 12, stride=24), :]


def first_body(own, low, upper, lower):
    low[...] = jnp.concatenate([own[j].astype(F32)[:SHIFT_H] for j in range(12)], 0).astype(BF16)
    upper[...] = jnp.concatenate(
        [own[j].astype(F32)[SHIFT_H : SHIFT_H + HALF_ROWS] for j in range(SHIFT_W)], 0
    ).astype(BF16)
    lower[...] = jnp.concatenate(
        [own[SHIFT_W + i].astype(F32)[SHIFT_H + HALF_ROWS :] for i in range(SHIFT_W)], 0
    ).astype(BF16)


def to_east_body(lower, low, out):
    count = HALF_ROWS - SHIFT_H
    out[...] = jnp.concatenate(
        [
            piece
            for i in range(SHIFT_W)
            for piece in (
                f32_rows(lower, i * count, count),
                f32_rows(low, (SHIFT_W + i) * SHIFT_H, SHIFT_H),
            )
        ],
        0,
    ).astype(BF16)


def forward_body(
    scale, own, east, west, low, w, query_bias, value_bias, pair_bias, row, col, x, projected, attended, grid, rows, wide, sems
):
    copies = []
    for g in range(3):
        for j in range(3):
            at = pl.ds(j * HC + g * 256, 256)
            copies.append(pltpu.make_async_copy(w.at[:, at], wide.at[:, at], sems.at[3 * g + j]))
            copies[-1].start()
    window_rows(own, east, west, low, grid, rows)
    x[...] = rows[...].astype(BF16)
    pens = penalties(row[...], col[...])
    for g in range(3):
        for j in range(3):
            lo = j * HC + g * 256
            copies[3 * g + j].wait()
            product = dot(x[...], wide[:, lo : lo + 256])
            if j != 1:
                product = product + (query_bias, None, value_bias)[j][g * 256 : (g + 1) * 256].reshape(1, 256)
            projected[:, lo : lo + 256] = product
        for half in range(2):
            lo = g * 256 + half * 128
            head = lo // HEAD_DIM
            factor = two_heads(scale, head)
            q = normalized(projected[:, lo : lo + 128])[0]
            k = normalized(projected[:, HC + lo : HC + lo + 128])[0]
            v = projected[:, 2 * HC + lo : 2 * HC + lo + 128]
            pb = pair_bias[head * WIN : (head + 2) * WIN, :]
            cosines = [dot(stacked(q[at]), k[at].astype(BF16), NT) for at in SPANS]
            attention = softmax_of([c * factor + pb + pen for c, pen in zip(cosines, pens)])
            outs = [dot(a.astype(BF16), v[at].astype(BF16)) for a, at in zip(attention, SPANS)]
            attended[:, lo : lo + 128] = jnp.concatenate([unstacked(o) for o in outs], 0).astype(BF16)


def norm_part(attended, rows, pw, gain, mixed_low, attended_grad, gain_part, mixed_all):
    for n in range(6):
        at = slice(n * 256, (n + 1) * 256)
        mixed_all[:, at] = dot(attended[...], pw[at, :], NT)
    total = jnp.zeros((1, C), F32)
    for r in range(6):
        at = slice(r * 48, (r + 1) * 48)
        mixed = mixed_all[at, :]
        center = mixed - jnp.mean(mixed, -1, keepdims=True)
        inv_std = lax.rsqrt(jnp.mean(center * center, -1, keepdims=True) + NORM_EPS)
        normed = center * inv_std
        up = rows[at, :]
        total = total + jnp.sum(up * normed, 0, keepdims=True)
        scaled = up * gain[...].reshape(1, C)
        grad = inv_std * (
            scaled
            - jnp.mean(scaled, -1, keepdims=True)
            - normed * jnp.mean(scaled * normed, -1, keepdims=True)
        )
        mixed_low[at, :] = grad.astype(BF16)
    gain_part[...] = total
    for n in range(3):
        at = slice(n * 256, (n + 1) * 256)
        attended_grad[:, at] = dot(mixed_low[...], pw[:, at]).astype(BF16).astype(F32)


def attention_pair(scale, head, q, k, v, da, pb, pens, gains):
    factor = two_heads(scale, head)
    q, q_inv = normalized(q)
    k, k_inv = normalized(k)
    qs = [stacked(q[at]) for at in SPANS]
    das = [stacked(da[at]) for at in SPANS]
    kb = [k[at].astype(BF16) for at in SPANS]
    vb = [v[at].astype(BF16) for at in SPANS]
    cosines = [dot(a, b, NT) for a, b in zip(qs, kb)]
    prob_grads = [dot(a, b, NT) for a, b in zip(das, vb)]
    attention = softmax_of([c * factor + pb + pen for c, pen in zip(cosines, pens)])
    v_grad = jnp.concatenate([dot(a.astype(BF16), b, TN) for a, b in zip(attention, das)], 0)
    means = [jnp.sum(a * p, -1, keepdims=True) for a, p in zip(attention, prob_grads)]
    score_grads = [a * (p - m) for a, p, m in zip(attention, prob_grads, means)]
    cosine_grads = [(s * factor).astype(BF16) for s in score_grads]
    gq = jnp.concatenate([unstacked(dot(c, b)) for c, b in zip(cosine_grads, kb)], 0)
    gk = jnp.concatenate([dot(c, b, TN) for c, b in zip(cosine_grads, qs)], 0)
    pair = (score_grads[0] + score_grads[1]) + (score_grads[2] + score_grads[3])
    scaled = sum(s * c for s, c in zip(score_grads, cosines))
    lane = lax.broadcasted_iota(jnp.int32, (1, 128), 1)
    scale_line = jnp.zeros((1, 128), F32)
    for i in range(2):
        one = jnp.sum(jnp.sum(scaled[i * WIN : (i + 1) * WIN], 0, keepdims=True), 1, keepdims=True)
        scale_line = scale_line + jnp.where(lane == head + i, one * factor[i * WIN : i * WIN + 1], 0.0)
    q_grad = q_inv * (gq - q * head_sum(q * gq))
    k_grad = k_inv * (gk - k * head_sum(k * gk))
    lines = jnp.concatenate(
        [
            jnp.sum(q_grad, 0, keepdims=True),
            jnp.sum(v_grad, 0, keepdims=True),
            scale_line,
            gains[:, :128],
            gains[:, 128:],
            jnp.zeros((11, 128), F32),
        ],
        0,
    )
    return (q_grad, k_grad, v_grad), pair, lines


def store_pair(grads, small, at, parts, pair, lines):
    for i, part in enumerate(parts):
        grads[:, at * HALF + i * 128 : at * HALF + (i + 1) * 128] = part.astype(BF16)
    rows = slice(at * 48, (at + 1) * 48)
    for g in range(3):
        small[rows, g * 128 : g * 128 + WIN] = pair[g * 48 : (g + 1) * 48]
    small[at * 48 : at * 48 + 16, 384:] = lines


def attention_body(
    side, scale, q_ref, k_ref, v_ref, da_ref, pair_bias, row, col, gain_part, grads, small
):
    pens = penalties(row[...], col[...])
    head = side[0] * 6 + 2 * pl.program_id(0)
    small[...] = jnp.zeros_like(small)
    store_pair(
        grads,
        small,
        0,
        *attention_pair(
            scale, head, q_ref[...], k_ref[...], v_ref[...], da_ref[...], pair_bias[...], pens, gain_part[...]
        ),
    )


def backward_body(
    side,
    scale,
    attended,
    own,
    east,
    west,
    low,
    pw,
    gain,
    projected,
    pair_bias,
    row,
    col,
    mixed_low,
    grad_other,
    gain_part,
    grads,
    small,
    attended_near,
    attended_far,
    grid,
    rows,
    mixed_all,
    weight,
    heads,
    attended_grad,
    sems,
):
    copies = [pltpu.make_async_copy(pw, weight, sems.at[0])]
    for j in range(3):
        at = pl.ds(pl.multiple_of(j * HC + side[0] * HALF, 128), HALF)
        copies.append(pltpu.make_async_copy(projected.at[:, at], heads.at[j], sems.at[1 + j]))
    for copy in copies:
        copy.start()
    window_rows(own, east, west, low, grid, rows)
    copies[0].wait()
    norm_part(attended, rows, weight, gain, mixed_low, attended_grad, gain_part, mixed_all)
    pens = penalties(row[...], col[...])
    near = pl.ds(pl.multiple_of((1 - side[0]) * HALF, 128), HALF)
    far = pl.ds(pl.multiple_of(side[0] * HALF, 128), HALF)
    grad_other[...] = attended_grad[:, near]
    attended_near[...] = attended[:, near]
    attended_far[...] = attended[:, far]
    small[...] = jnp.zeros_like(small)
    for copy in copies[1:]:
        copy.wait()
    for hp in range(3):
        cols = slice(hp * 128, (hp + 1) * 128)
        head = side[0] * 6 + 2 * hp
        gains = gain_part[:, pl.ds(pl.multiple_of(side[0] * HC + hp * 256, 128), 256)]
        store_pair(
            grads,
            small,
            hp,
            *attention_pair(
                scale,
                head,
                heads[0, :, cols],
                heads[1, :, cols],
                heads[2, :, cols],
                attended_grad[:, pl.ds(pl.multiple_of(side[0] * HALF + hp * 128, 128), 128)],
                pair_bias[pl.ds(pl.multiple_of(head * WIN, 8), 2 * WIN), :],
                pens,
                gains,
            ),
        )


def write_coded(value, lines, outs, base):
    high = lines.astype(BF16)
    low = (lines - high.astype(F32)).astype(BF16)
    for i, tail in enumerate((high, low)):
        block = jnp.concatenate([value[i][:, :384].astype(BF16), tail], 1)
        for out in outs:
            out[base + i] = block


def add_coded(keep, recv, outs, source, base):
    value = [keep[source + i].astype(F32) + recv[source + i].astype(F32) for i in range(EXTRA)]
    write_coded(value, value[0][:, 384:] + value[1][:, 384:], outs, base)


def row_of(place):
    y = place["y"]
    return 24 * ((y // 2) * 32 + place["x"] * 8 + place["z"] * 2 + y % 2)


def first_order(core, at):
    end, left = (at == 0) | (at == 3), at < 2
    zero = [jnp.where(end, a, b) for a, b in ((0, 1), (3, 2), (1, 0), (2, 3))]
    one = [jnp.where(left, a, b) for a, b in ((0, 2), (1, 3), (2, 0), (3, 1))]
    return [jnp.where(core == 0, a, b) for a, b in zip(zero, one)]


def second_order(core, at):
    kept = jnp.where(core == 0, at // 2, at % 2)
    return [kept, 1 - kept]


def order_of(place, j, axis, second):
    at = place[1 + "xyz".index(ORDERS[j][axis])]
    return (second_order if second else first_order)(place[0], at)


def weight_body(place, x0, x1, p0, p1, m0, m1, a0, a1, s0, s1, *rest):
    outs, (left, grads, mixed, heads, total, sems) = rest[:6], rest[6:]
    pairs = ((x0, x1, left), (p0, p1, grads), (m0, m1, mixed), (a0, a1, heads))
    copies = []
    for i, (own, other, joined) in enumerate(pairs):
        for k, source in enumerate((own, other)):
            copies.append(
                pltpu.make_async_copy(source, joined.at[k * CELLS : (k + 1) * CELLS], sems.at[2 * i + k])
            )
            copies[-1].start()
    for copy in copies[:4]:
        copy.wait()
    for m in range(4):
        at = slice(m * 384, (m + 1) * 384)
        part = dot(left[:, at], grads[...], TN)
        for j in range(3):
            total[at, j * 512 : j * 512 + HALF] = part[:, j * HALF : (j + 1) * HALF]
    for copy in copies[4:]:
        copy.wait()
    for m in range(4):
        at = slice(m * 384, (m + 1) * 384)
        part = dot(mixed[:, at], heads[...], TN)
        for j in range(3):
            total[at, j * 512 + HALF : (j + 1) * 512] = part[:, j * 128 : (j + 1) * 128]
    for j in range(3):
        cols = slice(j * 512, (j + 1) * 512)
        order = order_of(place, j, 0, False)
        for i in range(4):
            out = outs[2 * j + i // 2]
            for second in range(4):
                for third in range(4):
                    places = (order[i], second, third)
                    start = row_of(dict(zip(ORDERS[j], places)))
                    rows = pl.ds(pl.multiple_of(start, 8), 24)
                    out[i % 2 * 16 + second * 4 + third] = total[rows, cols].astype(BF16)
        at = slice(j * 48, (j + 1) * 48)
        value = s0[at, :] + s1[at, :]
        write_coded([value[:24], value[24:]], value[:24, 384:], outs[2 * j : 2 * j + 2], 32)


def halve_body(count, size, axis, place, *refs):
    ins, outs = refs[:6], refs[6:]
    for j in range(3):
        keep, recv = ins[2 * j : 2 * j + 2]
        order = order_of(place, j, axis, count == 1)
        for i in range(2 * count):
            out = outs[2 * j + i // count]
            for b in range(size):
                at = order[i] * size + b
                out[i % count * size + b] = (keep[at].astype(F32) + recv[at].astype(F32)).astype(BF16)
        add_coded(keep, recv, outs[2 * j : 2 * j + 2], 2 * count * size, count * size)


def total_body(*refs):
    ins, out = refs[:6], refs[6]
    for j in range(3):
        keep, recv = ins[2 * j : 2 * j + 2]
        out[3 * j] = (keep[0].astype(F32) + recv[0].astype(F32)).astype(BF16)
        add_coded(keep, recv, [out], 1, 3 * j + 1)


def finish_body(core, own, other, qkv, proj, pair, gain, qb, vb, scale):
    which = core[0]
    scales = jnp.zeros((128,), F32)
    for side in range(2):
        for j in range(3):
            def block(i):
                return jnp.where(which == side, own[3 * j + i].astype(F32), other[3 * j + i].astype(F32))

            rows = block(0)
            rows = jnp.where(which == 0, rows[:12], rows[12:])
            at = side * HALF + j * 128
            for t in range(3):
                qkv[:, t * HC + at : t * HC + at + 128] = rows[:, t * 128 : (t + 1) * 128]
            proj[:, at : at + 128] = rows[:, HALF:]
            top, bottom = block(1), block(2)
            for g in range(3):
                start = (side * 3 + j) * 144 + g * 48
                pair[start : start + 24, :] = top[:, g * 128 : g * 128 + WIN]
                pair[start + 24 : start + 48, :] = bottom[:, g * 128 : g * 128 + WIN]
            lines = top[:, 384:] + bottom[:, 384:]
            qb[at : at + 128] = lines[0]
            vb[at : at + 128] = lines[1]
            scales = scales + lines[2]
            gain[side * HC + j * 256 : side * HC + j * 256 + 128] = lines[3]
            gain[side * HC + j * 256 + 128 : side * HC + j * 256 + 256] = lines[4]
    scale[...] = scales[:HEADS]


def branch_body(side, w, own, theirs, to_east, to_west, stay_low, stay_high, grads, rows):
    which = side[0]

    @pl.when(pl.program_id(0) == 0)
    def _():
        for pair in range(3):
            for j in range(3):
                at = j * HC + pair * 128
                cols = slice(pair * HALF + j * 128, pair * HALF + (j + 1) * 128)
                grads[:, pl.ds(pl.multiple_of(at + which * HALF, 128), 128)] = own[:, cols]
                grads[:, pl.ds(pl.multiple_of(at + (1 - which) * HALF, 128), 128)] = theirs[:, cols]

    product = dot(grads[...], w[...], NT)
    for i in range(2):
        rows[i] = product[:, i * 128 : (i + 1) * 128]
    columns = [
        jnp.concatenate([rows[i, pl.ds(j, 24, stride=12), :] for i in range(2)], 1) for j in range(12)
    ]
    for out, cols, start in (
        (stay_low, columns[:SHIFT_W], 0),
        (to_east, columns[SHIFT_W:], 0),
        (to_west, columns[:SHIFT_W], HALF_ROWS),
        (stay_high, columns[SHIFT_W:], HALF_ROWS),
    ):
        out[...] = jnp.concatenate([one[start : start + HALF_ROWS] for one in cols], 0).astype(BF16)


def last_rows_body(stay_high, from_east, out):
    start = HALF_ROWS - SHIFT_H
    out[...] = jnp.concatenate(
        [
            f32_rows(half, i * HALF_ROWS + start, SHIFT_H)
            for half in (stay_high, from_east)
            for i in range(SHIFT_W)
        ],
        0,
    ).astype(BF16)


def merge_body(upstream, stay_low, stay_high, from_west, from_east, low, out):
    for j in range(12):
        i = j % SHIFT_W
        upper, lower = (from_west, stay_high) if j < SHIFT_W else (stay_low, from_east)
        back = jnp.concatenate(
            [
                f32_rows(low, j * SHIFT_H, SHIFT_H),
                f32_rows(upper, i * HALF_ROWS, HALF_ROWS),
                f32_rows(lower, i * HALF_ROWS, HALF_ROWS - SHIFT_H),
            ],
            0,
        )
        out[j] = (upstream[j].astype(F32) + back).astype(BF16)


def permuted(value, axes, target):
    sizes = [lax.axis_size(a) for a in axes]
    pairs = []
    for source in range(int(np.prod(sizes))):
        place = np.unravel_index(source, sizes)
        to = target(*[int(v) for v in place])
        pairs.append((source, int(np.ravel_multi_index(to, sizes))))
    return lax.ppermute(value, axes, pairs)


def lon_step(value, steps):
    return permuted(value, LON, lambda *at: np.unravel_index((np.ravel_multi_index(at, (2, 4, 4)) + steps) % 32, (2, 4, 4)))


def lat_step(value, steps):
    return permuted(value, LAT, lambda *at: np.unravel_index((np.ravel_multi_index(at, (2, 2)) + steps) % 4, (2, 2)))


def core_swap(value):
    return permuted(value, ("c",), lambda c: (1 - c,))


def ring_swap(value, axis, step):
    def partner(place, c):
        return place ^ 1 if (step == 0) == (c == 0) else 3 - place

    if axis == "y":
        def target(yh, yl, c):
            to = partner(yh * 2 + yl, c)
            return (to // 2, to % 2, c)
    else:
        def target(place, c):
            return (partner(place, c), c)

    return permuted(value, AXES[axis] + ("c",), target)


def first_messages(grid):
    return call(
        first_body,
        [shape((36, C), BF16), shape((72, C), BF16), shape((54, C), BF16)],
        [grid],
        scalars=0,
        name="first",
    )


def halo(low, upper, lower):
    low = lat_step(low, -1)
    east = lon_step(upper, -1)
    (lower,) = call(to_east_body, [shape((72, C), BF16)], [lower, low], scalars=0, name="to_east")
    return east, low, lower


def shards(
    features,
    upstream,
    region_ids,
    qkv_weight,
    query_bias,
    value_bias,
    logit_scale,
    pair_bias,
    proj_weight,
    norm_gain,
):
    core = lax.axis_index("c")
    place = jnp.stack(
        [core, lax.axis_index("x"), lax.axis_index("yh") * 2 + lax.axis_index("yl"), lax.axis_index("z")]
    ).astype(jnp.int32)
    mine = core.astype(jnp.int32).reshape(1)
    theirs = 1 - mine
    scale = logit_scale
    pair_rows = pair_bias.reshape(HEADS * WIN, WIN)
    gain = norm_gain

    features = features.transpose(1, 0, 2)
    upstream = upstream.transpose(1, 0, 2)
    late = first_messages(upstream)
    east, low, lower = halo(*first_messages(features))
    late, region_ids, lower = lax.optimization_barrier((late, region_ids, lower))
    came = east, lon_step(lower, 1), low
    lower_ids = lon_step(region_ids[HALF_ROWS:], 1)
    region_ids = jnp.concatenate([region_ids[:HALF_ROWS], lower_ids], 0)
    region_row = region_ids.reshape(WINDOWS, WIN)
    region_col = region_ids.reshape(-1, 1)
    east, low, lower = halo(*late)
    came_late = east, lon_step(lower, 1), low
    x, projected, attended = call(
        forward_body,
        [shape((CELLS, C), BF16), shape((CELLS, 3 * HC), F32), shape((CELLS, HC), BF16)],
        [scale, features, *came, qkv_weight, query_bias, value_bias, pair_rows, region_row, region_col],
        scratch=[
            pltpu.VMEM((12, CELLS, 128), F32),
            pltpu.VMEM((CELLS, C), F32),
            pltpu.VMEM((C, 3 * HC), BF16),
            pltpu.SemaphoreType.DMA((9,)),
        ],
        flops=2 * CELLS * C * 3 * HC,
        far=(5,),
        vmem=60,
        name="forward",
    )
    x_other = core_swap(x)
    mixed_low, grad_mine, gain_part, grads_theirs, small_theirs, attended_mine, attended_theirs = call(
        backward_body,
        [
            shape((CELLS, C), BF16),
            shape((CELLS, HALF), F32),
            shape((1, C), F32),
            shape((CELLS, 3 * HALF), BF16),
            shape((144, 512), F32),
            shape((CELLS, HALF), BF16),
            shape((CELLS, HALF), BF16),
        ],
        [
            theirs,
            scale,
            attended,
            upstream,
            *came_late,
            proj_weight,
            gain,
            projected,
            pair_rows,
            region_row,
            region_col,
        ],
        scalars=2,
        scratch=[
            pltpu.VMEM((12, CELLS, 128), F32),
            pltpu.VMEM((CELLS, C), F32),
            pltpu.VMEM((CELLS, C), F32),
            pltpu.VMEM((C, HC), BF16),
            pltpu.VMEM((3, CELLS, HALF), F32),
            pltpu.VMEM((CELLS, HC), F32),
            pltpu.SemaphoreType.DMA((4,)),
        ],
        far=(7,),
        near=(9,),
        flops=4 * CELLS * C * HC + 2 * CELLS * WIN * 128 * 18,
        vmem=60,
        name="backward",
    )
    mixed_other = core_swap(mixed_low)
    attended_other = core_swap(attended_theirs)

    grads_other = core_swap(grads_theirs)
    small_other = core_swap(small_theirs)
    def attention(side):
        def cols(base):
            return lambda i, side, scale: (0, base + side[0] * 3 + i)

        whole = lambda i, side, scale: (0, 0)
        block = (CELLS, 128)
        return grid_call(
            attention_body,
            (3,),
            [side, scale],
            [
                (projected, block, cols(0)),
                (projected, block, cols(6)),
                (projected, block, cols(12)),
                (grad_mine, block, lambda i, side, scale: (0, i)),
                (pair_rows, (2 * WIN, WIN), lambda i, side, scale: (side[0] * 3 + i, 0)),
                (region_row, (WINDOWS, WIN), whole),
                (region_col, (CELLS, 1), whole),
                (gain_part, (1, 256), cols(0)),
            ],
            [
                (shape((CELLS, 3 * HALF), BF16), (CELLS, HALF), lambda i, side, scale: (0, i)),
                (shape((144, 512), F32), (48, 512), lambda i, side, scale: (i, 0)),
            ],
            flops=2 * CELLS * WIN * 128 * 6 * 3,
            vmem=16,
            name="attention",
        )

    grads_mine, small_mine = attention(mine)

    parts = call(
        weight_body,
        [shape((32 + EXTRA,) + BLOCK, BF16)] * 6,
        [
            place,
            x,
            x_other,
            grads_mine,
            grads_other,
            mixed_low,
            mixed_other,
            attended_mine,
            attended_other,
            small_mine,
            small_other,
        ],
        scratch=[
            pltpu.VMEM((2 * CELLS, C), BF16),
            pltpu.VMEM((2 * CELLS, 3 * HALF), BF16),
            pltpu.VMEM((2 * CELLS, C), BF16),
            pltpu.VMEM((2 * CELLS, HALF), BF16),
            pltpu.VMEM((C, C), F32),
            pltpu.SemaphoreType.DMA((8,)),
        ],
        near=tuple(range(1, 9)),
        flops=4 * CELLS * C * C,
        vmem=26,
        name="weights",
    )
    side, parts = lax.optimization_barrier((mine, parts))
    order = place
    whole = lambda i, side: (0, 0)
    to_east, to_west, stay_low, stay_high = grid_call(
        branch_body,
        (6,),
        [side],
        [
            (qkv_weight, (256, 3 * HC), lambda i, side: (i, 0)),
            (grads_mine, (CELLS, 3 * HALF), whole),
            (grads_theirs, (CELLS, 3 * HALF), whole),
        ],
        [(shape((72, C), BF16), (72, 256), lambda i, side: (0, i))] * 4,
        scratch=[pltpu.VMEM((CELLS, 3 * HC), BF16), pltpu.VMEM((2, CELLS, 128), F32)],
        flops=2 * CELLS * C * 3 * HC,
        vmem=16,
        name="branch",
    )
    from_west = lon_step(to_east, 1)
    from_east = lon_step(to_west, -1)
    (last,) = call(
        last_rows_body, [shape((36, C), BF16)], [stay_high, from_east], scalars=0, vmem=6, name="last_rows"
    )
    low = lat_step(last, 1)
    for step in range(6):
        terms = []
        for j, names in enumerate(ORDERS):
            terms += [parts[2 * j], ring_swap(parts[2 * j + 1], names[step // 2], step % 2)]
        if step == 5:
            break
        left = 32 >> step
        if step % 2 == 0:
            body = functools.partial(halve_body, 1, left // 2, step // 2)
        else:
            body = functools.partial(halve_body, 2, left // 4, step // 2 + 1)
        if step == 0:
            order, stay_low = lax.optimization_barrier((order, stay_low))
        if step == 3:
            order, last = lax.optimization_barrier((order, last))
        parts = call(body, [shape((left // 2 + EXTRA,) + BLOCK, BF16)] * 6, [order, *terms], vmem=10, name="halve")
    (input_grad,) = call(
        merge_body,
        [shape((12, 24, C), BF16)],
        [upstream, stay_low, stay_high, from_west, from_east, low],
        scalars=0,
        vmem=10,
        name="merge",
    )
    terms, input_grad = lax.optimization_barrier((terms, input_grad))
    (sums,) = call(total_body, [shape((9,) + BLOCK, BF16)], terms, scalars=0, vmem=6, name="total")
    sums_other = core_swap(sums)
    qkv_weight_grad, proj_weight_grad, pair_grad, gain_grad, query_bias_grad, value_bias_grad, scale_grad = call(
        finish_body,
        [
            shape((12, 3 * HC), F32),
            shape((12, HC), F32),
            shape((HEADS * WIN, WIN), F32),
            shape((C,), F32),
            shape((HC,), F32),
            shape((HC,), F32),
            shape((HEADS,), F32),
        ],
        [mine, sums, sums_other],
        vmem=8,
        name="finish",
    )
    pair_grad = pair_grad.reshape(HEADS, WIN, WIN)

    return (
        input_grad.transpose(1, 0, 2),
        qkv_weight_grad,
        proj_weight_grad,
        gain_grad,
        query_bias_grad,
        value_bias_grad,
        scale_grad,
        pair_grad,
    )


def solution(mesh):
    fine = Mesh(mesh.devices.reshape(2, 4, 4, 2, 2), ("yh", "x", "z", "yl", "c"))
    every = LON + LAT
    return jax.shard_map(
        shards,
        mesh=fine,
        in_specs=(P(LAT, LON, None), P(LAT, LON, None), P(LAT, LON)) + (P(),) * 7,
        out_specs=(P(LAT, LON, None), P(every, None), P(every, None)) + (P(),) * 5,
        check_vma=False,
    )
```

```python
import functools

import jax
import jax.numpy as jnp
import numpy as np
from jax import lax
from jax.experimental import pallas as pl
from jax.experimental.pallas import tpu as pltpu
from jax.sharding import Mesh
from jax.sharding import PartitionSpec as P

HEADS = 12
HEAD_DIM = 64
WIN_H = 6
WIN_W = 12
SHIFT_H = 3
SHIFT_W = 6
WIN = 72
C = 1536
HC = 768
HALF = 384
CELLS = 288
WINDOWS = 4
COSINE_EPS = 1e-06
NORM_EPS = 1e-05

F32 = jnp.float32
BF16 = jnp.bfloat16
LON = ("yh", "x", "z")
LAT = ("yl", "c")
Y = ("yh", "yl")
ORDERS = (("x", "y", "z"), ("y", "z", "x"), ("z", "x", "y"))
AXES = {"x": ("x",), "y": Y, "z": ("z",)}
BLOCK = (24, 512)
EXTRA = 2
NT = (((1,), (1,)), ((), ()))
TN = (((0,), (0,)), ((), ()))
NN = (((1,), (0,)), ((), ()))
VMEM = pl.BlockSpec(memory_space=pltpu.VMEM)
HBM = pl.BlockSpec(memory_space=pltpu.HBM)
ANY = pl.BlockSpec(memory_space=pl.ANY)
SMEM = pl.BlockSpec(memory_space=pltpu.SMEM)


def dot(left, right, dims=NN):
    return lax.dot_general(left, right, dims, preferred_element_type=F32)


def cost(outs, operands, flops):
    moved = sum(int(np.prod(o.shape)) * o.dtype.itemsize for o in (*outs, *operands))
    return pl.CostEstimate(flops=flops, bytes_accessed=moved, transcendentals=0)


def call(body, outs, operands, scalars=1, scratch=(), flops=0, vmem=50, far=(), near=(), name=None):
    specs = [SMEM] * scalars + [VMEM] * (len(operands) - scalars)
    for i in far:
        specs[i] = HBM
    for i in near:
        specs[i] = ANY
    return pl.pallas_call(
        body,
        out_shape=list(outs),
        in_specs=specs,
        out_specs=[VMEM] * len(outs),
        scratch_shapes=list(scratch),
        compiler_params=pltpu.CompilerParams(vmem_limit_bytes=vmem * 2**20),
        cost_estimate=cost(outs, operands, flops),
        name=name,
    )(*operands)


def grid_call(body, grid, scalars, ins, outs, scratch=(), flops=0, vmem=50, name=None):
    operands = [array for array, _, _ in ins]
    results = [result for result, _, _ in outs]
    spec = pltpu.PrefetchScalarGridSpec(
        num_scalar_prefetch=len(scalars),
        grid=grid,
        in_specs=[pl.BlockSpec(block, at) for _, block, at in ins],
        out_specs=[pl.BlockSpec(block, at) for _, block, at in outs],
        scratch_shapes=list(scratch),
    )
    return pl.pallas_call(
        body,
        grid_spec=spec,
        out_shape=results,
        compiler_params=pltpu.CompilerParams(vmem_limit_bytes=vmem * 2**20),
        cost_estimate=cost(results, operands, flops),
        name=name,
    )(*scalars, *operands)


def shape(dims, dtype):
    return jax.ShapeDtypeStruct(dims, dtype)


def head_sum(value):
    rows = lax.broadcasted_iota(jnp.int32, (128, 128), 0) // HEAD_DIM
    cols = lax.broadcasted_iota(jnp.int32, (128, 128), 1) // HEAD_DIM
    ones = (rows == cols).astype(F32).astype(BF16)
    high = value.astype(BF16)
    low = (value - high.astype(F32)).astype(BF16)
    return dot(high, ones) + dot(low, ones)


def low_half(rows):
    return lax.broadcasted_iota(jnp.int32, (rows, 128), 1) < HEAD_DIM


def stacked(value):
    mask = low_half(WIN)
    return jnp.concatenate([jnp.where(mask, value, 0.0), jnp.where(mask, 0.0, value)], 0).astype(BF16)


def unstacked(value):
    return jnp.where(low_half(WIN), value[:WIN], value[WIN:])


def normalized(rows):
    inv = lax.rsqrt(head_sum(rows * rows) + COSINE_EPS)
    return rows * inv, inv


def penalties(region_row, region_col):
    out = []
    for w in range(WINDOWS):
        same = region_row[w : w + 1, :] == region_col[w * WIN : (w + 1) * WIN, :]
        one = jnp.where(same, 0.0, -100.0).astype(F32)
        out.append(jnp.concatenate([one, one], 0))
    return out


def two_heads(scale_ref, head):
    top = lax.broadcasted_iota(jnp.int32, (2 * WIN, 1), 0) < WIN
    return jnp.exp(jnp.where(top, scale_ref[head], scale_ref[head + 1]))


def softmax_of(scores):
    exp_scores = [jnp.exp(one) for one in scores]
    sums = [jnp.sum(one, -1, keepdims=True) for one in exp_scores]
    return [one / total for one, total in zip(exp_scores, sums)]


SPANS = [slice(n * WIN, (n + 1) * WIN) for n in range(WINDOWS)]


HALF_ROWS = 12


def f32_rows(ref, start, count):
    return ref[...].astype(F32)[start : start + count]


def window_rows(own, east, west, low, grid, rows):
    for j in range(12):
        i = j % SHIFT_W
        if j < SHIFT_W:
            upper = own[SHIFT_W + i].astype(F32)[SHIFT_H : SHIFT_H + HALF_ROWS]
            lower = [f32_rows(west, i * HALF_ROWS, HALF_ROWS)]
        else:
            upper = f32_rows(east, i * HALF_ROWS, HALF_ROWS)
            lower = [own[i].astype(F32)[SHIFT_H + HALF_ROWS :], f32_rows(low, i * SHIFT_H, SHIFT_H)]
        column = jnp.concatenate([upper] + lower, 0)
        for t in range(12):
            grid[t, j * 24 : (j + 1) * 24, :] = column[:, t * 128 : (t + 1) * 128]
    for r in range(24):
        for t in range(12):
            rows[r * 12 : (r + 1) * 12, t * 128 : (t + 1) * 128] = grid[t, pl.ds(r, 12, stride=24), :]


def first_body(own, low, upper, lower):
    low[...] = jnp.concatenate([own[j].astype(F32)[:SHIFT_H] for j in range(12)], 0).astype(BF16)
    upper[...] = jnp.concatenate(
        [own[j].astype(F32)[SHIFT_H : SHIFT_H + HALF_ROWS] for j in range(SHIFT_W)], 0
    ).astype(BF16)
    lower[...] = jnp.concatenate(
        [own[SHIFT_W + i].astype(F32)[SHIFT_H + HALF_ROWS :] for i in range(SHIFT_W)], 0
    ).astype(BF16)


def to_east_body(lower, low, out):
    count = HALF_ROWS - SHIFT_H
    out[...] = jnp.concatenate(
        [
            piece
            for i in range(SHIFT_W)
            for piece in (
                f32_rows(lower, i * count, count),
                f32_rows(low, (SHIFT_W + i) * SHIFT_H, SHIFT_H),
            )
        ],
        0,
    ).astype(BF16)


def forward_body(
    scale, own, east, west, low, w, query_bias, value_bias, pair_bias, row, col, x, projected, attended, grid, rows, wide, sems
):
    copies = []
    for g in range(3):
        for j in range(3):
            at = pl.ds(j * HC + g * 256, 256)
            copies.append(pltpu.make_async_copy(w.at[:, at], wide.at[:, at], sems.at[3 * g + j]))
            copies[-1].start()
    window_rows(own, east, west, low, grid, rows)
    x[...] = rows[...].astype(BF16)
    pens = penalties(row[...], col[...])
    for g in range(3):
        for j in range(3):
            lo = j * HC + g * 256
            copies[3 * g + j].wait()
            product = dot(x[...], wide[:, lo : lo + 256])
            if j != 1:
                product = product + (query_bias, None, value_bias)[j][g * 256 : (g + 1) * 256].reshape(1, 256)
            projected[:, lo : lo + 256] = product
        for half in range(2):
            lo = g * 256 + half * 128
            head = lo // HEAD_DIM
            factor = two_heads(scale, head)
            q = normalized(projected[:, lo : lo + 128])[0]
            k = normalized(projected[:, HC + lo : HC + lo + 128])[0]
            v = projected[:, 2 * HC + lo : 2 * HC + lo + 128]
            pb = pair_bias[head * WIN : (head + 2) * WIN, :]
            cosines = [dot(stacked(q[at]), k[at].astype(BF16), NT) for at in SPANS]
            attention = softmax_of([c * factor + pb + pen for c, pen in zip(cosines, pens)])
            outs = [dot(a.astype(BF16), v[at].astype(BF16)) for a, at in zip(attention, SPANS)]
            attended[:, lo : lo + 128] = jnp.concatenate([unstacked(o) for o in outs], 0).astype(BF16)


def norm_part(attended, rows, pw, gain, mixed_low, attended_grad, gain_part, mixed_all):
    for n in range(6):
        at = slice(n * 256, (n + 1) * 256)
        mixed_all[:, at] = dot(attended[...], pw[at, :], NT)
    total = jnp.zeros((1, C), F32)
    for r in range(6):
        at = slice(r * 48, (r + 1) * 48)
        mixed = mixed_all[at, :]
        center = mixed - jnp.mean(mixed, -1, keepdims=True)
        inv_std = lax.rsqrt(jnp.mean(center * center, -1, keepdims=True) + NORM_EPS)
        normed = center * inv_std
        up = rows[at, :]
        total = total + jnp.sum(up * normed, 0, keepdims=True)
        scaled = up * gain[...].reshape(1, C)
        grad = inv_std * (
            scaled
            - jnp.mean(scaled, -1, keepdims=True)
            - normed * jnp.mean(scaled * normed, -1, keepdims=True)
        )
        mixed_low[at, :] = grad.astype(BF16)
    gain_part[...] = total
    for n in range(3):
        at = slice(n * 256, (n + 1) * 256)
        attended_grad[:, at] = dot(mixed_low[...], pw[:, at]).astype(BF16).astype(F32)


def attention_pair(scale, head, q, k, v, da, pb, pens, gains):
    factor = two_heads(scale, head)
    q, q_inv = normalized(q)
    k, k_inv = normalized(k)
    qs = [stacked(q[at]) for at in SPANS]
    das = [stacked(da[at]) for at in SPANS]
    kb = [k[at].astype(BF16) for at in SPANS]
    vb = [v[at].astype(BF16) for at in SPANS]
    cosines = [dot(a, b, NT) for a, b in zip(qs, kb)]
    prob_grads = [dot(a, b, NT) for a, b in zip(das, vb)]
    attention = softmax_of([c * factor + pb + pen for c, pen in zip(cosines, pens)])
    v_grad = jnp.concatenate([dot(a.astype(BF16), b, TN) for a, b in zip(attention, das)], 0)
    means = [jnp.sum(a * p, -1, keepdims=True) for a, p in zip(attention, prob_grads)]
    score_grads = [a * (p - m) for a, p, m in zip(attention, prob_grads, means)]
    cosine_grads = [(s * factor).astype(BF16) for s in score_grads]
    gq = jnp.concatenate([unstacked(dot(c, b)) for c, b in zip(cosine_grads, kb)], 0)
    gk = jnp.concatenate([dot(c, b, TN) for c, b in zip(cosine_grads, qs)], 0)
    pair = (score_grads[0] + score_grads[1]) + (score_grads[2] + score_grads[3])
    scaled = sum(s * c for s, c in zip(score_grads, cosines))
    lane = lax.broadcasted_iota(jnp.int32, (1, 128), 1)
    scale_line = jnp.zeros((1, 128), F32)
    for i in range(2):
        one = jnp.sum(jnp.sum(scaled[i * WIN : (i + 1) * WIN], 0, keepdims=True), 1, keepdims=True)
        scale_line = scale_line + jnp.where(lane == head + i, one * factor[i * WIN : i * WIN + 1], 0.0)
    q_grad = q_inv * (gq - q * head_sum(q * gq))
    k_grad = k_inv * (gk - k * head_sum(k * gk))
    lines = jnp.concatenate(
        [
            jnp.sum(q_grad, 0, keepdims=True),
            jnp.sum(v_grad, 0, keepdims=True),
            scale_line,
            gains[:, :128],
            gains[:, 128:],
            jnp.zeros((11, 128), F32),
        ],
        0,
    )
    return (q_grad, k_grad, v_grad), pair, lines


def store_pair(grads, small, at, parts, pair, lines):
    for i, part in enumerate(parts):
        grads[:, at * HALF + i * 128 : at * HALF + (i + 1) * 128] = part.astype(BF16)
    rows = slice(at * 48, (at + 1) * 48)
    for g in range(3):
        small[rows, g * 128 : g * 128 + WIN] = pair[g * 48 : (g + 1) * 48]
    small[at * 48 : at * 48 + 16, 384:] = lines


def attention_body(
    side, scale, q_ref, k_ref, v_ref, da_ref, pair_bias, row, col, gain_part, grads, small
):
    pens = penalties(row[...], col[...])
    head = side[0] * 6 + 2 * pl.program_id(0)
    small[...] = jnp.zeros_like(small)
    store_pair(
        grads,
        small,
        0,
        *attention_pair(
            scale, head, q_ref[...], k_ref[...], v_ref[...], da_ref[...], pair_bias[...], pens, gain_part[...]
        ),
    )


def backward_body(
    side,
    scale,
    attended,
    own,
    east,
    west,
    low,
    pw,
    gain,
    projected,
    pair_bias,
    row,
    col,
    mixed_low,
    grad_other,
    gain_part,
    grads,
    small,
    attended_near,
    attended_far,
    grid,
    rows,
    mixed_all,
    weight,
    heads,
    attended_grad,
    sems,
):
    copies = [pltpu.make_async_copy(pw, weight, sems.at[0])]
    for j in range(3):
        at = pl.ds(pl.multiple_of(j * HC + side[0] * HALF, 128), HALF)
        copies.append(pltpu.make_async_copy(projected.at[:, at], heads.at[j], sems.at[1 + j]))
    for copy in copies:
        copy.start()
    window_rows(own, east, west, low, grid, rows)
    copies[0].wait()
    norm_part(attended, rows, weight, gain, mixed_low, attended_grad, gain_part, mixed_all)
    pens = penalties(row[...], col[...])
    near = pl.ds(pl.multiple_of((1 - side[0]) * HALF, 128), HALF)
    far = pl.ds(pl.multiple_of(side[0] * HALF, 128), HALF)
    grad_other[...] = attended_grad[:, near]
    attended_near[...] = attended[:, near]
    attended_far[...] = attended[:, far]
    small[...] = jnp.zeros_like(small)
    for copy in copies[1:]:
        copy.wait()
    for hp in range(3):
        cols = slice(hp * 128, (hp + 1) * 128)
        head = side[0] * 6 + 2 * hp
        gains = gain_part[:, pl.ds(pl.multiple_of(side[0] * HC + hp * 256, 128), 256)]
        store_pair(
            grads,
            small,
            hp,
            *attention_pair(
                scale,
                head,
                heads[0, :, cols],
                heads[1, :, cols],
                heads[2, :, cols],
                attended_grad[:, pl.ds(pl.multiple_of(side[0] * HALF + hp * 128, 128), 128)],
                pair_bias[pl.ds(pl.multiple_of(head * WIN, 8), 2 * WIN), :],
                pens,
                gains,
            ),
        )


def write_coded(value, lines, outs, base):
    high = lines.astype(BF16)
    low = (lines - high.astype(F32)).astype(BF16)
    for i, tail in enumerate((high, low)):
        block = jnp.concatenate([value[i][:, :384].astype(BF16), tail], 1)
        for out in outs:
            out[base + i] = block


def add_coded(keep, recv, outs, source, base):
    value = [keep[source + i].astype(F32) + recv[source + i].astype(F32) for i in range(EXTRA)]
    write_coded(value, value[0][:, 384:] + value[1][:, 384:], outs, base)


def row_of(place):
    y = place["y"]
    return 24 * ((y // 2) * 32 + place["x"] * 8 + place["z"] * 2 + y % 2)


def first_order(core, at):
    end, left = (at == 0) | (at == 3), at < 2
    zero = [jnp.where(end, a, b) for a, b in ((0, 1), (3, 2), (1, 0), (2, 3))]
    one = [jnp.where(left, a, b) for a, b in ((0, 2), (1, 3), (2, 0), (3, 1))]
    return [jnp.where(core == 0, a, b) for a, b in zip(zero, one)]


def second_order(core, at):
    kept = jnp.where(core == 0, at // 2, at % 2)
    return [kept, 1 - kept]


def order_of(place, j, axis, second):
    at = place[1 + "xyz".index(ORDERS[j][axis])]
    return (second_order if second else first_order)(place[0], at)


def weight_body(place, x0, x1, p0, p1, m0, m1, a0, a1, s0, s1, *rest):
    outs, (left, grads, mixed, heads, total, sems) = rest[:6], rest[6:]
    pairs = ((x0, x1, left), (p0, p1, grads), (m0, m1, mixed), (a0, a1, heads))
    copies = []
    for i, (own, other, joined) in enumerate(pairs):
        for k, source in enumerate((own, other)):
            copies.append(
                pltpu.make_async_copy(source, joined.at[k * CELLS : (k + 1) * CELLS], sems.at[2 * i + k])
            )
            copies[-1].start()
    for copy in copies[:4]:
        copy.wait()
    for m in range(4):
        at = slice(m * 384, (m + 1) * 384)
        part = dot(left[:, at], grads[...], TN)
        for j in range(3):
            total[at, j * 512 : j * 512 + HALF] = part[:, j * HALF : (j + 1) * HALF]
    for copy in copies[4:]:
        copy.wait()
    for m in range(4):
        at = slice(m * 384, (m + 1) * 384)
        part = dot(mixed[:, at], heads[...], TN)
        for j in range(3):
            total[at, j * 512 + HALF : (j + 1) * 512] = part[:, j * 128 : (j + 1) * 128]
    for j in range(3):
        cols = slice(j * 512, (j + 1) * 512)
        order = order_of(place, j, 0, False)
        for i in range(4):
            out = outs[2 * j + i // 2]
            for second in range(4):
                for third in range(4):
                    places = (order[i], second, third)
                    start = row_of(dict(zip(ORDERS[j], places)))
                    rows = pl.ds(pl.multiple_of(start, 8), 24)
                    out[i % 2 * 16 + second * 4 + third] = total[rows, cols].astype(BF16)
        at = slice(j * 48, (j + 1) * 48)
        value = s0[at, :] + s1[at, :]
        write_coded([value[:24], value[24:]], value[:24, 384:], outs[2 * j : 2 * j + 2], 32)


def halve_body(count, size, axis, place, *refs):
    ins, outs = refs[:6], refs[6:]
    for j in range(3):
        keep, recv = ins[2 * j : 2 * j + 2]
        order = order_of(place, j, axis, count == 1)
        for i in range(2 * count):
            out = outs[2 * j + i // count]
            for b in range(size):
                at = order[i] * size + b
                out[i % count * size + b] = (keep[at].astype(F32) + recv[at].astype(F32)).astype(BF16)
        add_coded(keep, recv, outs[2 * j : 2 * j + 2], 2 * count * size, count * size)


def total_body(*refs):
    ins, out = refs[:6], refs[6]
    for j in range(3):
        keep, recv = ins[2 * j : 2 * j + 2]
        out[3 * j] = (keep[0].astype(F32) + recv[0].astype(F32)).astype(BF16)
        add_coded(keep, recv, [out], 1, 3 * j + 1)


def finish_body(core, own, other, qkv, proj, pair, gain, qb, vb, scale):
    which = core[0]
    scales = jnp.zeros((128,), F32)
    for side in range(2):
        for j in range(3):
            def block(i):
                return jnp.where(which == side, own[3 * j + i].astype(F32), other[3 * j + i].astype(F32))

            rows = block(0)
            rows = jnp.where(which == 0, rows[:12], rows[12:])
            at = side * HALF + j * 128
            for t in range(3):
                qkv[:, t * HC + at : t * HC + at + 128] = rows[:, t * 128 : (t + 1) * 128]
            proj[:, at : at + 128] = rows[:, HALF:]
            top, bottom = block(1), block(2)
            for g in range(3):
                start = (side * 3 + j) * 144 + g * 48
                pair[start : start + 24, :] = top[:, g * 128 : g * 128 + WIN]
                pair[start + 24 : start + 48, :] = bottom[:, g * 128 : g * 128 + WIN]
            lines = top[:, 384:] + bottom[:, 384:]
            qb[at : at + 128] = lines[0]
            vb[at : at + 128] = lines[1]
            scales = scales + lines[2]
            gain[side * HC + j * 256 : side * HC + j * 256 + 128] = lines[3]
            gain[side * HC + j * 256 + 128 : side * HC + j * 256 + 256] = lines[4]
    scale[...] = scales[:HEADS]


def branch_body(side, w, own, theirs, to_east, to_west, stay_low, stay_high, grads, rows):
    which = side[0]

    @pl.when(pl.program_id(0) == 0)
    def _():
        for pair in range(3):
            for j in range(3):
                at = j * HC + pair * 128
                cols = slice(pair * HALF + j * 128, pair * HALF + (j + 1) * 128)
                grads[:, pl.ds(pl.multiple_of(at + which * HALF, 128), 128)] = own[:, cols]
                grads[:, pl.ds(pl.multiple_of(at + (1 - which) * HALF, 128), 128)] = theirs[:, cols]

    product = dot(grads[...], w[...], NT)
    for i in range(2):
        rows[i] = product[:, i * 128 : (i + 1) * 128]
    columns = [
        jnp.concatenate([rows[i, pl.ds(j, 24, stride=12), :] for i in range(2)], 1) for j in range(12)
    ]
    for out, cols, start in (
        (stay_low, columns[:SHIFT_W], 0),
        (to_east, columns[SHIFT_W:], 0),
        (to_west, columns[:SHIFT_W], HALF_ROWS),
        (stay_high, columns[SHIFT_W:], HALF_ROWS),
    ):
        out[...] = jnp.concatenate([one[start : start + HALF_ROWS] for one in cols], 0).astype(BF16)


def last_rows_body(stay_high, from_east, out):
    start = HALF_ROWS - SHIFT_H
    out[...] = jnp.concatenate(
        [
            f32_rows(half, i * HALF_ROWS + start, SHIFT_H)
            for half in (stay_high, from_east)
            for i in range(SHIFT_W)
        ],
        0,
    ).astype(BF16)


def merge_body(upstream, stay_low, stay_high, from_west, from_east, low, out):
    for j in range(12):
        i = j % SHIFT_W
        upper, lower = (from_west, stay_high) if j < SHIFT_W else (stay_low, from_east)
        back = jnp.concatenate(
            [
                f32_rows(low, j * SHIFT_H, SHIFT_H),
                f32_rows(upper, i * HALF_ROWS, HALF_ROWS),
                f32_rows(lower, i * HALF_ROWS, HALF_ROWS - SHIFT_H),
            ],
            0,
        )
        out[j] = (upstream[j].astype(F32) + back).astype(BF16)


def permuted(value, axes, target):
    sizes = [lax.axis_size(a) for a in axes]
    pairs = []
    for source in range(int(np.prod(sizes))):
        place = np.unravel_index(source, sizes)
        to = target(*[int(v) for v in place])
        pairs.append((source, int(np.ravel_multi_index(to, sizes))))
    return lax.ppermute(value, axes, pairs)


def lon_step(value, steps):
    return permuted(value, LON, lambda *at: np.unravel_index((np.ravel_multi_index(at, (2, 4, 4)) + steps) % 32, (2, 4, 4)))


def lat_step(value, steps):
    return permuted(value, LAT, lambda *at: np.unravel_index((np.ravel_multi_index(at, (2, 2)) + steps) % 4, (2, 2)))


def core_swap(value):
    return permuted(value, ("c",), lambda c: (1 - c,))


def ring_swap(value, axis, step):
    def partner(place, c):
        return place ^ 1 if (step == 0) == (c == 0) else 3 - place

    if axis == "y":
        def target(yh, yl, c):
            to = partner(yh * 2 + yl, c)
            return (to // 2, to % 2, c)
    else:
        def target(place, c):
            return (partner(place, c), c)

    return permuted(value, AXES[axis] + ("c",), target)


def first_messages(grid):
    return call(
        first_body,
        [shape((36, C), BF16), shape((72, C), BF16), shape((54, C), BF16)],
        [grid],
        scalars=0,
        name="first",
    )


def halo(low, upper, lower):
    low = lat_step(low, -1)
    east = lon_step(upper, -1)
    (lower,) = call(to_east_body, [shape((72, C), BF16)], [lower, low], scalars=0, name="to_east")
    return east, low, lower


def shards(
    features,
    upstream,
    region_ids,
    qkv_weight,
    query_bias,
    value_bias,
    logit_scale,
    pair_bias,
    proj_weight,
    norm_gain,
):
    core = lax.axis_index("c")
    place = jnp.stack(
        [core, lax.axis_index("x"), lax.axis_index("yh") * 2 + lax.axis_index("yl"), lax.axis_index("z")]
    ).astype(jnp.int32)
    mine = core.astype(jnp.int32).reshape(1)
    theirs = 1 - mine
    scale = logit_scale
    pair_rows = pair_bias.reshape(HEADS * WIN, WIN)
    gain = norm_gain

    features = features.transpose(1, 0, 2)
    upstream = upstream.transpose(1, 0, 2)
    late = first_messages(upstream)
    east, low, lower = halo(*first_messages(features))
    late, region_ids, lower = lax.optimization_barrier((late, region_ids, lower))
    came = east, lon_step(lower, 1), low
    lower_ids = lon_step(region_ids[HALF_ROWS:], 1)
    region_ids = jnp.concatenate([region_ids[:HALF_ROWS], lower_ids], 0)
    region_row = region_ids.reshape(WINDOWS, WIN)
    region_col = region_ids.reshape(-1, 1)
    east, low, lower = halo(*late)
    came_late = east, lon_step(lower, 1), low
    x, projected, attended = call(
        forward_body,
        [shape((CELLS, C), BF16), shape((CELLS, 3 * HC), F32), shape((CELLS, HC), BF16)],
        [scale, features, *came, qkv_weight, query_bias, value_bias, pair_rows, region_row, region_col],
        scratch=[
            pltpu.VMEM((12, CELLS, 128), F32),
            pltpu.VMEM((CELLS, C), F32),
            pltpu.VMEM((C, 3 * HC), BF16),
            pltpu.SemaphoreType.DMA((9,)),
        ],
        flops=2 * CELLS * C * 3 * HC,
        far=(5,),
        vmem=60,
        name="forward",
    )
    x_other = core_swap(x)
    mixed_low, grad_mine, gain_part, grads_theirs, small_theirs, attended_mine, attended_theirs = call(
        backward_body,
        [
            shape((CELLS, C), BF16),
            shape((CELLS, HALF), F32),
            shape((1, C), F32),
            shape((CELLS, 3 * HALF), BF16),
            shape((144, 512), F32),
            shape((CELLS, HALF), BF16),
            shape((CELLS, HALF), BF16),
        ],
        [
            theirs,
            scale,
            attended,
            upstream,
            *came_late,
            proj_weight,
            gain,
            projected,
            pair_rows,
            region_row,
            region_col,
        ],
        scalars=2,
        scratch=[
            pltpu.VMEM((12, CELLS, 128), F32),
            pltpu.VMEM((CELLS, C), F32),
            pltpu.VMEM((CELLS, C), F32),
            pltpu.VMEM((C, HC), BF16),
            pltpu.VMEM((3, CELLS, HALF), F32),
            pltpu.VMEM((CELLS, HC), F32),
            pltpu.SemaphoreType.DMA((4,)),
        ],
        far=(7,),
        near=(9,),
        flops=4 * CELLS * C * HC + 2 * CELLS * WIN * 128 * 18,
        vmem=60,
        name="backward",
    )
    mixed_other = core_swap(mixed_low)
    attended_other = core_swap(attended_theirs)

    grads_other = core_swap(grads_theirs)
    small_other = core_swap(small_theirs)
    def attention(side):
        def cols(base):
            return lambda i, side, scale: (0, base + side[0] * 3 + i)

        whole = lambda i, side, scale: (0, 0)
        block = (CELLS, 128)
        return grid_call(
            attention_body,
            (3,),
            [side, scale],
            [
                (projected, block, cols(0)),
                (projected, block, cols(6)),
                (projected, block, cols(12)),
                (grad_mine, block, lambda i, side, scale: (0, i)),
                (pair_rows, (2 * WIN, WIN), lambda i, side, scale: (side[0] * 3 + i, 0)),
                (region_row, (WINDOWS, WIN), whole),
                (region_col, (CELLS, 1), whole),
                (gain_part, (1, 256), cols(0)),
            ],
            [
                (shape((CELLS, 3 * HALF), BF16), (CELLS, HALF), lambda i, side, scale: (0, i)),
                (shape((144, 512), F32), (48, 512), lambda i, side, scale: (i, 0)),
            ],
            flops=2 * CELLS * WIN * 128 * 6 * 3,
            vmem=60,
            name="attention",
        )

    grads_mine, small_mine = attention(mine)

    parts = call(
        weight_body,
        [shape((32 + EXTRA,) + BLOCK, BF16)] * 6,
        [
            place,
            x,
            x_other,
            grads_mine,
            grads_other,
            mixed_low,
            mixed_other,
            attended_mine,
            attended_other,
            small_mine,
            small_other,
        ],
        scratch=[
            pltpu.VMEM((2 * CELLS, C), BF16),
            pltpu.VMEM((2 * CELLS, 3 * HALF), BF16),
            pltpu.VMEM((2 * CELLS, C), BF16),
            pltpu.VMEM((2 * CELLS, HALF), BF16),
            pltpu.VMEM((C, C), F32),
            pltpu.SemaphoreType.DMA((8,)),
        ],
        near=tuple(range(1, 9)),
        flops=4 * CELLS * C * C,
        vmem=26,
        name="weights",
    )
    side, parts = lax.optimization_barrier((mine, parts))
    order = place
    whole = lambda i, side: (0, 0)
    to_east, to_west, stay_low, stay_high = grid_call(
        branch_body,
        (6,),
        [side],
        [
            (qkv_weight, (256, 3 * HC), lambda i, side: (i, 0)),
            (grads_mine, (CELLS, 3 * HALF), whole),
            (grads_theirs, (CELLS, 3 * HALF), whole),
        ],
        [(shape((72, C), BF16), (72, 256), lambda i, side: (0, i))] * 4,
        scratch=[pltpu.VMEM((CELLS, 3 * HC), BF16), pltpu.VMEM((2, CELLS, 128), F32)],
        flops=2 * CELLS * C * 3 * HC,
        vmem=16,
        name="branch",
    )
    from_west = lon_step(to_east, 1)
    from_east = lon_step(to_west, -1)
    (last,) = call(
        last_rows_body, [shape((36, C), BF16)], [stay_high, from_east], scalars=0, vmem=6, name="last_rows"
    )
    low = lat_step(last, 1)
    for step in range(6):
        terms = []
        for j, names in enumerate(ORDERS):
            terms += [parts[2 * j], ring_swap(parts[2 * j + 1], names[step // 2], step % 2)]
        if step == 5:
            break
        left = 32 >> step
        if step % 2 == 0:
            body = functools.partial(halve_body, 1, left // 2, step // 2)
        else:
            body = functools.partial(halve_body, 2, left // 4, step // 2 + 1)
        if step == 0:
            order, stay_low = lax.optimization_barrier((order, stay_low))
        if step == 3:
            order, last = lax.optimization_barrier((order, last))
        parts = call(body, [shape((left // 2 + EXTRA,) + BLOCK, BF16)] * 6, [order, *terms], vmem=10, name="halve")
    (input_grad,) = call(
        merge_body,
        [shape((12, 24, C), BF16)],
        [upstream, stay_low, stay_high, from_west, from_east, low],
        scalars=0,
        vmem=10,
        name="merge",
    )
    terms, input_grad = lax.optimization_barrier((terms, input_grad))
    (sums,) = call(total_body, [shape((9,) + BLOCK, BF16)], terms, scalars=0, vmem=6, name="total")
    sums_other = core_swap(sums)
    qkv_weight_grad, proj_weight_grad, pair_grad, gain_grad, query_bias_grad, value_bias_grad, scale_grad = call(
        finish_body,
        [
            shape((12, 3 * HC), F32),
            shape((12, HC), F32),
            shape((HEADS * WIN, WIN), F32),
            shape((C,), F32),
            shape((HC,), F32),
            shape((HC,), F32),
            shape((HEADS,), F32),
        ],
        [mine, sums, sums_other],
        vmem=8,
        name="finish",
    )
    pair_grad = pair_grad.reshape(HEADS, WIN, WIN)

    return (
        input_grad.transpose(1, 0, 2),
        qkv_weight_grad,
        proj_weight_grad,
        gain_grad,
        query_bias_grad,
        value_bias_grad,
        scale_grad,
        pair_grad,
    )


def solution(mesh):
    fine = Mesh(mesh.devices.reshape(2, 4, 4, 2, 2), ("yh", "x", "z", "yl", "c"))
    every = LON + LAT
    return jax.shard_map(
        shards,
        mesh=fine,
        in_specs=(P(LAT, LON, None), P(LAT, LON, None), P(LAT, LON)) + (P(),) * 7,
        out_specs=(P(LAT, LON, None), P(every, None), P(every, None)) + (P(),) * 5,
        check_vma=False,
    )
```

```python
import functools

import jax
import jax.numpy as jnp
import numpy as np
from jax import lax
from jax.experimental import pallas as pl
from jax.experimental.pallas import tpu as pltpu
from jax.sharding import Mesh
from jax.sharding import PartitionSpec as P

HEADS = 12
HEAD_DIM = 64
WIN_H = 6
WIN_W = 12
SHIFT_H = 3
SHIFT_W = 6
WIN = 72
C = 1536
HC = 768
HALF = 384
CELLS = 288
WINDOWS = 4
COSINE_EPS = 1e-06
NORM_EPS = 1e-05

F32 = jnp.float32
BF16 = jnp.bfloat16
LON = ("yh", "x", "z")
LAT = ("yl", "c")
Y = ("yh", "yl")
ORDERS = (("x", "y", "z"), ("y", "z", "x"), ("z", "x", "y"))
AXES = {"x": ("x",), "y": Y, "z": ("z",)}
BLOCK = (24, 512)
EXTRA = 2
NT = (((1,), (1,)), ((), ()))
TN = (((0,), (0,)), ((), ()))
NN = (((1,), (0,)), ((), ()))
VMEM = pl.BlockSpec(memory_space=pltpu.VMEM)
HBM = pl.BlockSpec(memory_space=pltpu.HBM)
ANY = pl.BlockSpec(memory_space=pl.ANY)
SMEM = pl.BlockSpec(memory_space=pltpu.SMEM)


def dot(left, right, dims=NN):
    return lax.dot_general(left, right, dims, preferred_element_type=F32)


def cost(outs, operands, flops):
    moved = sum(int(np.prod(o.shape)) * o.dtype.itemsize for o in (*outs, *operands))
    return pl.CostEstimate(flops=flops, bytes_accessed=moved, transcendentals=0)


def call(body, outs, operands, scalars=1, scratch=(), flops=0, vmem=50, far=(), near=(), sent=(), name=None):
    specs = [SMEM] * scalars + [VMEM] * (len(operands) - scalars)
    for i in far:
        specs[i] = HBM
    for i in near:
        specs[i] = ANY
    return pl.pallas_call(
        body,
        out_shape=list(outs),
        in_specs=specs,
        out_specs=[ANY if i in sent else VMEM for i in range(len(outs))],
        scratch_shapes=list(scratch),
        compiler_params=pltpu.CompilerParams(vmem_limit_bytes=vmem * 2**20),
        cost_estimate=cost(outs, operands, flops),
        name=name,
    )(*operands)


def grid_call(body, grid, scalars, ins, outs, scratch=(), flops=0, vmem=50, name=None):
    operands = [array for array, _, _ in ins]
    results = [result for result, _, _ in outs]
    spec = pltpu.PrefetchScalarGridSpec(
        num_scalar_prefetch=len(scalars),
        grid=grid,
        in_specs=[pl.BlockSpec(block, at) for _, block, at in ins],
        out_specs=[pl.BlockSpec(block, at) for _, block, at in outs],
        scratch_shapes=list(scratch),
    )
    return pl.pallas_call(
        body,
        grid_spec=spec,
        out_shape=results,
        compiler_params=pltpu.CompilerParams(vmem_limit_bytes=vmem * 2**20),
        cost_estimate=cost(results, operands, flops),
        name=name,
    )(*scalars, *operands)


def shape(dims, dtype):
    return jax.ShapeDtypeStruct(dims, dtype)


def head_sum(value):
    rows = lax.broadcasted_iota(jnp.int32, (128, 128), 0) // HEAD_DIM
    cols = lax.broadcasted_iota(jnp.int32, (128, 128), 1) // HEAD_DIM
    ones = (rows == cols).astype(F32).astype(BF16)
    high = value.astype(BF16)
    low = (value - high.astype(F32)).astype(BF16)
    return dot(high, ones) + dot(low, ones)


def low_half(rows):
    return lax.broadcasted_iota(jnp.int32, (rows, 128), 1) < HEAD_DIM


def stacked(value):
    mask = low_half(WIN)
    return jnp.concatenate([jnp.where(mask, value, 0.0), jnp.where(mask, 0.0, value)], 0).astype(BF16)


def unstacked(value):
    return jnp.where(low_half(WIN), value[:WIN], value[WIN:])


def normalized(rows):
    inv = lax.rsqrt(head_sum(rows * rows) + COSINE_EPS)
    return rows * inv, inv


def penalties(region_row, region_col):
    out = []
    for w in range(WINDOWS):
        same = region_row[w : w + 1, :] == region_col[w * WIN : (w + 1) * WIN, :]
        one = jnp.where(same, 0.0, -100.0).astype(F32)
        out.append(jnp.concatenate([one, one], 0))
    return out


def two_heads(scale_ref, head):
    top = lax.broadcasted_iota(jnp.int32, (2 * WIN, 1), 0) < WIN
    return jnp.exp(jnp.where(top, scale_ref[head], scale_ref[head + 1]))


def softmax_of(scores):
    exp_scores = [jnp.exp(one) for one in scores]
    sums = [jnp.sum(one, -1, keepdims=True) for one in exp_scores]
    return [one / total for one, total in zip(exp_scores, sums)]


SPANS = [slice(n * WIN, (n + 1) * WIN) for n in range(WINDOWS)]


HALF_ROWS = 12


def f32_rows(ref, start, count):
    return ref[...].astype(F32)[start : start + count]


def window_rows(own, east, west, low, grid, rows):
    for j in range(12):
        i = j % SHIFT_W
        if j < SHIFT_W:
            upper = own[SHIFT_W + i].astype(F32)[SHIFT_H : SHIFT_H + HALF_ROWS]
            lower = [f32_rows(west, i * HALF_ROWS, HALF_ROWS)]
        else:
            upper = f32_rows(east, i * HALF_ROWS, HALF_ROWS)
            lower = [own[i].astype(F32)[SHIFT_H + HALF_ROWS :], f32_rows(low, i * SHIFT_H, SHIFT_H)]
        column = jnp.concatenate([upper] + lower, 0)
        for t in range(12):
            grid[t, j * 24 : (j + 1) * 24, :] = column[:, t * 128 : (t + 1) * 128]
    for r in range(24):
        for t in range(12):
            rows[r * 12 : (r + 1) * 12, t * 128 : (t + 1) * 128] = grid[t, pl.ds(r, 12, stride=24), :]


def first_body(own, low, upper, lower):
    low[...] = jnp.concatenate([own[j].astype(F32)[:SHIFT_H] for j in range(12)], 0).astype(BF16)
    upper[...] = jnp.concatenate(
        [own[j].astype(F32)[SHIFT_H : SHIFT_H + HALF_ROWS] for j in range(SHIFT_W)], 0
    ).astype(BF16)
    lower[...] = jnp.concatenate(
        [own[SHIFT_W + i].astype(F32)[SHIFT_H + HALF_ROWS :] for i in range(SHIFT_W)], 0
    ).astype(BF16)


def to_east_body(lower, low, out):
    count = HALF_ROWS - SHIFT_H
    out[...] = jnp.concatenate(
        [
            piece
            for i in range(SHIFT_W)
            for piece in (
                f32_rows(lower, i * count, count),
                f32_rows(low, (SHIFT_W + i) * SHIFT_H, SHIFT_H),
            )
        ],
        0,
    ).astype(BF16)


def forward_body(
    scale, own, east, west, low, w, query_bias, value_bias, pair_bias, row, col, x_out, projected_out, attended, grid, rows, wide, x, projected, sems
):
    copies = []
    for g in range(3):
        for j in range(3):
            at = pl.ds(j * HC + g * 256, 256)
            copies.append(pltpu.make_async_copy(w.at[:, at], wide.at[:, at], sems.at[3 * g + j]))
            copies[-1].start()
    window_rows(own, east, west, low, grid, rows)
    x[...] = rows[...].astype(BF16)
    sends = [pltpu.make_async_copy(x, x_out, sems.at[9])]
    sends[0].start()
    pens = penalties(row[...], col[...])
    for g in range(3):
        for j in range(3):
            lo = j * HC + g * 256
            copies[3 * g + j].wait()
            product = dot(x[...], wide[:, lo : lo + 256])
            if j != 1:
                product = product + (query_bias, None, value_bias)[j][g * 256 : (g + 1) * 256].reshape(1, 256)
            projected[:, lo : lo + 256] = product
            at = pl.ds(lo, 256)
            sends.append(
                pltpu.make_async_copy(projected.at[:, at], projected_out.at[:, at], sems.at[10 + 3 * g + j])
            )
            sends[-1].start()
        for half in range(2):
            lo = g * 256 + half * 128
            head = lo // HEAD_DIM
            factor = two_heads(scale, head)
            q = normalized(projected[:, lo : lo + 128])[0]
            k = normalized(projected[:, HC + lo : HC + lo + 128])[0]
            v = projected[:, 2 * HC + lo : 2 * HC + lo + 128]
            pb = pair_bias[head * WIN : (head + 2) * WIN, :]
            cosines = [dot(stacked(q[at]), k[at].astype(BF16), NT) for at in SPANS]
            attention = softmax_of([c * factor + pb + pen for c, pen in zip(cosines, pens)])
            outs = [dot(a.astype(BF16), v[at].astype(BF16)) for a, at in zip(attention, SPANS)]
            attended[:, lo : lo + 128] = jnp.concatenate([unstacked(o) for o in outs], 0).astype(BF16)
    for send in sends:
        send.wait()


def norm_part(attended, rows, pw, gain, mixed_low, attended_grad, gain_part, mixed_all):
    for n in range(6):
        at = slice(n * 256, (n + 1) * 256)
        mixed_all[:, at] = dot(attended[...], pw[at, :], NT)
    total = jnp.zeros((1, C), F32)
    for r in range(6):
        at = slice(r * 48, (r + 1) * 48)
        mixed = mixed_all[at, :]
        center = mixed - jnp.mean(mixed, -1, keepdims=True)
        inv_std = lax.rsqrt(jnp.mean(center * center, -1, keepdims=True) + NORM_EPS)
        normed = center * inv_std
        up = rows[at, :]
        total = total + jnp.sum(up * normed, 0, keepdims=True)
        scaled = up * gain[...].reshape(1, C)
        grad = inv_std * (
            scaled
            - jnp.mean(scaled, -1, keepdims=True)
            - normed * jnp.mean(scaled * normed, -1, keepdims=True)
        )
        mixed_low[at, :] = grad.astype(BF16)
    gain_part[...] = total
    for n in range(3):
        at = slice(n * 256, (n + 1) * 256)
        attended_grad[:, at] = dot(mixed_low[...], pw[:, at]).astype(BF16).astype(F32)


def attention_pair(scale, head, q, k, v, da, pb, pens, gains):
    factor = two_heads(scale, head)
    q, q_inv = normalized(q)
    k, k_inv = normalized(k)
    qs = [stacked(q[at]) for at in SPANS]
    das = [stacked(da[at]) for at in SPANS]
    kb = [k[at].astype(BF16) for at in SPANS]
    vb = [v[at].astype(BF16) for at in SPANS]
    cosines = [dot(a, b, NT) for a, b in zip(qs, kb)]
    prob_grads = [dot(a, b, NT) for a, b in zip(das, vb)]
    attention = softmax_of([c * factor + pb + pen for c, pen in zip(cosines, pens)])
    v_grad = jnp.concatenate([dot(a.astype(BF16), b, TN) for a, b in zip(attention, das)], 0)
    means = [jnp.sum(a * p, -1, keepdims=True) for a, p in zip(attention, prob_grads)]
    score_grads = [a * (p - m) for a, p, m in zip(attention, prob_grads, means)]
    cosine_grads = [(s * factor).astype(BF16) for s in score_grads]
    gq = jnp.concatenate([unstacked(dot(c, b)) for c, b in zip(cosine_grads, kb)], 0)
    gk = jnp.concatenate([dot(c, b, TN) for c, b in zip(cosine_grads, qs)], 0)
    pair = (score_grads[0] + score_grads[1]) + (score_grads[2] + score_grads[3])
    scaled = sum(s * c for s, c in zip(score_grads, cosines))
    lane = lax.broadcasted_iota(jnp.int32, (1, 128), 1)
    scale_line = jnp.zeros((1, 128), F32)
    for i in range(2):
        one = jnp.sum(jnp.sum(scaled[i * WIN : (i + 1) * WIN], 0, keepdims=True), 1, keepdims=True)
        scale_line = scale_line + jnp.where(lane == head + i, one * factor[i * WIN : i * WIN + 1], 0.0)
    q_grad = q_inv * (gq - q * head_sum(q * gq))
    k_grad = k_inv * (gk - k * head_sum(k * gk))
    lines = jnp.concatenate(
        [
            jnp.sum(q_grad, 0, keepdims=True),
            jnp.sum(v_grad, 0, keepdims=True),
            scale_line,
            gains[:, :128],
            gains[:, 128:],
            jnp.zeros((11, 128), F32),
        ],
        0,
    )
    return (q_grad, k_grad, v_grad), pair, lines


def store_pair(grads, small, at, parts, pair, lines):
    for i, part in enumerate(parts):
        grads[:, at * HALF + i * 128 : at * HALF + (i + 1) * 128] = part.astype(BF16)
    rows = slice(at * 48, (at + 1) * 48)
    for g in range(3):
        small[rows, g * 128 : g * 128 + WIN] = pair[g * 48 : (g + 1) * 48]
    small[at * 48 : at * 48 + 16, 384:] = lines


def attention_body(
    side, scale, q_ref, k_ref, v_ref, da_ref, pair_bias, row, col, gain_part, grads, small
):
    pens = penalties(row[...], col[...])
    head = side[0] * 6 + 2 * pl.program_id(0)
    small[...] = jnp.zeros_like(small)
    store_pair(
        grads,
        small,
        0,
        *attention_pair(
            scale, head, q_ref[...], k_ref[...], v_ref[...], da_ref[...], pair_bias[...], pens, gain_part[...]
        ),
    )


def backward_body(
    side,
    scale,
    attended,
    own,
    east,
    west,
    low,
    pw,
    gain,
    projected,
    pair_bias,
    row,
    col,
    mixed_out,
    grad_other,
    gain_part,
    grads,
    small,
    attended_near,
    attended_far,
    grid,
    rows,
    mixed_all,
    weight,
    heads,
    attended_grad,
    mixed_low,
    sems,
):
    copies = [pltpu.make_async_copy(pw, weight, sems.at[0])]
    for j in range(3):
        at = pl.ds(pl.multiple_of(j * HC + side[0] * HALF, 128), HALF)
        copies.append(pltpu.make_async_copy(projected.at[:, at], heads.at[j], sems.at[1 + j]))
    for copy in copies:
        copy.start()
    window_rows(own, east, west, low, grid, rows)
    copies[0].wait()
    norm_part(attended, rows, weight, gain, mixed_low, attended_grad, gain_part, mixed_all)
    pens = penalties(row[...], col[...])
    send = pltpu.make_async_copy(mixed_low, mixed_out, sems.at[4])
    send.start()
    near = pl.ds(pl.multiple_of((1 - side[0]) * HALF, 128), HALF)
    far = pl.ds(pl.multiple_of(side[0] * HALF, 128), HALF)
    grad_other[...] = attended_grad[:, near]
    attended_near[...] = attended[:, near]
    attended_far[...] = attended[:, far]
    small[...] = jnp.zeros_like(small)
    for copy in copies[1:]:
        copy.wait()
    for hp in range(3):
        cols = slice(hp * 128, (hp + 1) * 128)
        head = side[0] * 6 + 2 * hp
        gains = gain_part[:, pl.ds(pl.multiple_of(side[0] * HC + hp * 256, 128), 256)]
        store_pair(
            grads,
            small,
            hp,
            *attention_pair(
                scale,
                head,
                heads[0, :, cols],
                heads[1, :, cols],
                heads[2, :, cols],
                attended_grad[:, pl.ds(pl.multiple_of(side[0] * HALF + hp * 128, 128), 128)],
                pair_bias[pl.ds(pl.multiple_of(head * WIN, 8), 2 * WIN), :],
                pens,
                gains,
            ),
        )
    send.wait()


def write_coded(value, lines, outs, base):
    high = lines.astype(BF16)
    low = (lines - high.astype(F32)).astype(BF16)
    for i, tail in enumerate((high, low)):
        block = jnp.concatenate([value[i][:, :384].astype(BF16), tail], 1)
        for out in outs:
            out[base + i] = block


def add_coded(keep, recv, outs, source, base):
    value = [keep[source + i].astype(F32) + recv[source + i].astype(F32) for i in range(EXTRA)]
    write_coded(value, value[0][:, 384:] + value[1][:, 384:], outs, base)


def row_of(place):
    y = place["y"]
    return 24 * ((y // 2) * 32 + place["x"] * 8 + place["z"] * 2 + y % 2)


def first_order(core, at):
    end, left = (at == 0) | (at == 3), at < 2
    zero = [jnp.where(end, a, b) for a, b in ((0, 1), (3, 2), (1, 0), (2, 3))]
    one = [jnp.where(left, a, b) for a, b in ((0, 2), (1, 3), (2, 0), (3, 1))]
    return [jnp.where(core == 0, a, b) for a, b in zip(zero, one)]


def second_order(core, at):
    kept = jnp.where(core == 0, at // 2, at % 2)
    return [kept, 1 - kept]


def order_of(place, j, axis, second):
    at = place[1 + "xyz".index(ORDERS[j][axis])]
    return (second_order if second else first_order)(place[0], at)


def weight_body(place, x0, x1, p0, p1, m0, m1, a0, a1, s0, s1, *rest):
    outs, (left, grads, mixed, heads, total, sems) = rest[:6], rest[6:]
    pairs = ((x0, x1, left), (p0, p1, grads), (m0, m1, mixed), (a0, a1, heads))
    copies = []
    for i, (own, other, joined) in enumerate(pairs):
        for k, source in enumerate((own, other)):
            copies.append(
                pltpu.make_async_copy(source, joined.at[k * CELLS : (k + 1) * CELLS], sems.at[2 * i + k])
            )
            copies[-1].start()
    for copy in copies[:4]:
        copy.wait()
    for m in range(4):
        at = slice(m * 384, (m + 1) * 384)
        part = dot(left[:, at], grads[...], TN)
        for j in range(3):
            total[at, j * 512 : j * 512 + HALF] = part[:, j * HALF : (j + 1) * HALF]
    for copy in copies[4:]:
        copy.wait()
    for m in range(4):
        at = slice(m * 384, (m + 1) * 384)
        part = dot(mixed[:, at], heads[...], TN)
        for j in range(3):
            total[at, j * 512 + HALF : (j + 1) * 512] = part[:, j * 128 : (j + 1) * 128]
    for j in range(3):
        cols = slice(j * 512, (j + 1) * 512)
        order = order_of(place, j, 0, False)
        for i in range(4):
            out = outs[2 * j + i // 2]
            for second in range(4):
                for third in range(4):
                    places = (order[i], second, third)
                    start = row_of(dict(zip(ORDERS[j], places)))
                    rows = pl.ds(pl.multiple_of(start, 8), 24)
                    out[i % 2 * 16 + second * 4 + third] = total[rows, cols].astype(BF16)
        at = slice(j * 48, (j + 1) * 48)
        value = s0[at, :] + s1[at, :]
        write_coded([value[:24], value[24:]], value[:24, 384:], outs[2 * j : 2 * j + 2], 32)


def halve_body(count, size, axis, place, *refs):
    ins, outs = refs[:6], refs[6:]
    for j in range(3):
        keep, recv = ins[2 * j : 2 * j + 2]
        order = order_of(place, j, axis, count == 1)
        for i in range(2 * count):
            out = outs[2 * j + i // count]
            for b in range(size):
                at = order[i] * size + b
                out[i % count * size + b] = (keep[at].astype(F32) + recv[at].astype(F32)).astype(BF16)
        add_coded(keep, recv, outs[2 * j : 2 * j + 2], 2 * count * size, count * size)


def total_body(*refs):
    ins, out = refs[:6], refs[6]
    for j in range(3):
        keep, recv = ins[2 * j : 2 * j + 2]
        out[3 * j] = (keep[0].astype(F32) + recv[0].astype(F32)).astype(BF16)
        add_coded(keep, recv, [out], 1, 3 * j + 1)


def finish_body(core, own, other, qkv, proj, pair, gain, qb, vb, scale):
    which = core[0]
    scales = jnp.zeros((128,), F32)
    for side in range(2):
        for j in range(3):
            def block(i):
                return jnp.where(which == side, own[3 * j + i].astype(F32), other[3 * j + i].astype(F32))

            rows = block(0)
            rows = jnp.where(which == 0, rows[:12], rows[12:])
            at = side * HALF + j * 128
            for t in range(3):
                qkv[:, t * HC + at : t * HC + at + 128] = rows[:, t * 128 : (t + 1) * 128]
            proj[:, at : at + 128] = rows[:, HALF:]
            top, bottom = block(1), block(2)
            for g in range(3):
                start = (side * 3 + j) * 144 + g * 48
                pair[start : start + 24, :] = top[:, g * 128 : g * 128 + WIN]
                pair[start + 24 : start + 48, :] = bottom[:, g * 128 : g * 128 + WIN]
            lines = top[:, 384:] + bottom[:, 384:]
            qb[at : at + 128] = lines[0]
            vb[at : at + 128] = lines[1]
            scales = scales + lines[2]
            gain[side * HC + j * 256 : side * HC + j * 256 + 128] = lines[3]
            gain[side * HC + j * 256 + 128 : side * HC + j * 256 + 256] = lines[4]
    scale[...] = scales[:HEADS]


def branch_body(side, w, own, theirs, to_east, to_west, stay_low, stay_high, grads, rows):
    which = side[0]

    @pl.when(pl.program_id(0) == 0)
    def _():
        for pair in range(3):
            for j in range(3):
                at = j * HC + pair * 128
                cols = slice(pair * HALF + j * 128, pair * HALF + (j + 1) * 128)
                grads[:, pl.ds(pl.multiple_of(at + which * HALF, 128), 128)] = own[:, cols]
                grads[:, pl.ds(pl.multiple_of(at + (1 - which) * HALF, 128), 128)] = theirs[:, cols]

    product = dot(grads[...], w[...], NT)
    for i in range(2):
        rows[i] = product[:, i * 128 : (i + 1) * 128]
    columns = [
        jnp.concatenate([rows[i, pl.ds(j, 24, stride=12), :] for i in range(2)], 1) for j in range(12)
    ]
    for out, cols, start in (
        (stay_low, columns[:SHIFT_W], 0),
        (to_east, columns[SHIFT_W:], 0),
        (to_west, columns[:SHIFT_W], HALF_ROWS),
        (stay_high, columns[SHIFT_W:], HALF_ROWS),
    ):
        out[...] = jnp.concatenate([one[start : start + HALF_ROWS] for one in cols], 0).astype(BF16)


def last_rows_body(stay_high, from_east, out):
    start = HALF_ROWS - SHIFT_H
    out[...] = jnp.concatenate(
        [
            f32_rows(half, i * HALF_ROWS + start, SHIFT_H)
            for half in (stay_high, from_east)
            for i in range(SHIFT_W)
        ],
        0,
    ).astype(BF16)


def merge_body(upstream, stay_low, stay_high, from_west, from_east, low, out):
    for j in range(12):
        i = j % SHIFT_W
        upper, lower = (from_west, stay_high) if j < SHIFT_W else (stay_low, from_east)
        back = jnp.concatenate(
            [
                f32_rows(low, j * SHIFT_H, SHIFT_H),
                f32_rows(upper, i * HALF_ROWS, HALF_ROWS),
                f32_rows(lower, i * HALF_ROWS, HALF_ROWS - SHIFT_H),
            ],
            0,
        )
        out[j] = (upstream[j].astype(F32) + back).astype(BF16)


def permuted(value, axes, target):
    sizes = [lax.axis_size(a) for a in axes]
    pairs = []
    for source in range(int(np.prod(sizes))):
        place = np.unravel_index(source, sizes)
        to = target(*[int(v) for v in place])
        pairs.append((source, int(np.ravel_multi_index(to, sizes))))
    return lax.ppermute(value, axes, pairs)


def lon_step(value, steps):
    return permuted(value, LON, lambda *at: np.unravel_index((np.ravel_multi_index(at, (2, 4, 4)) + steps) % 32, (2, 4, 4)))


def lat_step(value, steps):
    return permuted(value, LAT, lambda *at: np.unravel_index((np.ravel_multi_index(at, (2, 2)) + steps) % 4, (2, 2)))


def core_swap(value):
    return permuted(value, ("c",), lambda c: (1 - c,))


def ring_swap(value, axis, step):
    def partner(place, c):
        return place ^ 1 if (step == 0) == (c == 0) else 3 - place

    if axis == "y":
        def target(yh, yl, c):
            to = partner(yh * 2 + yl, c)
            return (to // 2, to % 2, c)
    else:
        def target(place, c):
            return (partner(place, c), c)

    return permuted(value, AXES[axis] + ("c",), target)


def first_messages(grid):
    return call(
        first_body,
        [shape((36, C), BF16), shape((72, C), BF16), shape((54, C), BF16)],
        [grid],
        scalars=0,
        name="first",
    )


def halo(low, upper, lower):
    low = lat_step(low, -1)
    east = lon_step(upper, -1)
    (lower,) = call(to_east_body, [shape((72, C), BF16)], [lower, low], scalars=0, name="to_east")
    return east, low, lower


def shards(
    features,
    upstream,
    region_ids,
    qkv_weight,
    query_bias,
    value_bias,
    logit_scale,
    pair_bias,
    proj_weight,
    norm_gain,
):
    core = lax.axis_index("c")
    place = jnp.stack(
        [core, lax.axis_index("x"), lax.axis_index("yh") * 2 + lax.axis_index("yl"), lax.axis_index("z")]
    ).astype(jnp.int32)
    mine = core.astype(jnp.int32).reshape(1)
    theirs = 1 - mine
    scale = logit_scale
    pair_rows = pair_bias.reshape(HEADS * WIN, WIN)
    gain = norm_gain

    features = features.transpose(1, 0, 2)
    upstream = upstream.transpose(1, 0, 2)
    late = first_messages(upstream)
    east, low, lower = halo(*first_messages(features))
    late, region_ids, lower = lax.optimization_barrier((late, region_ids, lower))
    came = east, lon_step(lower, 1), low
    lower_ids = lon_step(region_ids[HALF_ROWS:], 1)
    region_ids = jnp.concatenate([region_ids[:HALF_ROWS], lower_ids], 0)
    region_row = region_ids.reshape(WINDOWS, WIN)
    region_col = region_ids.reshape(-1, 1)
    east, low, lower = halo(*late)
    came_late = east, lon_step(lower, 1), low
    x, projected, attended = call(
        forward_body,
        [shape((CELLS, C), BF16), shape((CELLS, 3 * HC), F32), shape((CELLS, HC), BF16)],
        [scale, features, *came, qkv_weight, query_bias, value_bias, pair_rows, region_row, region_col],
        scratch=[
            pltpu.VMEM((12, CELLS, 128), F32),
            pltpu.VMEM((CELLS, C), F32),
            pltpu.VMEM((C, 3 * HC), BF16),
            pltpu.VMEM((CELLS, C), BF16),
            pltpu.VMEM((CELLS, 3 * HC), F32),
            pltpu.SemaphoreType.DMA((19,)),
        ],
        flops=2 * CELLS * C * 3 * HC,
        far=(5,),
        vmem=60,
        sent=(0, 1),
        name="forward",
    )
    x_other = core_swap(x)
    mixed_low, grad_mine, gain_part, grads_theirs, small_theirs, attended_mine, attended_theirs = call(
        backward_body,
        [
            shape((CELLS, C), BF16),
            shape((CELLS, HALF), F32),
            shape((1, C), F32),
            shape((CELLS, 3 * HALF), BF16),
            shape((144, 512), F32),
            shape((CELLS, HALF), BF16),
            shape((CELLS, HALF), BF16),
        ],
        [
            theirs,
            scale,
            attended,
            upstream,
            *came_late,
            proj_weight,
            gain,
            projected,
            pair_rows,
            region_row,
            region_col,
        ],
        scalars=2,
        scratch=[
            pltpu.VMEM((12, CELLS, 128), F32),
            pltpu.VMEM((CELLS, C), F32),
            pltpu.VMEM((CELLS, C), F32),
            pltpu.VMEM((C, HC), BF16),
            pltpu.VMEM((3, CELLS, HALF), F32),
            pltpu.VMEM((CELLS, HC), F32),
            pltpu.VMEM((CELLS, C), BF16),
            pltpu.SemaphoreType.DMA((5,)),
        ],
        far=(7,),
        near=(9,),
        flops=4 * CELLS * C * HC + 2 * CELLS * WIN * 128 * 18,
        vmem=60,
        sent=(0,),
        name="backward",
    )
    mixed_other = core_swap(mixed_low)
    attended_other = core_swap(attended_theirs)

    grads_other = core_swap(grads_theirs)
    small_other = core_swap(small_theirs)
    def attention(side):
        def cols(base):
            return lambda i, side, scale: (0, base + side[0] * 3 + i)

        whole = lambda i, side, scale: (0, 0)
        block = (CELLS, 128)
        return grid_call(
            attention_body,
            (3,),
            [side, scale],
            [
                (projected, block, cols(0)),
                (projected, block, cols(6)),
                (projected, block, cols(12)),
                (grad_mine, block, lambda i, side, scale: (0, i)),
                (pair_rows, (2 * WIN, WIN), lambda i, side, scale: (side[0] * 3 + i, 0)),
                (region_row, (WINDOWS, WIN), whole),
                (region_col, (CELLS, 1), whole),
                (gain_part, (1, 256), cols(0)),
            ],
            [
                (shape((CELLS, 3 * HALF), BF16), (CELLS, HALF), lambda i, side, scale: (0, i)),
                (shape((144, 512), F32), (48, 512), lambda i, side, scale: (i, 0)),
            ],
            flops=2 * CELLS * WIN * 128 * 6 * 3,
            vmem=16,
            name="attention",
        )

    grads_mine, small_mine = attention(mine)

    parts = call(
        weight_body,
        [shape((32 + EXTRA,) + BLOCK, BF16)] * 6,
        [
            place,
            x,
            x_other,
            grads_mine,
            grads_other,
            mixed_low,
            mixed_other,
            attended_mine,
            attended_other,
            small_mine,
            small_other,
        ],
        scratch=[
            pltpu.VMEM((2 * CELLS, C), BF16),
            pltpu.VMEM((2 * CELLS, 3 * HALF), BF16),
            pltpu.VMEM((2 * CELLS, C), BF16),
            pltpu.VMEM((2 * CELLS, HALF), BF16),
            pltpu.VMEM((C, C), F32),
            pltpu.SemaphoreType.DMA((8,)),
        ],
        near=tuple(range(1, 9)),
        flops=4 * CELLS * C * C,
        vmem=26,
        name="weights",
    )
    side, parts = lax.optimization_barrier((mine, parts))
    order = place
    whole = lambda i, side: (0, 0)
    to_east, to_west, stay_low, stay_high = grid_call(
        branch_body,
        (6,),
        [side],
        [
            (qkv_weight, (256, 3 * HC), lambda i, side: (i, 0)),
            (grads_mine, (CELLS, 3 * HALF), whole),
            (grads_theirs, (CELLS, 3 * HALF), whole),
        ],
        [(shape((72, C), BF16), (72, 256), lambda i, side: (0, i))] * 4,
        scratch=[pltpu.VMEM((CELLS, 3 * HC), BF16), pltpu.VMEM((2, CELLS, 128), F32)],
        flops=2 * CELLS * C * 3 * HC,
        vmem=16,
        name="branch",
    )
    from_west = lon_step(to_east, 1)
    from_east = lon_step(to_west, -1)
    (last,) = call(
        last_rows_body, [shape((36, C), BF16)], [stay_high, from_east], scalars=0, vmem=6, name="last_rows"
    )
    low = lat_step(last, 1)
    for step in range(6):
        terms = []
        for j, names in enumerate(ORDERS):
            terms += [parts[2 * j], ring_swap(parts[2 * j + 1], names[step // 2], step % 2)]
        if step == 5:
            break
        left = 32 >> step
        if step % 2 == 0:
            body = functools.partial(halve_body, 1, left // 2, step // 2)
        else:
            body = functools.partial(halve_body, 2, left // 4, step // 2 + 1)
        if step == 0:
            order, stay_low = lax.optimization_barrier((order, stay_low))
        if step == 3:
            order, last = lax.optimization_barrier((order, last))
        parts = call(body, [shape((left // 2 + EXTRA,) + BLOCK, BF16)] * 6, [order, *terms], vmem=10, name="halve")
    (input_grad,) = call(
        merge_body,
        [shape((12, 24, C), BF16)],
        [upstream, stay_low, stay_high, from_west, from_east, low],
        scalars=0,
        vmem=10,
        name="merge",
    )
    terms, input_grad = lax.optimization_barrier((terms, input_grad))
    (sums,) = call(total_body, [shape((9,) + BLOCK, BF16)], terms, scalars=0, vmem=6, name="total")
    sums_other = core_swap(sums)
    qkv_weight_grad, proj_weight_grad, pair_grad, gain_grad, query_bias_grad, value_bias_grad, scale_grad = call(
        finish_body,
        [
            shape((12, 3 * HC), F32),
            shape((12, HC), F32),
            shape((HEADS * WIN, WIN), F32),
            shape((C,), F32),
            shape((HC,), F32),
            shape((HC,), F32),
            shape((HEADS,), F32),
        ],
        [mine, sums, sums_other],
        vmem=8,
        name="finish",
    )
    pair_grad = pair_grad.reshape(HEADS, WIN, WIN)

    return (
        input_grad.transpose(1, 0, 2),
        qkv_weight_grad,
        proj_weight_grad,
        gain_grad,
        query_bias_grad,
        value_bias_grad,
        scale_grad,
        pair_grad,
    )


def solution(mesh):
    fine = Mesh(mesh.devices.reshape(2, 4, 4, 2, 2), ("yh", "x", "z", "yl", "c"))
    every = LON + LAT
    return jax.shard_map(
        shards,
        mesh=fine,
        in_specs=(P(LAT, LON, None), P(LAT, LON, None), P(LAT, LON)) + (P(),) * 7,
        out_specs=(P(LAT, LON, None), P(every, None), P(every, None)) + (P(),) * 5,
        check_vma=False,
    )
```
